32 devices in a mesh: lat: 4 (over z), lon: 8 (over y, x, core).
Axes of the slice: x: 2, y: 2, z: 4, core: 2. Of those that a mesh axis runs over, the one named last changes fastest.
Arguments:
- control: float32 [4, 90, 32, 1024], P(None, None, 'lat', 'lon'), may hold values from -6 to 6
- kappa: float32 [4, 90, 32, 1024], P(None, None, 'lat', 'lon'), may hold values from 0.25 to 0.5
- pc_obs: bfloat16 [1024, 128, 300], P(('lat', 'lon')), may hold values from -6 to 6
- owner: int32 [1024, 1], P(('lat', 'lon')), may hold values from 0 to 31; in each aligned block of 32 rows (0 to 31, 32 to 63, ...) at most 2 rows name the same one
- columns: int32 [1024, 128], P(('lat', 'lon')), may hold values from 0 to 1023
- counts: int32 [1024], P(('lat', 'lon')), may hold values from 1 to 128, as said below
- jacobian: bfloat16 [360, 300], replicated, may hold values from -0.3125 to 0.3125
- obs_weight: float32 [300], replicated, may hold values from 0.3 to 3
Outputs:
- gradient: float32 [4, 90, 32, 1024], P(None, None, 'lat', 'lon')
The draws below stay inside these ranges and needn't reach their ends.
Inputs may be any that keep to these rules, and one draw needn't show every extreme that they name: Among the 32 blocks of one device no owner is named more than 2 times, a bound that some block reaches. `counts`: the first block of every device is full.
All inputs are finite; a program needn't handle non-finite values.
Results may differ from the reference program's by a relative error of at most 0.0017.
Values may be sent and summed in bfloat16 or wider, within the bound.
A program may use at most 256 MiB of HBM per device.

```python
import math
import jax
import jax.numpy as jnp
import numpy as np
from jax import lax

FIELDS = 4
LEV = 90
PCS = 300
LAT_DEV = 8
LON_DEV = 128
SND = 128
CAP = 2
STEPS = 4
NB_DEV = 32
NLAT = 32
NLON = 1024
BLOCKS = 1024
N_LON = 8
DEVICES = 32


def draw_counts(key, part):
    values = jax.random.randint(key, (BLOCKS,), 1, SND + 1, dtype=jnp.int32)
    return values.at[::NB_DEV].set(SND)


def place_ends(drawn, key, low, top_value):
    extent = drawn.shape
    index_at = [jax.random.randint(jax.random.fold_in(key, axis), (), 0, extent[axis]) for axis in range(len(extent))]
    drawn = drawn.at[tuple(index_at)].set(low)
    longest = extent.index(max(extent))
    index_at[longest] = (index_at[longest] + 1) % extent[longest]
    return drawn.at[tuple(index_at)].set(top_value)


def shard_levels(stream_key, shape, shards, smallest, largest):
    def one(dim, shards_of):
        heights = jax.random.uniform(jax.random.fold_in(jax.random.fold_in(stream_key, 6), dim), (shards_of,), jnp.float32, smallest / len(shards), largest / len(shards))
        return jnp.repeat(jnp.exp(heights), shape[dim] // shards_of).reshape((-1,) + (1,) * (len(shape) - dim - 1))

    level = one(*shards[0])
    for cut in shards[1:]:
        level = level * one(*cut)
    return level


def shared_out(stream_key, own, number, rows, amount, top, reach, skew):
    ranking = jax.random.permutation(stream_key, amount)
    packed, ordinary = load_shares(amount, rows * top, reach, skew, True), load_shares(amount, rows * top, reach, skew, False)
    places = jnp.arange(amount)

    def named(lengths, rotation):
        used = int((lengths > 0).sum())
        fixed = max(1, used // 4)
        passed = fixed + (places - fixed + rotation * (used - fixed)) % max(1, amount - fixed)
        return jnp.zeros((amount,), jnp.int32).at[ranking[jnp.where(places < fixed, places, passed)]].set(jnp.asarray(lengths, jnp.int32))

    lengths = jnp.where(number % 4 == 0, named(packed, number // 4), named(ordinary, number - number // 4 - 1))
    mixed = jax.random.permutation(jax.random.fold_in(own, 3), amount)
    source_of, taker = mixed[0:amount // 2 * 2:2], mixed[1:amount // 2 * 2:2]
    room = jnp.minimum(lengths[source_of] - 1, reach - lengths[taker]) // 2
    room = jnp.where((source_of == ranking[0]) | (taker == ranking[0]) | (lengths[taker] == 0), 0, jnp.maximum(room, 0))
    passed = jax.random.randint(jax.random.fold_in(own, 4), (amount // 2,), 0, 1 << 20) % (room + 1)
    lengths = lengths.at[source_of].add(-passed).at[taker].add(passed)
    items = jnp.searchsorted(jnp.cumsum(lengths), jnp.arange(rows * top), side="right").astype(jnp.int32)
    table = items.reshape(top, rows).T
    table = table[jax.random.permutation(jax.random.fold_in(own, 1), rows)]
    rotation = jax.random.randint(jax.random.fold_in(own, 2), (rows, 1), 0, top)
    return jnp.take_along_axis(table, (jnp.arange(top)[None, :] + rotation) % top, axis=1)


def load_shares(count, total, reach, slope, full):
    portions = [(1 << 20) // math.isqrt(rank ** slope) + 1 for rank in range(1, count + 1)]
    largest = reach if full else min(reach, max(-(-total // count), total * portions[0] // sum(portions)))
    least = 1 if total - largest >= count - 1 else 0
    holding, surplus = [largest] + [least] * (count - 1), total - largest - least * (count - 1)
    while surplus > 0:
        free = [i for i in range(1, count) if holding[i] < largest] or [i for i in range(1, count) if holding[i] < reach]
        mass, remaining = sum([portions[i] for i in free]), surplus
        for i in free:
            extra = min(reach - holding[i], max(1, remaining * portions[i] // mass), surplus)
            holding[i] = holding[i] + extra
            surplus = surplus - extra
    return np.array(holding)


def bell_draw(rng, extent, scale, limit, shards=(), held_as=jnp.bfloat16):
    entries = jax.random.normal(rng, extent, jnp.float32) * scale
    if len(shards) > 0:
        entries = shard_levels(rng, extent, shards, -0.22, 0.18) * entries
    return jnp.clip(entries, min=-limit, max=limit).astype(held_as)


def setup_inputs(seed: int = 0) -> dict:
    key_list = jax.random.split(jax.random.key(seed), 9)
    control = bell_draw(key_list[0], (FIELDS, LEV, NLAT, NLON), 1.0, 6.0, ((2, 4), (3, 8)), jnp.float32)
    kappa = jnp.clip(jnp.exp(math.log(0.5) - 0.6931472 * jax.random.uniform(key_list[1], (FIELDS, LEV, NLAT, NLON), jnp.float32) ** shard_levels(key_list[1], (FIELDS, LEV, NLAT, NLON), ((2, 4), (3, 8)), -0.2, 0.2)), 0.25, 0.5)
    pc_obs = bell_draw(key_list[2], (BLOCKS, SND, PCS), 1.0, 6.0, ((0, 32),))
    owner_keys = jax.random.split(jax.random.fold_in(key_list[3], 1), BLOCKS // NB_DEV)
    owner_turns = jax.random.permutation(jax.random.fold_in(key_list[3], 3), BLOCKS // NB_DEV)
    owner = jax.vmap(lambda own, number: shared_out(jax.random.fold_in(key_list[3], 2), own, number, NB_DEV, DEVICES, 1, CAP, 2))(owner_keys, owner_turns).reshape((BLOCKS, 1))
    columns = place_ends(jax.random.randint(key_list[4], (BLOCKS, SND), 0, LAT_DEV * LON_DEV), jax.random.fold_in(key_list[4], 1), 0, (LAT_DEV * LON_DEV) - 1).astype(jnp.int32)
    counts = draw_counts(jax.random.fold_in(key_list[8], 71), 0)
    jacobian = bell_draw(key_list[6], (FIELDS * LEV, PCS), (FIELDS * LEV) ** -0.5, 0.3125)
    obs_weight = jnp.clip(jnp.exp(jax.random.uniform(key_list[7], (PCS,), jnp.float32, math.log(0.3), math.log(3.0))), 0.3, 3.0)
    return dict(control=control, kappa=kappa, pc_obs=pc_obs, owner=owner, columns=columns, counts=counts, jacobian=jacobian, obs_weight=obs_weight)


def relax(field, coef):
    centre = field[..., 1:-1, 1:-1]
    inner = coef[..., 1:-1, 1:-1]
    result = centre + inner * coef[..., :-2, 1:-1] * (field[..., :-2, 1:-1] - centre)
    result = result + inner * coef[..., 2:, 1:-1] * (field[..., 2:, 1:-1] - centre)
    result = result + inner * coef[..., 1:-1, :-2] * (field[..., 1:-1, :-2] - centre)
    result = result + inner * coef[..., 1:-1, 2:] * (field[..., 1:-1, 2:] - centre)
    return result


def pad_grid(plane):
    plane = jnp.pad(plane, ((1, 1), (0, 0)))
    return jnp.concatenate([plane[:, -1:], plane, plane[:, :1]], axis=1)


def spread(pair):
    field, coef = pair
    coef_pad = pad_grid(coef)
    for repeat in range(STEPS):
        field = relax(pad_grid(field), coef_pad)
    return field


def reference(control, kappa, pc_obs, owner, columns, counts, jacobian, obs_weight):
    depth = FIELDS * LEV
    flat_v = control.reshape(depth, NLAT, NLON)
    flat_k = kappa.reshape(depth, NLAT, NLON)
    state = lax.map(spread, (flat_v, flat_k))
    state_b = state.astype(jnp.bfloat16).reshape(depth, NLAT * NLON)
    order = jnp.arange(SND, dtype=jnp.int32)

    def visit(total, item):
        own, cols, count_part, obs_part = item
        glat = ((own // N_LON) * LAT_DEV)[:, None] + cols // LON_DEV
        glon = ((own % N_LON) * LON_DEV)[:, None] + cols % LON_DEV
        cell = (glat * NLON + glon).reshape(-1).astype(jnp.int32)
        picked = state_b[:, cell]
        model = lax.dot_general(picked, jacobian, (((0,), (0,)), ((), ())), preferred_element_type=jnp.float32)
        valid = (order[None, :] < count_part[:, None]).astype(jnp.float32).reshape(-1, 1)
        misfit = (model - obs_part.reshape(-1, PCS).astype(jnp.float32)) * obs_weight[None, :] * valid
        return total.at[cell].add(misfit), None

    start = jnp.zeros((NLAT * NLON, PCS), jnp.float32)
    items = (owner[:, 0].reshape(DEVICES, NB_DEV), columns.reshape(DEVICES, NB_DEV, SND),
             counts.reshape(DEVICES, NB_DEV), pc_obs.reshape(DEVICES, NB_DEV, SND, PCS))
    total = lax.scan(visit, start, items)[0]
    back = lax.dot_general(jacobian, total.astype(jnp.bfloat16), (((1,), (1,)), ((), ())),
                           preferred_element_type=jnp.float32)
    adjoint = lax.map(spread, (back.reshape(depth, NLAT, NLON), flat_k))
    return control + adjoint.reshape(control.shape)
```

```python
import functools

import jax
import jax.numpy as jnp
from jax import lax
from jax.experimental import pallas as pl
from jax.experimental.pallas import tpu as pltpu
from jax.sharding import PartitionSpec as P

CAP = 2
STEPS = 4
LANES = 128
EDGE = 8
HEAD = 4
COUNT_BASE = 64
MESH = pl.DeviceIdType.MESH
F32 = jnp.float32
BF16 = jnp.bfloat16
SIDES = ((0, -1), (0, 1), (-1, -1), (-1, 1), (1, -1), (1, 1))


def iota(shape, dim):
    return lax.broadcasted_iota(jnp.int32, shape, dim)


def pack_kernel(group, owner_ref, obs_ref, columns_ref, counts_ref, out_ref, wide, source):
    blocks = columns_ref.shape[0]
    comps = obs_ref.shape[0]
    height = out_ref.shape[1]
    slots = source.shape[0]

    @pl.when(pl.program_id(0) == 0)
    def _():
        @pl.loop(0, slots)
        def _(t):
            source[t] = -1

        @pl.loop(0, blocks)
        def _(b):
            first = owner_ref[b] * CAP
            source[jnp.where(source[first] < 0, first, first + 1)] = b

        columns = columns_ref[...]
        valid = iota(columns.shape, 1) < counts_ref[...]
        low = jnp.bitwise_and(columns, 31)
        high = jnp.where(valid, jnp.right_shift(columns - low, 5), -1)
        wide[0:blocks, :] = jnp.ones(columns.shape, F32)
        wide[blocks : 2 * blocks, :] = high.astype(F32)
        wide[2 * blocks : 3 * blocks, :] = low.astype(F32)
        wide[3 * blocks : 4 * blocks, :] = jnp.zeros(columns.shape, F32)

        @pl.loop(0, comps, unroll=4)
        def _(c):
            start = pl.multiple_of((HEAD + c) * blocks, blocks)
            wide[pl.ds(start, blocks), :] = obs_ref[c].astype(F32)

        rest = (HEAD + comps) * blocks
        if rest < wide.shape[0]:
            wide[rest:, :] = jnp.zeros((wide.shape[0] - rest, wide.shape[1]), F32)

    for g in range(group):
        block = source[pl.program_id(0) * group + g]
        rows = wide[pl.ds(jnp.maximum(block, 0), height, stride=blocks), :]
        out_ref[g] = jnp.where(block < 0, -1.0, rows).astype(BF16)


def pack(pc_obs, owner, columns, counts, peers, height):
    blocks, soundings, comps = pc_obs.shape
    slots = peers * CAP
    group = 8
    return pl.pallas_call(
        functools.partial(pack_kernel, group),
        out_shape=jax.ShapeDtypeStruct((slots, height, soundings), BF16),
        grid_spec=pltpu.PrefetchScalarGridSpec(
            num_scalar_prefetch=1,
            grid=(slots // group,),
            in_specs=[
                pl.BlockSpec((comps, blocks, soundings), lambda i, s: (0, 0, 0)),
                pl.BlockSpec((blocks, soundings), lambda i, s: (0, 0)),
                pl.BlockSpec((blocks, 1), lambda i, s: (0, 0)),
            ],
            out_specs=pl.BlockSpec((group, height, soundings), lambda i, s: (i, 0, 0)),
            scratch_shapes=[
                pltpu.VMEM((height * blocks, soundings), F32),
                pltpu.SMEM((slots,), jnp.int32),
            ],
        ),
        compiler_params=pltpu.CompilerParams(vmem_limit_bytes=56 * 2**20),
    )(owner[:, 0], jnp.transpose(pc_obs, (2, 0, 1)), columns, counts[:, None])


def main_kernel(
    n_lat, n_lon, planes, parts, order,
    sent, control, kappa, jac, weight, out,
    recv, part_out, part_in, sums, number, model,
    field, coef, south, east, raw, band_out, band_in, tile_f, tile_out, tile_in,
    total, total_north, total_south, side_out, side_in,
    load_sem, own_sem, blk_send, blk_recv, part_send, part_recv,
    band_send, band_recv, tile_send, tile_recv, row_send, row_recv, side_send, side_recv, store_sem,
):
    lat, lon = lax.axis_index("lat"), lax.axis_index("lon")
    height, cells = sums.shape
    chunks, extent, wide, _ = field.shape
    rows = extent - 2 * STEPS
    width = wide - 2 * EDGE
    area = planes * rows
    step_rows = LANES * rows

    def remote(src, dst, send, recv_, to):
        return pltpu.make_async_remote_copy(
            src_ref=src, dst_ref=dst, send_sem=send, recv_sem=recv_, device_id=to, device_id_type=MESH
        )

    def block_copy(d, h, i):
        lo, size = parts[h]
        return remote(
            sent.at[lax.rem(lat + order[d], n_lat), lax.rem(lon + i, n_lon), :, pl.ds(lo, size), :],
            recv.at[d, i, :, pl.ds(lo, size), :],
            blk_send.at[d, h, i], blk_recv.at[d, h, i], (lat, lax.rem(lon + i, n_lon)),
        )

    def own_copy(d):
        return pltpu.make_async_copy(
            sent.at[lax.rem(lat + order[d], n_lat), lon], recv.at[d, 0], own_sem.at[d]
        )

    def part_copy(d, h):
        lo, size = parts[h]
        return remote(
            part_out.at[d, pl.ds(lo, size), :], part_in.at[d, pl.ds(lo, size), :],
            part_send.at[d, h], part_recv.at[d, h], (lax.rem(lat + order[d], n_lat), lon),
        )

    def band_copy(a, s):
        return remote(
            band_out.at[a, pl.ds((1 - s) * (rows - STEPS), STEPS)], band_in.at[a, s],
            band_send.at[a, s], band_recv.at[a, s], (lat + (1 - 2 * s), lon),
        )

    def peer(k):
        return (lat - SIDES[k][0], lax.rem(lon - SIDES[k][1] + n_lon, n_lon))

    def tile_copy(a, k):
        return remote(tile_out.at[a], tile_in.at[a, k], tile_send.at[a, k], tile_recv.at[a, k], peer(k))

    def row_copy(h, s):
        lo, size = parts[h]
        span = STEPS * width
        return remote(
            total.at[pl.ds(lo, size), pl.ds((1 - s) * (rows * width - span), span)],
            (total_north if s == 0 else total_south).at[pl.ds(lo, size), :],
            row_send.at[h, s], row_recv.at[h, s], (lat + (1 - 2 * s), lon),
        )

    def side_copy(h, k):
        lo, size = parts[h]
        return remote(
            side_out.at[pl.ds(lo, size), :], side_in.at[k, pl.ds(lo, size), :],
            side_send.at[h, k], side_recv.at[h, k], peer(k),
        )

    def has(step):
        return (lat + step >= 0) & (lat + step < n_lat)

    def only(step, act):
        if step == 0:
            act()
        else:
            pl.when(has(step))(act)

    for d in range(n_lat):
        for h in range(len(parts)):
            @pl.loop(1, n_lon)
            def _(i):
                block_copy(d, h, i).start()
        own_copy(d).start()

    loads = [
        pltpu.make_async_copy(ref, raw.at[a, pl.ds(0, area), :], load_sem.at[a])
        for a, ref in enumerate((control, kappa))
    ]
    for load in loads:
        load.start()
    sub = iota((EDGE, LANES), 0)

    for a, grid in enumerate((field, coef)):
        loads[a].wait()
        if chunks * step_rows > area:
            raw[a, area:, :] = jnp.zeros((chunks * step_rows - area, width), F32)

        @pl.loop(0, rows)
        def _(r):
            for j in range(chunks):
                turned = jnp.transpose(raw[a, pl.ds(j * step_rows + r, LANES, stride=rows), :])
                grid[j, STEPS + r, EDGE : EDGE + width, :] = turned
                band_out[a, r, j] = turned.astype(BF16)
                tile_f[j, r] = jnp.where(sub < STEPS, turned[:EDGE], turned[width - EDGE :])

        tile_out[a] = tile_f[...].reshape(chunks, rows * EDGE, LANES).astype(BF16)
        for s in range(2):
            only(1 - 2 * s, lambda: band_copy(a, s).start())
        for k in range(len(SIDES)):
            only(-SIDES[k][0], lambda: tile_copy(a, k).start())

    def reduce(d, h):
        lo, size = parts[h]

        @pl.loop(1, n_lon)
        def _(i):
            block_copy(d, h, i).wait_recv()

        if h == 0:
            own_copy(d).wait()
        heads = [recv[d, i, k, 0:16, :].astype(F32) for i in range(n_lon) for k in range(CAP)]
        code = jnp.concatenate([x[1:2] * 32.0 + x[2:3] for x in heads], axis=1).astype(jnp.int32)
        tile = 256
        line = iota((size, tile), 0)

        @pl.loop(0, cells // tile)
        def _(n):
            obs = jnp.concatenate(
                [recv[d, i, k, lo : lo + size, :] for i in range(n_lon) for k in range(CAP)], axis=1
            )
            hot = jnp.where(iota((tile, code.shape[1]), 0) == code - n * tile, 1.0, 0.0).astype(BF16)
            part = lax.dot_general(obs, hot, (((1,), (1,)), ((), ())), preferred_element_type=F32)
            at = pl.ds(pl.multiple_of(n * tile, tile), tile)
            if order[d] == 0:
                sums[lo : lo + size, at] = part
            else:
                if h == 0:
                    count = part[0:1]
                    high = jnp.floor(count * (1.0 / COUNT_BASE))
                    part = jnp.where(line == 0, count - high * COUNT_BASE, jnp.where(line == 1, high, part))
                part_out[d, lo : lo + size, at] = part.astype(BF16)

        if order[d] != 0:
            part_copy(d, h).start()

    def fill_edges(a, grid):
        def band(s):
            first = (rows + STEPS) * s

            def arrived():
                band_copy(a, s).wait_recv()
                for r in range(STEPS):
                    for j in range(chunks):
                        grid[j, first + r, EDGE : EDGE + width, :] = band_in[a, s, r, j].astype(F32)

            def closed():
                for r in range(STEPS):
                    for j in range(chunks):
                        grid[j, first + r] = jnp.zeros((wide, LANES), F32)

            pl.when(has(2 * s - 1))(arrived)
            pl.when(jnp.logical_not(has(2 * s - 1)))(closed)

        for s in range(2):
            band(s)

        def sides(west, count, place, source_row):
            tile_copy(a, west).wait_recv()
            tile_copy(a, west + 1).wait_recv()
            shape = (chunks, rows, EDGE, LANES)
            both = [tile_in[a, k].astype(F32).reshape(shape) for k in (west, west + 1)]
            for j in range(chunks):
                for r in range(count):
                    tile = jnp.where(sub < STEPS, both[1][j, source_row + r], both[0][j, source_row + r])
                    grid[j, place + r, 0:EDGE, :] = tile
                    grid[j, place + r, EDGE + width :, :] = tile

        sides(0, rows, STEPS, 0)
        only(-1, lambda: sides(2, STEPS, 0, rows - STEPS))
        only(1, lambda: sides(4, STEPS, rows + STEPS, 0))

    def spread():
        for step in range(STEPS):
            first, last = step + 1, extent - 1 - step

            @pl.loop(0, chunks)
            def _(j):
                here = field[j, first]
                above = south[j, first - 1] * (here - field[j, first - 1])

                def line(r, carry):
                    here, above = carry
                    below = field[j, r + 1]
                    down = south[j, r] * (below - here)
                    along = east[j, r] * (pltpu.roll(here, wide - 1, 0) - here)
                    field[j, r] = here + (down - above) + (along - pltpu.roll(along, 1, 0))
                    return below, down

                lax.fori_loop(first, last, line, (here, above))

    reduce(0, 0)
    for h in range(1, len(parts)):
        reduce(0, h)

    fill_edges(1, coef)

    @pl.loop(0, chunks)
    def _(j):
        @pl.loop(0, extent - 1)
        def _(r):
            here = coef[j, r]
            south[j, r] = here * coef[j, r + 1]
            east[j, r] = here * pltpu.roll(here, wide - 1, 0)

    fill_edges(0, field)
    spread()

    @pl.loop(0, rows)
    def _(r):
        state = jnp.concatenate(
            [field[j, STEPS + r, EDGE : EDGE + width, :].astype(BF16) for j in range(chunks)], axis=1
        )
        model[:, pl.ds(pl.multiple_of(r * width, width), width)] = lax.dot_general(
            jac[...], state, (((1,), (1,)), ((), ())), preferred_element_type=F32
        )

    for d in range(1, n_lat):
        for h in range(len(parts)):
            reduce(d, h)

    for s, ref in enumerate((total_north, total_south)):
        def blank():
            ref[...] = jnp.zeros(ref.shape, BF16)
            side_in[2 + 2 * s] = jnp.zeros(side_in.shape[1:], BF16)
            side_in[3 + 2 * s] = jnp.zeros(side_in.shape[1:], BF16)

        pl.when(jnp.logical_not(has(2 * s - 1)))(blank)

    away = [d for d in range(n_lat) if order[d] != 0]
    for h, (lo, size) in enumerate(parts):
        for d in away:
            part_copy(d, h).wait_recv()
        if h == 0:
            count = sums[0:8, :][0:1]
            for d in away:
                digits = part_in[d, 0:16, :].astype(F32)
                count = count + digits[0:1] + digits[1:2] * COUNT_BASE
            number[...] = jnp.broadcast_to(count, number.shape)
        lane = iota((size, width), 1)
        scale = weight[lo : lo + size, :]
        tile = jnp.zeros((size, width), F32)
        for r in range(rows):
            at = slice(r * width, (r + 1) * width)
            summed = sums[lo : lo + size, at]
            for d in away:
                summed = summed + part_in[d, lo : lo + size, at].astype(F32)
            value = ((number[0:1, at] * model[lo : lo + size, at] - summed) * scale).astype(BF16)
            total[lo : lo + size, at] = value
            value = value.astype(F32)
            ends = jnp.where(lane < STEPS, value, pltpu.roll(value, EDGE, 1))
            if r > 0:
                ends = pltpu.roll(ends, EDGE * r, 1)
            tile = jnp.where((lane >= EDGE * r) & (lane < EDGE * (r + 1)), ends, tile)
        side_out[lo : lo + size, :] = tile.astype(BF16)
        for s in range(2):
            only(1 - 2 * s, lambda: row_copy(h, s).start())
        for k in range(len(SIDES)):
            only(-SIDES[k][0], lambda: side_copy(h, k).start())

    def back(values):
        return lax.dot_general(values, jac[...], (((0,), (0,)), ((), ())), preferred_element_type=F32)

    def put_row(values, r):
        result = back(values)
        for j in range(chunks):
            field[j, r, EDGE : EDGE + width, :] = result[:, j * LANES : (j + 1) * LANES]

    @pl.loop(0, rows)
    def _(r):
        put_row(total[:, pl.ds(pl.multiple_of(r * width, width), width)], STEPS + r)

    for h in range(len(parts)):
        for k in range(len(SIDES)):
            only(SIDES[k][0], lambda: side_copy(h, k).wait_recv())
        for s in range(2):
            only(2 * s - 1, lambda: row_copy(h, s).wait_recv())

    lane = iota((height, width), 1)
    west_east = [
        jnp.where(lax.rem(lane, EDGE) < STEPS, side_in[k + 1].astype(F32), side_in[k].astype(F32))
        for k in (0, 2, 4)
    ]
    middle = pltpu.roll(west_east[0], STEPS * EDGE, 1)
    upper = pltpu.roll(west_east[1], width - (rows - STEPS) * EDGE, 1)
    lower = pltpu.roll(west_east[2], (rows + STEPS) * EDGE, 1)
    side = jnp.where(
        lane < STEPS * EDGE, upper, jnp.where(lane < (rows + STEPS) * EDGE, middle, lower)
    )
    result = back(side.astype(BF16))
    for j in range(chunks):
        for r in range(extent):
            piece = result[r * EDGE : (r + 1) * EDGE, j * LANES : (j + 1) * LANES]
            field[j, r, 0:EDGE, :] = piece
            field[j, r, EDGE + width :, :] = piece

    @pl.loop(0, STEPS)
    def _(r):
        at = pl.ds(pl.multiple_of(r * width, width), width)
        put_row(total_north[:, at], r)
        put_row(total_south[:, at], STEPS + rows + r)

    spread()

    @pl.loop(0, rows)
    def _(r):
        for j in range(chunks):
            at = pl.ds(j * step_rows + r, LANES, stride=rows)
            raw[0, at, :] = raw[0, at, :] + jnp.transpose(field[j, STEPS + r, EDGE : EDGE + width, :])

    store = pltpu.make_async_copy(raw.at[0, pl.ds(0, area), :], out, store_sem)
    store.start()

    for d in range(n_lat):
        for h in range(len(parts)):
            @pl.loop(1, n_lon)
            def _(i):
                block_copy(d, h, i).wait_send()
    for h in range(len(parts)):
        for d in away:
            part_copy(d, h).wait_send()
        for s in range(2):
            only(1 - 2 * s, lambda: row_copy(h, s).wait_send())
        for k in range(len(SIDES)):
            only(-SIDES[k][0], lambda: side_copy(h, k).wait_send())
    for a in range(2):
        for s in range(2):
            only(1 - 2 * s, lambda: band_copy(a, s).wait_send())
        for k in range(len(SIDES)):
            only(-SIDES[k][0], lambda: tile_copy(a, k).wait_send())
    store.wait()


def per_device(control, kappa, pc_obs, owner, columns, counts, jacobian, obs_weight):
    n_lat, n_lon = lax.axis_size("lat"), lax.axis_size("lon")
    fields, levels, rows, width = control.shape
    soundings, comps = pc_obs.shape[1:]
    planes = fields * levels
    cells = rows * width
    height = -(-(comps + HEAD) // 16) * 16
    chunks = -(-planes // LANES)
    extent, wide = rows + 2 * STEPS, width + 2 * EDGE
    half = -(-height // 32) * 16
    parts = ((0, half), (half, height - half))
    order = tuple(sorted(range(1, n_lat), key=lambda d: -min(d, n_lat - d))) + (0,)
    sent = pack(pc_obs, owner, columns, counts, n_lat * n_lon, height)
    sent = sent.reshape(n_lat, n_lon, CAP, height, soundings)
    room = (HEAD, height - HEAD - comps)
    jac = jnp.pad(jnp.transpose(jacobian), (room, (0, chunks * LANES - planes)))
    weight = jnp.pad(obs_weight[:, None], (room, (0, 0)))
    n_parts, n_sides = len(parts), len(SIDES)
    grid = pltpu.VMEM((chunks, extent, wide, LANES), F32)
    dma = pltpu.SemaphoreType.DMA
    result = pl.pallas_call(
        functools.partial(main_kernel, n_lat, n_lon, planes, parts, order),
        out_shape=jax.ShapeDtypeStruct((planes * rows, width), F32),
        in_specs=[pl.BlockSpec(memory_space=pl.ANY)] * 3
        + [pl.BlockSpec(memory_space=pltpu.VMEM)] * 2,
        out_specs=pl.BlockSpec(memory_space=pl.ANY),
        scratch_shapes=[
            pltpu.VMEM((n_lat, n_lon, CAP, height, soundings), BF16),
            pltpu.VMEM((n_lat - 1, height, cells), BF16),
            pltpu.VMEM((n_lat - 1, height, cells), BF16),
            pltpu.VMEM((height, cells), F32),
            pltpu.VMEM((8, cells), F32),
            pltpu.VMEM((height, cells), F32),
            grid, grid, grid, grid,
            pltpu.VMEM((2, chunks * LANES * rows, width), F32),
            pltpu.VMEM((2, rows, chunks, width, LANES), BF16),
            pltpu.VMEM((2, 2, STEPS, chunks, width, LANES), BF16),
            pltpu.VMEM((chunks, rows, EDGE, LANES), F32),
            pltpu.VMEM((2, chunks, rows * EDGE, LANES), BF16),
            pltpu.VMEM((2, n_sides, chunks, rows * EDGE, LANES), BF16),
            pltpu.VMEM((height, cells), BF16),
            pltpu.VMEM((height, STEPS * width), BF16),
            pltpu.VMEM((height, STEPS * width), BF16),
            pltpu.VMEM((height, width), BF16),
            pltpu.VMEM((n_sides, height, width), BF16),
            dma((2,)), dma((n_lat,)),
            dma((n_lat, n_parts, n_lon)), dma((n_lat, n_parts, n_lon)),
            dma((n_lat, n_parts)), dma((n_lat, n_parts)),
            dma((2, 2)), dma((2, 2)), dma((2, n_sides)), dma((2, n_sides)),
            dma((n_parts, 2)), dma((n_parts, 2)), dma((n_parts, n_sides)), dma((n_parts, n_sides)),
            dma,
        ],
        compiler_params=pltpu.CompilerParams(vmem_limit_bytes=60 * 2**20, has_side_effects=True),
    )(
        sent, control.reshape(planes * rows, width), kappa.reshape(planes * rows, width), jac, weight
    )
    return result.reshape(control.shape)


def solution(mesh):
    placed = (
        P(None, None, "lat", "lon"),
        P(None, None, "lat", "lon"),
        P(("lat", "lon"), None, None),
        P(("lat", "lon"), None),
        P(("lat", "lon"), None),
        P(("lat", "lon")),
        P(),
        P(),
    )
    return jax.shard_map(
        per_device,
        mesh=mesh,
        in_specs=placed,
        out_specs=P(None, None, "lat", "lon"),
        check_vma=False,
    )
```

```python
import functools

import jax
import jax.numpy as jnp
from jax import lax
from jax.experimental import pallas as pl
from jax.experimental.pallas import tpu as pltpu
from jax.sharding import PartitionSpec as P

CAP = 2
STEPS = 4
LANES = 128
GROUP = 16
EDGE = 8
TAIL = 4
COUNT_BASE = 64
TILE = 256
MESH = pl.DeviceIdType.MESH
F32 = jnp.float32
BF16 = jnp.bfloat16
SIDES = ((0, -1), (0, 1), (-1, -1), (-1, 1), (1, -1), (1, 1))


def iota(shape, dim):
    return lax.broadcasted_iota(jnp.int32, shape, dim)


def to_column(row, size):
    shape = (size, row.shape[1])
    return jnp.sum(jnp.where(iota(shape, 0) == iota(shape, 1), row, 0.0), axis=1, keepdims=True)


def digits(columns, counts):
    low = jnp.bitwise_and(columns, 31)
    valid = iota(columns.shape, 1).astype(F32) < counts
    high = jnp.where(valid, jnp.right_shift(columns - low, 5) + 1, 0)
    zero = jnp.zeros(columns.shape, F32)
    return [zero + 1.0, high.astype(F32), low.astype(F32), zero]


def pack_kernel(group, owner_ref, obs_ref, columns_ref, counts_ref, out_ref, wide, source):
    blocks = columns_ref.shape[0]
    comps = obs_ref.shape[0]
    height = out_ref.shape[1]
    slots = source.shape[0]

    @pl.when(pl.program_id(0) == 0)
    def _():
        @pl.loop(0, slots)
        def _(t):
            source[t] = -1

        @pl.loop(0, blocks)
        def _(b):
            first = owner_ref[b] * CAP
            source[jnp.where(source[first] < 0, first, first + 1)] = b

        @pl.loop(0, comps, unroll=4)
        def _(c):
            wide[pl.ds(pl.multiple_of(c * blocks, blocks), blocks), :] = obs_ref[c].astype(F32)

        for k, row in enumerate(digits(columns_ref[...], to_column(counts_ref[...].astype(F32), blocks))):
            wide[(comps + k) * blocks : (comps + k + 1) * blocks, :] = row

    for g in range(group):
        block = source[pl.program_id(0) * group + g]
        rows = wide[pl.ds(jnp.maximum(block, 0), height, stride=blocks), :]
        out_ref[g] = jnp.where(block < 0, 0.0, rows).astype(BF16)


def pack(obs, owner, columns, counts, peers, height):
    comps, blocks, soundings = obs.shape
    slots = peers * CAP
    group = 8
    return pl.pallas_call(
        functools.partial(pack_kernel, group),
        out_shape=jax.ShapeDtypeStruct((slots, height, soundings), BF16),
        grid_spec=pltpu.PrefetchScalarGridSpec(
            num_scalar_prefetch=1,
            grid=(slots // group,),
            in_specs=[
                pl.BlockSpec((comps, blocks, soundings), lambda i, s: (0, 0, 0)),
                pl.BlockSpec((blocks, soundings), lambda i, s: (0, 0)),
                pl.BlockSpec((1, blocks), lambda i, s: (0, 0)),
            ],
            out_specs=pl.BlockSpec((group, height, soundings), lambda i, s: (i, 0, 0)),
            scratch_shapes=[
                pltpu.VMEM((height * blocks, soundings), F32),
                pltpu.SMEM((slots,), jnp.int32),
            ],
        ),
        compiler_params=pltpu.CompilerParams(vmem_limit_bytes=56 * 2**20),
    )(owner[:, 0], obs, columns, counts[None, :])


def main_kernel(n_lat, n_lon, planes, parts, packed, *refs):
    source, control, kappa, jac_in, weight_in, owner, counts, columns, out, *refs = refs
    sent, obs, codes = (source, None, None) if packed else refs[:3]
    (
        recv, ring, part_out, part_in, sums, number, model, jac, scale,
        field, coef, east, raw, band_out, band_in, tile_f, tile_out, tile_in,
        total, total_north, total_south, side_out, side_in,
        load_sem, own_sem, blk_send, blk_recv, part_send, part_recv,
        band_send, band_recv, tile_send, tile_recv, row_send, row_recv, side_send, side_recv, store_sem,
    ) = refs if packed else refs[3:]
    lat, lon = lax.axis_index("lat"), lax.axis_index("lon")
    height, cells = sums.shape
    comps = jac_in.shape[0]
    chunks, extent, wide, _ = field.shape
    rows = extent - 2 * STEPS
    width = wide - 2 * EDGE
    area = planes * rows
    step_rows = LANES * rows
    slots = n_lon * CAP
    band_rows = STEPS * EDGE

    def plane_of(k):
        mirrored = lat >= n_lat - n_lat // 2
        z = jnp.where(mirrored, n_lat - 1 - lat, lat)
        o = jnp.where(k < n_lat - 1 - z, n_lat - 1 - k, k - (n_lat - 1 - z))
        return jnp.where(mirrored, n_lat - 1 - o, o)

    def remote(src, dst, send, recv_, to):
        return pltpu.make_async_remote_copy(
            src_ref=src, dst_ref=dst, send_sem=send, recv_sem=recv_, device_id=to, device_id_type=MESH
        )

    def around(step):
        return lax.rem(lon + step + n_lon, n_lon)

    def has(step):
        return (lat + step >= 0) & (lat + step < n_lat)

    def only(step, act):
        if step == 0:
            act()
        else:
            pl.when(has(step))(act)

    def slot_of(k):
        return plane_of(k) if packed else k

    def block_copy(k, h, i):
        lo, size = parts[h]
        return remote(
            sent.at[slot_of(k), around(i), :, pl.ds(lo, size), :], recv.at[k, i, :, pl.ds(lo, size), :],
            blk_send.at[k, h, i], blk_recv.at[k, h, i], (lat, around(i)),
        )

    def own_copy(k, h):
        lo, size = parts[h]
        return pltpu.make_async_copy(
            sent.at[slot_of(k), lon, :, pl.ds(lo, size), :],
            recv.at[k, 0, :, pl.ds(lo, size), :], own_sem.at[k, h],
        )

    def part_copy(k, h, slot, to):
        lo, size = parts[h]
        return remote(
            part_out.at[k, pl.ds(lo, size), :], part_in.at[slot, pl.ds(lo, size), :],
            part_send.at[k, h], part_recv.at[slot, h], (to, lon),
        )

    def part_sent(k, h):
        o = plane_of(k)
        north = o < lat
        slot = jnp.where(north & (o == lat - 1), n_lat, o)
        return part_copy(k, h, slot, jnp.where(north, lat - 1, lat + 1))

    def band_copy(a, s):
        return remote(
            band_out.at[a, pl.ds((1 - s) * (rows - STEPS), STEPS)], band_in.at[a, s],
            band_send.at[a, s], band_recv.at[a, s], (lat + (1 - 2 * s), lon),
        )

    def peer(k):
        return (lat - SIDES[k][0], around(-SIDES[k][1]))

    def side_span(k):
        step = SIDES[k][0]
        if step == 0:
            return pl.ds(0, rows * EDGE)
        return pl.ds((rows * EDGE - band_rows) if step < 0 else 0, band_rows)

    def tile_copy(a, k):
        span = side_span(k)
        return remote(
            tile_out.at[a, :, span, :], tile_in.at[a, k, :, span, :],
            tile_send.at[a, k], tile_recv.at[a, k], peer(k),
        )

    def row_copy(h, s):
        lo, size = parts[h]
        span = STEPS * width
        return remote(
            total.at[pl.ds(lo, size), pl.ds((1 - s) * (rows * width - span), span)],
            (total_north if s == 0 else total_south).at[pl.ds(lo, size), :],
            row_send.at[h, s], row_recv.at[h, s], (lat + (1 - 2 * s), lon),
        )

    def side_copy(k):
        span = side_span(k)
        return remote(
            side_out.at[span, :], side_in.at[k, span, :], side_send.at[k], side_recv.at[k], peer(k)
        )

    barrier = pltpu.get_barrier_semaphore()

    @pl.loop(1, n_lon)
    def _(i):
        pl.semaphore_signal(barrier, inc=1, device_id=(lat, around(i)), device_id_type=MESH)

    for step in (-1, 1):
        def greet():
            for side in (-1, 0, 1):
                pl.semaphore_signal(
                    barrier, inc=1, device_id=(lat + step, around(side)), device_id_type=MESH
                )

        only(step, greet)

    loads = [
        pltpu.make_async_copy(ref, raw.at[a, pl.ds(0, area), :], load_sem.at[a])
        for a, ref in enumerate((control, kappa))
    ]
    if not packed:
        obs_load = pltpu.make_async_copy(source, obs, load_sem.at[2])
        obs_load.start()
    for load in loads:
        load.start()

    if not packed:
        blocks = columns.shape[0]
        names = owner[...].astype(F32)
        square = (blocks, blocks)
        before = (to_column(names, blocks) == names) & (iota(square, 0) < iota(square, 1))
        place = names * CAP + jnp.sum(jnp.where(before, 1.0, 0.0), axis=0, keepdims=True)
        lined = (blocks, GROUP * blocks)
        comb = jnp.where(lax.rem(iota(lined, 1), blocks) == iota(lined, 0), 1.0, 0.0).astype(BF16)
        place = jnp.broadcast_to(place, (16, blocks)).astype(BF16)
        place = jnp.dot(place, comb, preferred_element_type=F32)[0:1].astype(jnp.int32)
        code = digits(columns[...], to_column(counts[...].astype(F32), blocks))
        codes[...] = jnp.concatenate(code, axis=0).astype(BF16)

    def pack_round(k, h):
        shape = (slots * GROUP, GROUP * blocks)
        at = plane_of(k) * slots + jnp.right_shift(iota(shape, 0), 4)
        hit = (place == at) & (jnp.bitwise_and(iota(shape, 0), GROUP - 1) == iota(shape, 1) // blocks)
        pick = jnp.where(hit, 1.0, 0.0).astype(BF16)
        lo, size = parts[h]
        span = GROUP * blocks

        def put(first, values):
            for t in range(slots):
                part = values[t * GROUP : (t + 1) * GROUP].astype(BF16)
                sent[k, t // CAP, t % CAP, pl.ds(first, GROUP), :] = part

        pairs = (min(lo + size, height - GROUP) - lo) // (2 * GROUP)

        @pl.loop(0, pairs)
        def _(p):
            first = pl.multiple_of(lo + p * 2 * GROUP, GROUP)
            start = pl.multiple_of(first * blocks, span)
            both = jnp.concatenate([obs[pl.ds(start, span), :], obs[pl.ds(start + span, span), :]], axis=1)
            values = jnp.dot(pick, both, preferred_element_type=F32)
            put(first, values[:, :LANES])
            put(pl.multiple_of(first + GROUP, GROUP), values[:, LANES:])

        if lo + size == height:
            last = jnp.concatenate([obs[(height - GROUP) * blocks :, :], codes[...]], axis=0)
            put(height - GROUP, jnp.dot(pick, last, preferred_element_type=F32))

    def send_round(k, h):
        if not packed:
            pack_round(k, h)
        if k == 0 and h == 0:
            pl.semaphore_wait(
                barrier, n_lon - 1 + 3 * (has(-1).astype(jnp.int32) + has(1).astype(jnp.int32))
            )

        @pl.loop(1, n_lon)
        def _(i):
            block_copy(k, h, i).start()

        own_copy(k, h).start()

    if not packed:
        obs_load.wait()
    send_round(0, 0)

    sub = iota((EDGE, LANES), 0)
    for a, grid in ((1, coef), (0, field)):
        loads[a].wait()
        if chunks * step_rows > area:
            raw[a, area:, :] = jnp.zeros((chunks * step_rows - area, width), F32)

        @pl.loop(0, rows)
        def _(r):
            for j in range(chunks):
                turned = jnp.transpose(raw[a, pl.ds(j * step_rows + r, LANES, stride=rows), :])
                grid[j, STEPS + r, EDGE : EDGE + width, :] = turned
                band_out[a, r, j] = turned.astype(BF16)
                tile_f[j, r] = jnp.where(sub < STEPS, turned[:EDGE], turned[width - EDGE :])

        tile_out[a] = tile_f[...].reshape(chunks, rows * EDGE, LANES).astype(BF16)
        for s in range(2):
            only(1 - 2 * s, lambda: band_copy(a, s).start())
        for k in range(len(SIDES)):
            only(-SIDES[k][0], lambda: tile_copy(a, k).start())
        if a == 1:
            send_round(0, 1)

    for k in range(1, n_lat):
        for h in range(len(parts)):
            send_round(k, h)

    matrix = jac_in[...].astype(F32)
    matrix = jnp.concatenate([matrix, jnp.zeros((height - comps, planes), F32)], axis=0)
    if chunks * LANES > planes:
        matrix = jnp.concatenate([matrix, jnp.zeros((height, chunks * LANES - planes), F32)], axis=1)
    jac[...] = matrix.astype(BF16)
    scale[...] = jnp.broadcast_to(to_column(weight_in[...], height), scale.shape)

    def pad_line(h):
        return comps - parts[h][0]

    def lanes(n):
        return pl.ds(pl.multiple_of(n * TILE, TILE), TILE)

    def reduce(k, h):
        lo, size = parts[h]

        @pl.loop(1, n_lon)
        def _(i):
            block_copy(k, h, i).wait_recv()

        own_copy(k, h).wait()
        base = height - GROUP
        first = comps - base
        heads = [recv[k, i, c, base:height, :].astype(F32) for i in range(n_lon) for c in range(CAP)]
        code = jnp.concatenate(
            [(x[first + 1 : first + 2] - 1.0) * 32.0 + x[first + 2 : first + 3] for x in heads], axis=1
        ).astype(jnp.int32)

        @pl.loop(0, cells // TILE)
        def _(n):
            values = jnp.concatenate(
                [recv[k, i, c, lo : lo + size, :] for i in range(n_lon) for c in range(CAP)], axis=1
            )
            hot = jnp.where(iota((TILE, code.shape[1]), 0) == code - n * TILE, 1.0, 0.0).astype(BF16)
            part = lax.dot_general(values, hot, (((1,), (1,)), ((), ())), preferred_element_type=F32)
            if k == n_lat - 1:
                sums[lo : lo + size, lanes(n)] = part
                if h == 0:
                    line = pad_line(h)
                    number[:, lanes(n)] = jnp.broadcast_to(part[line : line + 1], (8, TILE))
            else:
                ring[k % 2, lo : lo + size, lanes(n)] = part

        if k < n_lat - 1:
            pl.when(jnp.logical_not(has(-1) & has(1)))(lambda: emit(k, h, False))

    def emit(k, h, joined):
        lo, size = parts[h]
        o = plane_of(k)
        if joined:
            part_copy(k, h, o, lat).wait_recv()

        @pl.loop(0, cells // TILE)
        def _(n):
            value = ring[k % 2, lo : lo + size, lanes(n)]
            if h == 0:
                line = pad_line(h)
                count = value[line : line + 1]
            if joined:
                more = part_in[o, lo : lo + size, lanes(n)].astype(F32)
                value = value + more
                if h == 0:
                    count = count + more[line : line + 1] + more[line + 1 : line + 2] * COUNT_BASE
            if h == 0:
                high = jnp.floor(count * (1.0 / COUNT_BASE))
                at = iota(value.shape, 0)
                value = jnp.where(at == line, count - high * COUNT_BASE, jnp.where(at == line + 1, high, value))
            part_out[k, lo : lo + size, lanes(n)] = value.astype(BF16)

        part_sent(k, h).start()

    def join(k):
        for h in range(len(parts)):
            pl.when(has(-1) & has(1))(lambda: emit(k, h, True))

    def fill_edges(a, grid):
        def band(s):
            first = (rows + STEPS) * s

            def arrived():
                band_copy(a, s).wait_recv()
                for r in range(STEPS):
                    for j in range(chunks):
                        grid[j, first + r, EDGE : EDGE + width, :] = band_in[a, s, r, j].astype(F32)

            def closed():
                for r in range(STEPS):
                    for j in range(chunks):
                        grid[j, first + r] = jnp.zeros((wide, LANES), F32)

            pl.when(has(2 * s - 1))(arrived)
            pl.when(jnp.logical_not(has(2 * s - 1)))(closed)

        for s in range(2):
            band(s)

        def sides(west, count, place, source_row):
            tile_copy(a, west).wait_recv()
            tile_copy(a, west + 1).wait_recv()
            span = slice(source_row * EDGE, (source_row + count) * EDGE)
            shape = (chunks, count, EDGE, LANES)
            both = [tile_in[a, k, :, span, :].astype(F32).reshape(shape) for k in (west, west + 1)]
            for j in range(chunks):
                for r in range(count):
                    tile = jnp.where(sub < STEPS, both[1][j, r], both[0][j, r])
                    grid[j, place + r, 0:EDGE, :] = tile
                    grid[j, place + r, EDGE + width :, :] = tile

        sides(0, rows, STEPS, 0)
        only(-1, lambda: sides(2, STEPS, 0, rows - STEPS))
        only(1, lambda: sides(4, STEPS, rows + STEPS, 0))

    def spread(j):
        for step in range(STEPS):
            first, last = step + 1, extent - 1 - step
            here = field[j, first]
            above = coef[j, first - 1] * (here - field[j, first - 1])

            def line(r, carry):
                here, above = carry
                below = field[j, r + 1]
                down = coef[j, r] * (below - here)
                along = east[j, r] * (pltpu.roll(here, wide - 1, 0) - here)
                field[j, r] = here + (down - above) + (along - pltpu.roll(along, 1, 0))
                return below, down

            lax.fori_loop(first, last, line, (here, above))

    def make_state():
        fill_edges(1, coef)

        @pl.loop(0, chunks)
        def _(j):
            @pl.loop(0, extent - 1)
            def _(r):
                here = coef[j, r]
                east[j, r] = here * pltpu.roll(here, wide - 1, 0)
                coef[j, r] = here * coef[j, r + 1]

        fill_edges(0, field)
        pl.loop(0, chunks)(spread)

        @pl.loop(0, rows)
        def _(r):
            state = jnp.concatenate(
                [field[j, STEPS + r, EDGE : EDGE + width, :].astype(BF16) for j in range(chunks)], axis=1
            )
            model[:, pl.ds(pl.multiple_of(r * width, width), width)] = lax.dot_general(
                jac[...], state, (((1,), (1,)), ((), ())), preferred_element_type=F32
            )

    for k in range(n_lat - 1):
        for h in range(len(parts)):
            reduce(k, h)
        if k > 0:
            join(k - 1)
        if k == min(1, n_lat - 2):
            make_state()
    join(n_lat - 2)
    for h in range(len(parts)):
        reduce(n_lat - 1, h)

    for s, ref in enumerate((total_north, total_south)):
        def blank():
            ref[...] = jnp.zeros(ref.shape, BF16)
            side_in[2 + 2 * s] = jnp.zeros(side_in.shape[1:], BF16)
            side_in[3 + 2 * s] = jnp.zeros(side_in.shape[1:], BF16)

        pl.when(jnp.logical_not(has(2 * s - 1)))(blank)

    def add_part(slot, h):
        lo, size = parts[h]
        part_copy(0, h, slot, lat).wait_recv()

        @pl.loop(0, cells // TILE)
        def _(n):
            more = part_in[slot, lo : lo + size, lanes(n)].astype(F32)
            sums[lo : lo + size, lanes(n)] = sums[lo : lo + size, lanes(n)] + more
            if h == 0:
                line = pad_line(h)
                count = more[line : line + 1] + more[line + 1 : line + 2] * COUNT_BASE
                number[:, lanes(n)] = number[:, lanes(n)] + count

    for h, (lo, size) in enumerate(parts):
        only(-1, lambda: add_part(lat, h))
        only(1, lambda: add_part(n_lat, h))
        for r in range(rows):
            at = slice(r * width, (r + 1) * width)
            value = number[0:1, at] * model[lo : lo + size, at] - sums[lo : lo + size, at]
            total[lo : lo + size, at] = (value * scale[lo : lo + size, :]).astype(BF16)
        for s in range(2):
            only(1 - 2 * s, lambda: row_copy(h, s).start())

    ends = (rows * EDGE, cells)
    line = iota(ends, 0)
    spot = jnp.bitwise_and(line, EDGE - 1)
    spot = (line // EDGE) * width + jnp.where(spot < STEPS, spot, spot + width - EDGE)
    ends = jnp.where(iota(ends, 1) == spot, 1.0, 0.0).astype(BF16)
    side_out[...] = lax.dot_general(
        ends, total[...], (((1,), (1,)), ((), ())), preferred_element_type=F32
    ).astype(BF16)
    for k in range(len(SIDES)):
        only(-SIDES[k][0], lambda: side_copy(k).start())

    def put_row(values, r):
        result = lax.dot_general(values, jac[...], (((0,), (0,)), ((), ())), preferred_element_type=F32)
        for j in range(chunks):
            field[j, r, EDGE : EDGE + width, :] = result[:, j * LANES : (j + 1) * LANES]

    @pl.loop(0, rows)
    def _(r):
        put_row(total[:, pl.ds(pl.multiple_of(r * width, width), width)], STEPS + r)

    for k in range(len(SIDES)):
        only(SIDES[k][0], lambda: side_copy(k).wait_recv())

    def west_east(west, span):
        values = [side_in[k, span, :].astype(F32) for k in (west, west + 1)]
        left = jnp.bitwise_and(iota(values[0].shape, 0), EDGE - 1) < STEPS
        return jnp.where(left, values[1], values[0])

    side = jnp.concatenate(
        [
            west_east(2, slice((rows - STEPS) * EDGE, rows * EDGE)),
            west_east(0, slice(0, rows * EDGE)),
            west_east(4, slice(0, band_rows)),
        ],
        axis=0,
    ).astype(BF16)
    result = jnp.dot(side, jac[...], preferred_element_type=F32)
    for j in range(chunks):
        for r in range(extent):
            piece = result[r * EDGE : (r + 1) * EDGE, j * LANES : (j + 1) * LANES]
            field[j, r, 0:EDGE, :] = piece
            field[j, r, EDGE + width :, :] = piece

    for h in range(len(parts)):
        for s in range(2):
            only(2 * s - 1, lambda: row_copy(h, s).wait_recv())

    @pl.loop(0, STEPS)
    def _(r):
        at = pl.ds(pl.multiple_of(r * width, width), width)
        put_row(total_north[:, at], r)
        put_row(total_south[:, at], STEPS + rows + r)

    stores = []
    for j in range(chunks):
        spread(j)

        @pl.loop(0, rows)
        def _(r):
            at = pl.ds(j * step_rows + r, LANES, stride=rows)
            raw[0, at, :] = raw[0, at, :] + jnp.transpose(field[j, STEPS + r, EDGE : EDGE + width, :])

        span = pl.ds(j * step_rows, min(step_rows, area - j * step_rows))
        stores.append(pltpu.make_async_copy(raw.at[0, span, :], out.at[span, :], store_sem.at[j]))
        stores[-1].start()

    for k in range(n_lat):
        for h in range(len(parts)):
            @pl.loop(1, n_lon)
            def _(i):
                block_copy(k, h, i).wait_send()
    for h in range(len(parts)):
        for k in range(n_lat - 1):
            part_sent(k, h).wait_send()
        for s in range(2):
            only(1 - 2 * s, lambda: row_copy(h, s).wait_send())
    for k in range(len(SIDES)):
        only(-SIDES[k][0], lambda: side_copy(k).wait_send())
    for a in range(2):
        for s in range(2):
            only(1 - 2 * s, lambda: band_copy(a, s).wait_send())
        for k in range(len(SIDES)):
            only(-SIDES[k][0], lambda: tile_copy(a, k).wait_send())
    for store in stores:
        store.wait()


def per_device(control, kappa, pc_obs, owner, columns, counts, jacobian, obs_weight):
    n_lat, n_lon = lax.axis_size("lat"), lax.axis_size("lon")
    fields, levels, rows, width = control.shape
    blocks, soundings, comps = pc_obs.shape
    planes = fields * levels
    cells = rows * width
    height = comps + TAIL
    chunks = -(-planes // LANES)
    extent, wide = rows + 2 * STEPS, width + 2 * EDGE
    half = -(-height // 64) * 32
    parts = ((half, height - half), (0, half))
    obs = jnp.transpose(pc_obs, (2, 0, 1))
    slots_shape = (n_lat, n_lon, CAP, height, soundings)
    packed = blocks * GROUP > 1024
    if packed:
        source = pack(obs, owner, columns, counts, n_lat * n_lon, height).reshape(slots_shape)
        extra = []
    else:
        source = obs.reshape(comps * blocks, soundings)
        extra = [
            pltpu.VMEM(slots_shape, BF16),
            pltpu.VMEM(source.shape, BF16),
            pltpu.VMEM((TAIL * blocks, soundings), BF16),
        ]
    n_parts, n_sides = len(parts), len(SIDES)
    grid = pltpu.VMEM((chunks, extent, wide, LANES), F32)
    dma = pltpu.SemaphoreType.DMA
    result = pl.pallas_call(
        functools.partial(main_kernel, n_lat, n_lon, planes, parts, packed),
        out_shape=jax.ShapeDtypeStruct((planes * rows, width), F32),
        in_specs=[pl.BlockSpec(memory_space=pl.ANY)] * 3
        + [pl.BlockSpec(memory_space=pltpu.VMEM)] * 5,
        out_specs=pl.BlockSpec(memory_space=pl.ANY),
        scratch_shapes=extra
        + [
            pltpu.VMEM(slots_shape, BF16),
            pltpu.VMEM((2, height, cells), F32),
            pltpu.VMEM((n_lat - 1, height, cells), BF16),
            pltpu.VMEM((n_lat + 1, height, cells), BF16),
            pltpu.VMEM((height, cells), F32),
            pltpu.VMEM((8, cells), F32),
            pltpu.VMEM((height, cells), F32),
            pltpu.VMEM((height, chunks * LANES), BF16),
            pltpu.VMEM((height, LANES), F32),
            grid, grid, grid,
            pltpu.VMEM((2, chunks * LANES * rows, width), F32),
            pltpu.VMEM((2, rows, chunks, width, LANES), BF16),
            pltpu.VMEM((2, 2, STEPS, chunks, width, LANES), BF16),
            pltpu.VMEM((chunks, rows, EDGE, LANES), F32),
            pltpu.VMEM((2, chunks, rows * EDGE, LANES), BF16),
            pltpu.VMEM((2, n_sides, chunks, rows * EDGE, LANES), BF16),
            pltpu.VMEM((height, cells), BF16),
            pltpu.VMEM((height, STEPS * width), BF16),
            pltpu.VMEM((height, STEPS * width), BF16),
            pltpu.VMEM((rows * EDGE, height), BF16),
            pltpu.VMEM((n_sides, rows * EDGE, height), BF16),
            dma((3,)), dma((n_lat, n_parts)),
            dma((n_lat, n_parts, n_lon)), dma((n_lat, n_parts, n_lon)),
            dma((n_lat, n_parts)), dma((n_lat + 1, n_parts)),
            dma((2, 2)), dma((2, 2)), dma((2, n_sides)), dma((2, n_sides)),
            dma((n_parts, 2)), dma((n_parts, 2)), dma((n_sides,)), dma((n_sides,)),
            dma((chunks,)),
        ],
        compiler_params=pltpu.CompilerParams(
            vmem_limit_bytes=62 * 2**20, has_side_effects=True, collective_id=0
        ),
    )(
        source, control.reshape(planes * rows, width), kappa.reshape(planes * rows, width),
        jnp.transpose(jacobian), obs_weight[None, :], owner.reshape(1, blocks), counts[None, :], columns,
    )
    return result.reshape(control.shape)


def solution(mesh):
    placed = (
        P(None, None, "lat", "lon"),
        P(None, None, "lat", "lon"),
        P(("lat", "lon"), None, None),
        P(("lat", "lon"), None),
        P(("lat", "lon"), None),
        P(("lat", "lon")),
        P(),
        P(),
    )
    return jax.shard_map(
        per_device,
        mesh=mesh,
        in_specs=placed,
        out_specs=P(None, None, "lat", "lon"),
        check_vma=False,
    )
```

```python
import functools

import jax
import jax.numpy as jnp
from jax import lax
from jax.experimental import pallas as pl
from jax.experimental.pallas import tpu as pltpu
from jax.sharding import PartitionSpec as P

CAP = 2
STEPS = 4
LANES = 128
GROUP = 16
EDGE = 8
TAIL = 4
COUNT_BASE = 64
TILE = 256
MESH = pl.DeviceIdType.MESH
F32 = jnp.float32
BF16 = jnp.bfloat16
SIDES = ((0, -1), (0, 1), (-1, -1), (-1, 1), (1, -1), (1, 1))


def iota(shape, dim):
    return lax.broadcasted_iota(jnp.int32, shape, dim)


def to_column(row, size):
    shape = (size, row.shape[1])
    return jnp.sum(jnp.where(iota(shape, 0) == iota(shape, 1), row, 0.0), axis=1, keepdims=True)


def digits(columns, counts):
    low = jnp.bitwise_and(columns, 31)
    valid = iota(columns.shape, 1).astype(F32) < counts
    high = jnp.where(valid, jnp.right_shift(columns - low, 5) + 1, 0)
    zero = jnp.zeros(columns.shape, F32)
    return [zero + 1.0, high.astype(F32), low.astype(F32), zero]


def pack_kernel(group, owner_ref, obs_ref, columns_ref, counts_ref, out_ref, wide, source):
    blocks = columns_ref.shape[0]
    comps = obs_ref.shape[0]
    height = out_ref.shape[1]
    slots = source.shape[0]

    @pl.when(pl.program_id(0) == 0)
    def _():
        @pl.loop(0, slots)
        def _(t):
            source[t] = -1

        @pl.loop(0, blocks)
        def _(b):
            first = owner_ref[b] * CAP
            source[jnp.where(source[first] < 0, first, first + 1)] = b

        @pl.loop(0, comps, unroll=4)
        def _(c):
            wide[pl.ds(pl.multiple_of(c * blocks, blocks), blocks), :] = obs_ref[c].astype(F32)

        for k, row in enumerate(digits(columns_ref[...], to_column(counts_ref[...].astype(F32), blocks))):
            wide[(comps + k) * blocks : (comps + k + 1) * blocks, :] = row

    for g in range(group):
        block = source[pl.program_id(0) * group + g]
        rows = wide[pl.ds(jnp.maximum(block, 0), height, stride=blocks), :]
        out_ref[g] = jnp.where(block < 0, 0.0, rows).astype(BF16)


def pack(obs, owner, columns, counts, peers, height):
    comps, blocks, soundings = obs.shape
    slots = peers * CAP
    group = 8
    return pl.pallas_call(
        functools.partial(pack_kernel, group),
        out_shape=jax.ShapeDtypeStruct((slots, height, soundings), BF16),
        grid_spec=pltpu.PrefetchScalarGridSpec(
            num_scalar_prefetch=1,
            grid=(slots // group,),
            in_specs=[
                pl.BlockSpec((comps, blocks, soundings), lambda i, s: (0, 0, 0)),
                pl.BlockSpec((blocks, soundings), lambda i, s: (0, 0)),
                pl.BlockSpec((1, blocks), lambda i, s: (0, 0)),
            ],
            out_specs=pl.BlockSpec((group, height, soundings), lambda i, s: (i, 0, 0)),
            scratch_shapes=[
                pltpu.VMEM((height * blocks, soundings), F32),
                pltpu.SMEM((slots,), jnp.int32),
            ],
        ),
        compiler_params=pltpu.CompilerParams(vmem_limit_bytes=56 * 2**20),
    )(owner[:, 0], obs, columns, counts[None, :])


def main_kernel(n_lat, n_lon, planes, parts, packed, *refs):
    source, control, kappa, *small_in, out = refs[:9]
    small, refs = refs[9:14], refs[14:]
    jac_in, weight_in, owner, counts, columns = small
    sent, obs, codes = (source, None, None) if packed else refs[:3]
    (
        recv, ring, part_out, part_in, sums, number, model, jac, scale,
        field, coef, east, raw, band_out, band_in, band_f, tile_f, tile_out, tile_in,
        total, total_north, total_south, side_out, side_in,
        load_sem, own_sem, blk_send, blk_recv, part_send, part_recv,
        band_send, band_recv, tile_send, tile_recv, row_send, row_recv, side_send, side_recv, store_sem,
    ) = refs if packed else refs[3:]
    lat, lon = lax.axis_index("lat"), lax.axis_index("lon")
    height, cells = sums.shape
    comps = jac_in.shape[0]
    chunks, extent, wide, _ = field.shape
    rows = extent - 2 * STEPS
    width = wide - 2 * EDGE
    area = planes * rows
    step_rows = LANES * rows
    slots = n_lon * CAP
    band_rows = STEPS * EDGE

    def plane_of(k):
        mirrored = lat >= n_lat - n_lat // 2
        z = jnp.where(mirrored, n_lat - 1 - lat, lat)
        o = jnp.where(k < n_lat - 1 - z, n_lat - 1 - k, k - (n_lat - 1 - z))
        return jnp.where(mirrored, n_lat - 1 - o, o)

    def remote(src, dst, send, recv_, to):
        return pltpu.make_async_remote_copy(
            src_ref=src, dst_ref=dst, send_sem=send, recv_sem=recv_, device_id=to, device_id_type=MESH
        )

    def around(step):
        return lax.rem(lon + step + n_lon, n_lon)

    def has(step):
        return (lat + step >= 0) & (lat + step < n_lat)

    def only(step, act):
        if step == 0:
            act()
        else:
            pl.when(has(step))(act)

    def slot_of(k):
        return plane_of(k) if packed else k

    def block_copy(k, h, i):
        lo, size = parts[h]
        return remote(
            sent.at[slot_of(k), around(i), :, pl.ds(lo, size), :], recv.at[k, i, :, pl.ds(lo, size), :],
            blk_send.at[k, h, i], blk_recv.at[k, h, i], (lat, around(i)),
        )

    def own_copy(k, h):
        lo, size = parts[h]
        return pltpu.make_async_copy(
            sent.at[slot_of(k), lon, :, pl.ds(lo, size), :],
            recv.at[k, 0, :, pl.ds(lo, size), :], own_sem.at[k, h],
        )

    def part_copy(k, h, slot, to):
        lo, size = parts[h]
        return remote(
            part_out.at[k, pl.ds(lo, size), :], part_in.at[slot, pl.ds(lo, size), :],
            part_send.at[k, h], part_recv.at[slot, h], (to, lon),
        )

    def part_sent(k, h):
        o = plane_of(k)
        north = o < lat
        slot = jnp.where(north & (o == lat - 1), n_lat, o)
        return part_copy(k, h, slot, jnp.where(north, lat - 1, lat + 1))

    def band_copy(a, s):
        return remote(
            band_out.at[a, 1 - s], band_in.at[a, s],
            band_send.at[a, s], band_recv.at[a, s], (lat + (1 - 2 * s), lon),
        )

    def peer(k):
        return (lat - SIDES[k][0], around(-SIDES[k][1]))

    def side_span(k):
        step = SIDES[k][0]
        if step == 0:
            return pl.ds(0, rows * EDGE)
        return pl.ds((rows * EDGE - band_rows) if step < 0 else 0, band_rows)

    def tile_copy(a, k):
        span = side_span(k)
        return remote(
            tile_out.at[a, :, span, :], tile_in.at[a, k, :, span, :],
            tile_send.at[a, k], tile_recv.at[a, k], peer(k),
        )

    def row_copy(h, s):
        lo, size = parts[h]
        span = STEPS * width
        return remote(
            total.at[pl.ds(lo, size), pl.ds((1 - s) * (rows * width - span), span)],
            (total_north if s == 0 else total_south).at[pl.ds(lo, size), :],
            row_send.at[h, s], row_recv.at[h, s], (lat + (1 - 2 * s), lon),
        )

    def side_copy(k):
        span = side_span(k)
        return remote(
            side_out.at[span, :], side_in.at[k, span, :], side_send.at[k], side_recv.at[k], peer(k)
        )

    loads = [
        pltpu.make_async_copy(ref, raw.at[a, pl.ds(0, area), :], load_sem.at[a])
        for a, ref in enumerate((control, kappa))
    ]
    small_loads = [
        pltpu.make_async_copy(ref, to, load_sem.at[3 + n]) for n, (ref, to) in enumerate(zip(small_in, small))
    ]
    loads[1].start()
    loads[0].start()
    for load in small_loads[1:]:
        load.start()
    if not packed:
        obs_load = pltpu.make_async_copy(source, obs, load_sem.at[2])
        obs_load.start()
    small_loads[0].start()

    barrier = pltpu.get_barrier_semaphore()

    @pl.loop(1, n_lon)
    def _(i):
        pl.semaphore_signal(barrier, inc=1, device_id=(lat, around(i)), device_id_type=MESH)

    for step in (-1, 1):
        def greet():
            for side in (-1, 0, 1):
                pl.semaphore_signal(
                    barrier, inc=1, device_id=(lat + step, around(side)), device_id_type=MESH
                )

        only(step, greet)

    sub = iota((EDGE, LANES), 0)
    for a in (1, 0):
        loads[a].wait()
        if chunks * step_rows > area:
            raw[a, area:, :] = jnp.zeros((chunks * step_rows - area, width), F32)
        pairs = raw[a, 0:area, :].reshape(planes // 2, 2, rows, width)
        even, odd = pairs[:, 0], pairs[:, 1]
        upper = iota(even.shape, 1) < STEPS
        band_out[a, 0] = jnp.where(upper, even, pltpu.roll(odd, STEPS, 1)).reshape(area // 2, width).astype(BF16)
        band_out[a, 1] = jnp.where(upper, pltpu.roll(even, STEPS, 1), odd).reshape(area // 2, width).astype(BF16)
        if a == 1:
            pl.semaphore_wait(
                barrier, n_lon - 1 + 3 * (has(-1).astype(jnp.int32) + has(1).astype(jnp.int32))
            )
        for s in range(2):
            only(1 - 2 * s, lambda: band_copy(a, s).start())

    for load in small_loads[1:]:
        load.wait()

    if not packed:
        blocks = columns.shape[0]
        names = owner[...].astype(F32)
        square = (blocks, blocks)
        before = (to_column(names, blocks) == names) & (iota(square, 0) < iota(square, 1))
        place = names * CAP + jnp.sum(jnp.where(before, 1.0, 0.0), axis=0, keepdims=True)
        lined = (blocks, GROUP * blocks)
        comb = jnp.where(lax.rem(iota(lined, 1), blocks) == iota(lined, 0), 1.0, 0.0).astype(BF16)
        place = jnp.broadcast_to(place, (16, blocks)).astype(BF16)
        place = jnp.dot(place, comb, preferred_element_type=F32)[0:1].astype(jnp.int32)
        code = digits(columns[...], to_column(counts[...].astype(F32), blocks))
        codes[...] = jnp.concatenate(code, axis=0).astype(BF16)

    def pack_round(k, h):
        shape = (slots * GROUP, GROUP * blocks)
        at = plane_of(k) * slots + jnp.right_shift(iota(shape, 0), 4)
        hit = (place == at) & (jnp.bitwise_and(iota(shape, 0), GROUP - 1) == iota(shape, 1) // blocks)
        pick = jnp.where(hit, 1.0, 0.0).astype(BF16)
        lo, size = parts[h]
        span = GROUP * blocks

        def put(first, values):
            for t in range(slots):
                part = values[t * GROUP : (t + 1) * GROUP].astype(BF16)
                sent[k, t // CAP, t % CAP, pl.ds(first, GROUP), :] = part

        pairs = (min(lo + size, height - GROUP) - lo) // (2 * GROUP)

        @pl.loop(0, pairs)
        def _(p):
            first = pl.multiple_of(lo + p * 2 * GROUP, GROUP)
            start = pl.multiple_of(first * blocks, span)
            both = jnp.concatenate([obs[pl.ds(start, span), :], obs[pl.ds(start + span, span), :]], axis=1)
            values = jnp.dot(pick, both, preferred_element_type=F32)
            put(first, values[:, :LANES])
            put(pl.multiple_of(first + GROUP, GROUP), values[:, LANES:])

        if lo + size == height:
            last = jnp.concatenate([obs[(height - GROUP) * blocks :, :], codes[...]], axis=0)
            put(height - GROUP, jnp.dot(pick, last, preferred_element_type=F32))

    def send_round(k, h):
        if not packed:
            pack_round(k, h)

        @pl.loop(1, n_lon)
        def _(i):
            block_copy(k, h, i).start()

        own_copy(k, h).start()

    if not packed:
        obs_load.wait()
    for h in range(len(parts)):
        send_round(0, h)

    for a, grid in ((1, coef), (0, field)):
        @pl.loop(0, rows)
        def _(r):
            for j in range(chunks):
                turned = jnp.transpose(raw[a, pl.ds(j * step_rows + r, LANES, stride=rows), :])
                grid[j, STEPS + r, EDGE : EDGE + width, :] = turned
                tile_f[j, r] = jnp.where(sub < STEPS, turned[:EDGE], turned[width - EDGE :])

        tile_out[a] = tile_f[...].reshape(chunks, rows * EDGE, LANES).astype(BF16)
        for k in range(len(SIDES)):
            only(-SIDES[k][0], lambda: tile_copy(a, k).start())

    for k in range(1, n_lat):
        for h in range(len(parts)):
            send_round(k, h)

    small_loads[0].wait()
    matrix = jac_in[...].astype(F32)
    matrix = jnp.concatenate([matrix, jnp.zeros((height - comps, planes), F32)], axis=0)
    if chunks * LANES > planes:
        matrix = jnp.concatenate([matrix, jnp.zeros((height, chunks * LANES - planes), F32)], axis=1)
    jac[...] = matrix.astype(BF16)
    scale[...] = jnp.broadcast_to(to_column(weight_in[...].reshape(1, comps), height), scale.shape)

    def pad_line(h):
        return comps - parts[h][0]

    def lanes(n):
        return pl.ds(pl.multiple_of(n * TILE, TILE), TILE)

    def reduce(k, h):
        lo, size = parts[h]

        @pl.loop(1, n_lon)
        def _(i):
            block_copy(k, h, i).wait_recv()

        own_copy(k, h).wait()
        base = height - GROUP
        first = comps - base
        heads = [recv[k, i, c, base:height, :].astype(F32) for i in range(n_lon) for c in range(CAP)]
        code = jnp.concatenate(
            [(x[first + 1 : first + 2] - 1.0) * 32.0 + x[first + 2 : first + 3] for x in heads], axis=1
        ).astype(jnp.int32)

        @pl.loop(0, cells // TILE)
        def _(n):
            values = jnp.concatenate(
                [recv[k, i, c, lo : lo + size, :] for i in range(n_lon) for c in range(CAP)], axis=1
            )
            hot = jnp.where(iota((TILE, code.shape[1]), 0) == code - n * TILE, 1.0, 0.0).astype(BF16)
            part = lax.dot_general(values, hot, (((1,), (1,)), ((), ())), preferred_element_type=F32)
            if k == n_lat - 1:
                sums[lo : lo + size, lanes(n)] = part
                if h == 0:
                    line = pad_line(h)
                    number[:, lanes(n)] = jnp.broadcast_to(part[line : line + 1], (8, TILE))
            else:
                ring[k % 2, lo : lo + size, lanes(n)] = part

        if k < n_lat - 1:
            pl.when(jnp.logical_not(has(-1) & has(1)))(lambda: emit(k, h, False))

    def emit(k, h, joined):
        lo, size = parts[h]
        o = plane_of(k)
        if joined:
            part_copy(k, h, o, lat).wait_recv()

        @pl.loop(0, cells // TILE)
        def _(n):
            value = ring[k % 2, lo : lo + size, lanes(n)]
            if h == 0:
                line = pad_line(h)
                count = value[line : line + 1]
            if joined:
                more = part_in[o, lo : lo + size, lanes(n)].astype(F32)
                value = value + more
                if h == 0:
                    count = count + more[line : line + 1] + more[line + 1 : line + 2] * COUNT_BASE
            if h == 0:
                high = jnp.floor(count * (1.0 / COUNT_BASE))
                at = iota(value.shape, 0)
                value = jnp.where(at == line, count - high * COUNT_BASE, jnp.where(at == line + 1, high, value))
            part_out[k, lo : lo + size, lanes(n)] = value.astype(BF16)

        part_sent(k, h).start()

    def join(k):
        for h in range(len(parts)):
            pl.when(has(-1) & has(1))(lambda: emit(k, h, True))

    def fill_edges(a, grid):
        def band(s):
            first = (rows + STEPS) * s

            def arrived():
                band_copy(a, s).wait_recv()
                band_f[0 : area // 2, :] = band_in[a, s].astype(F32)

                @pl.loop(0, STEPS)
                def _(r):
                    for j in range(chunks):
                        piece = band_f[pl.ds(j * STEPS * LANES + r, LANES, stride=STEPS), :]
                        grid[j, first + r, EDGE : EDGE + width, :] = jnp.transpose(piece)

            def closed():
                for r in range(STEPS):
                    for j in range(chunks):
                        grid[j, first + r] = jnp.zeros((wide, LANES), F32)

            pl.when(has(2 * s - 1))(arrived)
            pl.when(jnp.logical_not(has(2 * s - 1)))(closed)

        for s in range(2):
            band(s)

        def sides(west, count, place, source_row):
            tile_copy(a, west).wait_recv()
            tile_copy(a, west + 1).wait_recv()
            span = slice(source_row * EDGE, (source_row + count) * EDGE)
            shape = (chunks, count, EDGE, LANES)
            both = [tile_in[a, k, :, span, :].astype(F32).reshape(shape) for k in (west, west + 1)]
            for j in range(chunks):
                for r in range(count):
                    tile = jnp.where(sub < STEPS, both[1][j, r], both[0][j, r])
                    grid[j, place + r, 0:EDGE, :] = tile
                    grid[j, place + r, EDGE + width :, :] = tile

        sides(0, rows, STEPS, 0)
        only(-1, lambda: sides(2, STEPS, 0, rows - STEPS))
        only(1, lambda: sides(4, STEPS, rows + STEPS, 0))

    def spread(j):
        for step in range(STEPS):
            first, last = step + 1, extent - 1 - step
            here = field[j, first]
            above = coef[j, first - 1] * (here - field[j, first - 1])

            def line(r, carry):
                here, above = carry
                below = field[j, r + 1]
                down = coef[j, r] * (below - here)
                along = east[j, r] * (pltpu.roll(here, wide - 1, 0) - here)
                field[j, r] = here + (down - above) + (along - pltpu.roll(along, 1, 0))
                return below, down

            lax.fori_loop(first, last, line, (here, above), unroll=2)

    def make_state():
        if chunks * LANES > planes:
            band_f[area // 2 :, :] = jnp.zeros((chunks * LANES * STEPS - area // 2, width), F32)
        fill_edges(1, coef)

        @pl.loop(0, chunks)
        def _(j):
            @pl.loop(0, extent - 1)
            def _(r):
                here = coef[j, r]
                east[j, r] = here * pltpu.roll(here, wide - 1, 0)
                coef[j, r] = here * coef[j, r + 1]

        fill_edges(0, field)
        pl.loop(0, chunks)(spread)

        @pl.loop(0, rows)
        def _(r):
            state = jnp.concatenate(
                [field[j, STEPS + r, EDGE : EDGE + width, :].astype(BF16) for j in range(chunks)], axis=1
            )
            model[:, pl.ds(pl.multiple_of(r * width, width), width)] = lax.dot_general(
                jac[...], state, (((1,), (1,)), ((), ())), preferred_element_type=F32
            )

    for k in range(n_lat - 1):
        for h in range(len(parts)):
            reduce(k, h)
        if k > 0:
            join(k - 1)
        if k == min(1, n_lat - 2):
            make_state()
    join(n_lat - 2)
    for h in range(len(parts)):
        reduce(n_lat - 1, h)

    for s, ref in enumerate((total_north, total_south)):
        def blank():
            ref[...] = jnp.zeros(ref.shape, BF16)
            side_in[2 + 2 * s] = jnp.zeros(side_in.shape[1:], BF16)
            side_in[3 + 2 * s] = jnp.zeros(side_in.shape[1:], BF16)

        pl.when(jnp.logical_not(has(2 * s - 1)))(blank)

    def add_part(slot, h):
        lo, size = parts[h]
        part_copy(0, h, slot, lat).wait_recv()

        @pl.loop(0, cells // TILE)
        def _(n):
            more = part_in[slot, lo : lo + size, lanes(n)].astype(F32)
            sums[lo : lo + size, lanes(n)] = sums[lo : lo + size, lanes(n)] + more
            if h == 0:
                line = pad_line(h)
                count = more[line : line + 1] + more[line + 1 : line + 2] * COUNT_BASE
                number[:, lanes(n)] = number[:, lanes(n)] + count

    for h, (lo, size) in enumerate(parts):
        only(-1, lambda: add_part(lat, h))
        only(1, lambda: add_part(n_lat, h))
        for r in range(rows):
            at = slice(r * width, (r + 1) * width)
            value = number[0:1, at] * model[lo : lo + size, at] - sums[lo : lo + size, at]
            total[lo : lo + size, at] = (value * scale[lo : lo + size, :]).astype(BF16)
        for s in range(2):
            only(1 - 2 * s, lambda: row_copy(h, s).start())

    ends = (rows * EDGE, cells)
    line = iota(ends, 0)
    spot = jnp.bitwise_and(line, EDGE - 1)
    spot = (line // EDGE) * width + jnp.where(spot < STEPS, spot, spot + width - EDGE)
    ends = jnp.where(iota(ends, 1) == spot, 1.0, 0.0).astype(BF16)
    side_out[...] = lax.dot_general(
        ends, total[...], (((1,), (1,)), ((), ())), preferred_element_type=F32
    ).astype(BF16)
    for k in range(len(SIDES)):
        only(-SIDES[k][0], lambda: side_copy(k).start())

    def put_row(values, r):
        result = lax.dot_general(values, jac[...], (((0,), (0,)), ((), ())), preferred_element_type=F32)
        for j in range(chunks):
            field[j, r, EDGE : EDGE + width, :] = result[:, j * LANES : (j + 1) * LANES]

    @pl.loop(0, rows)
    def _(r):
        put_row(total[:, pl.ds(pl.multiple_of(r * width, width), width)], STEPS + r)

    for k in range(len(SIDES)):
        only(SIDES[k][0], lambda: side_copy(k).wait_recv())

    def west_east(west, span):
        values = [side_in[k, span, :].astype(F32) for k in (west, west + 1)]
        left = jnp.bitwise_and(iota(values[0].shape, 0), EDGE - 1) < STEPS
        return jnp.where(left, values[1], values[0])

    side = jnp.concatenate(
        [
            west_east(2, slice((rows - STEPS) * EDGE, rows * EDGE)),
            west_east(0, slice(0, rows * EDGE)),
            west_east(4, slice(0, band_rows)),
        ],
        axis=0,
    ).astype(BF16)
    result = jnp.dot(side, jac[...], preferred_element_type=F32)
    for j in range(chunks):
        for r in range(extent):
            piece = result[r * EDGE : (r + 1) * EDGE, j * LANES : (j + 1) * LANES]
            field[j, r, 0:EDGE, :] = piece
            field[j, r, EDGE + width :, :] = piece

    for h in range(len(parts)):
        for s in range(2):
            only(2 * s - 1, lambda: row_copy(h, s).wait_recv())

    @pl.loop(0, STEPS)
    def _(r):
        at = pl.ds(pl.multiple_of(r * width, width), width)
        put_row(total_north[:, at], r)
        put_row(total_south[:, at], STEPS + rows + r)

    stores = []
    for j in range(chunks):
        spread(j)

        @pl.loop(0, rows)
        def _(r):
            at = pl.ds(j * step_rows + r, LANES, stride=rows)
            raw[0, at, :] = raw[0, at, :] + jnp.transpose(field[j, STEPS + r, EDGE : EDGE + width, :])

        span = pl.ds(j * step_rows, min(step_rows, area - j * step_rows))
        stores.append(pltpu.make_async_copy(raw.at[0, span, :], out.at[span, :], store_sem.at[j]))
        stores[-1].start()

    for k in range(n_lat):
        for h in range(len(parts)):
            @pl.loop(1, n_lon)
            def _(i):
                block_copy(k, h, i).wait_send()
    for h in range(len(parts)):
        for k in range(n_lat - 1):
            part_sent(k, h).wait_send()
        for s in range(2):
            only(1 - 2 * s, lambda: row_copy(h, s).wait_send())
    for k in range(len(SIDES)):
        only(-SIDES[k][0], lambda: side_copy(k).wait_send())
    for a in range(2):
        for s in range(2):
            only(1 - 2 * s, lambda: band_copy(a, s).wait_send())
        for k in range(len(SIDES)):
            only(-SIDES[k][0], lambda: tile_copy(a, k).wait_send())
    for store in stores:
        store.wait()


def per_device(control, kappa, pc_obs, owner, columns, counts, jacobian, obs_weight):
    n_lat, n_lon = lax.axis_size("lat"), lax.axis_size("lon")
    fields, levels, rows, width = control.shape
    blocks, soundings, comps = pc_obs.shape
    planes = fields * levels
    cells = rows * width
    height = comps + TAIL
    chunks = -(-planes // LANES)
    extent, wide = rows + 2 * STEPS, width + 2 * EDGE
    half = -(-height // 64) * 32
    parts = ((half, height - half), (0, half))
    obs = jnp.transpose(pc_obs, (2, 0, 1))
    slots_shape = (n_lat, n_lon, CAP, height, soundings)
    packed = blocks * GROUP > 1024
    if packed:
        source = pack(obs, owner, columns, counts, n_lat * n_lon, height).reshape(slots_shape)
        extra = []
    else:
        source = obs.reshape(comps * blocks, soundings)
        extra = [
            pltpu.VMEM(slots_shape, BF16),
            pltpu.VMEM(source.shape, BF16),
            pltpu.VMEM((TAIL * blocks, soundings), BF16),
        ]
    small = (jnp.transpose(jacobian), obs_weight, owner.reshape(1, blocks), counts[None, :], columns)
    n_parts, n_sides = len(parts), len(SIDES)
    grid = pltpu.VMEM((chunks, extent, wide, LANES), F32)
    dma = pltpu.SemaphoreType.DMA
    result = pl.pallas_call(
        functools.partial(main_kernel, n_lat, n_lon, planes, parts, packed),
        out_shape=jax.ShapeDtypeStruct((planes * rows, width), F32),
        in_specs=[pl.BlockSpec(memory_space=pl.ANY)] * (3 + len(small)),
        out_specs=pl.BlockSpec(memory_space=pl.ANY),
        scratch_shapes=[pltpu.VMEM(x.shape, x.dtype) for x in small]
        + extra
        + [
            pltpu.VMEM(slots_shape, BF16),
            pltpu.VMEM((2, height, cells), F32),
            pltpu.VMEM((n_lat - 1, height, cells), BF16),
            pltpu.VMEM((n_lat + 1, height, cells), BF16),
            pltpu.VMEM((height, cells), F32),
            pltpu.VMEM((8, cells), F32),
            pltpu.VMEM((height, cells), F32),
            pltpu.VMEM((height, chunks * LANES), BF16),
            pltpu.VMEM((height, LANES), F32),
            grid, grid, grid,
            pltpu.VMEM((2, chunks * LANES * rows, width), F32),
            pltpu.VMEM((2, 2, planes * STEPS, width), BF16),
            pltpu.VMEM((2, 2, planes * STEPS, width), BF16),
            pltpu.VMEM((chunks * LANES * STEPS, width), F32),
            pltpu.VMEM((chunks, rows, EDGE, LANES), F32),
            pltpu.VMEM((2, chunks, rows * EDGE, LANES), BF16),
            pltpu.VMEM((2, n_sides, chunks, rows * EDGE, LANES), BF16),
            pltpu.VMEM((height, cells), BF16),
            pltpu.VMEM((height, STEPS * width), BF16),
            pltpu.VMEM((height, STEPS * width), BF16),
            pltpu.VMEM((rows * EDGE, height), BF16),
            pltpu.VMEM((n_sides, rows * EDGE, height), BF16),
            dma((3 + len(small),)), dma((n_lat, n_parts)),
            dma((n_lat, n_parts, n_lon)), dma((n_lat, n_parts, n_lon)),
            dma((n_lat, n_parts)), dma((n_lat + 1, n_parts)),
            dma((2, 2)), dma((2, 2)), dma((2, n_sides)), dma((2, n_sides)),
            dma((n_parts, 2)), dma((n_parts, 2)), dma((n_sides,)), dma((n_sides,)),
            dma((chunks,)),
        ],
        compiler_params=pltpu.CompilerParams(
            vmem_limit_bytes=62 * 2**20, has_side_effects=True, collective_id=0
        ),
    )(
        source, control.reshape(planes * rows, width), kappa.reshape(planes * rows, width),
        *small,
    )
    return result.reshape(control.shape)


def solution(mesh):
    placed = (
        P(None, None, "lat", "lon"),
        P(None, None, "lat", "lon"),
        P(("lat", "lon"), None, None),
        P(("lat", "lon"), None),
        P(("lat", "lon"), None),
        P(("lat", "lon")),
        P(),
        P(),
    )
    return jax.shard_map(
        per_device,
        mesh=mesh,
        in_specs=placed,
        out_specs=P(None, None, "lat", "lon"),
        check_vma=False,
    )
```

```python
import functools

import jax
import jax.numpy as jnp
from jax import lax
from jax.experimental import pallas as pl
from jax.experimental.pallas import tpu as pltpu
from jax.sharding import PartitionSpec as P

CAP = 2
STEPS = 4
LANES = 128
GROUP = 16
EDGE = 8
TAIL = 4
COUNT_BASE = 64
TILE = 256
MESH = pl.DeviceIdType.MESH
F32 = jnp.float32
BF16 = jnp.bfloat16
SIDES = ((0, -1), (0, 1), (-1, -1), (-1, 1), (1, -1), (1, 1))


def iota(shape, dim):
    return lax.broadcasted_iota(jnp.int32, shape, dim)


def to_column(row, size):
    shape = (size, row.shape[1])
    return jnp.sum(jnp.where(iota(shape, 0) == iota(shape, 1), row, 0.0), axis=1, keepdims=True)


def digits(columns, counts):
    low = jnp.bitwise_and(columns, 31)
    valid = iota(columns.shape, 1).astype(F32) < counts
    high = jnp.where(valid, jnp.right_shift(columns - low, 5) + 1, 0)
    zero = jnp.zeros(columns.shape, F32)
    return [zero + 1.0, high.astype(F32), low.astype(F32), zero]


def pack_kernel(group, owner_ref, obs_ref, columns_ref, counts_ref, out_ref, wide, source):
    blocks = columns_ref.shape[0]
    comps = obs_ref.shape[0]
    height = out_ref.shape[1]
    slots = source.shape[0]

    @pl.when(pl.program_id(0) == 0)
    def _():
        @pl.loop(0, slots)
        def _(t):
            source[t] = -1

        @pl.loop(0, blocks)
        def _(b):
            first = owner_ref[b] * CAP
            source[jnp.where(source[first] < 0, first, first + 1)] = b

        @pl.loop(0, comps, unroll=4)
        def _(c):
            wide[pl.ds(pl.multiple_of(c * blocks, blocks), blocks), :] = obs_ref[c].astype(F32)

        for k, row in enumerate(digits(columns_ref[...], to_column(counts_ref[...].astype(F32), blocks))):
            wide[(comps + k) * blocks : (comps + k + 1) * blocks, :] = row

    for g in range(group):
        block = source[pl.program_id(0) * group + g]
        rows = wide[pl.ds(jnp.maximum(block, 0), height, stride=blocks), :]
        out_ref[g] = jnp.where(block < 0, 0.0, rows).astype(BF16)


def pack(obs, owner, columns, counts, peers, height):
    comps, blocks, soundings = obs.shape
    slots = peers * CAP
    group = 8
    return pl.pallas_call(
        functools.partial(pack_kernel, group),
        out_shape=jax.ShapeDtypeStruct((slots, height, soundings), BF16),
        grid_spec=pltpu.PrefetchScalarGridSpec(
            num_scalar_prefetch=1,
            grid=(slots // group,),
            in_specs=[
                pl.BlockSpec((comps, blocks, soundings), lambda i, s: (0, 0, 0)),
                pl.BlockSpec((blocks, soundings), lambda i, s: (0, 0)),
                pl.BlockSpec((1, blocks), lambda i, s: (0, 0)),
            ],
            out_specs=pl.BlockSpec((group, height, soundings), lambda i, s: (i, 0, 0)),
            scratch_shapes=[
                pltpu.VMEM((height * blocks, soundings), F32),
                pltpu.SMEM((slots,), jnp.int32),
            ],
        ),
        compiler_params=pltpu.CompilerParams(vmem_limit_bytes=56 * 2**20),
    )(owner[:, 0], obs, columns, counts[None, :])


def main_kernel(n_lat, n_lon, planes, parts, packed, *refs):
    source, control, kappa, *small_in, out = refs[:9]
    small, refs = refs[9:14], refs[14:]
    jac_in, weight_in, owner, counts, columns = small
    sent, obs, codes = (source, None, None) if packed else refs[:3]
    (
        recv, ring, part_out, part_in, sums, number, model, jac, scale,
        field, coef, east, raw, band_out, band_in, band_f, tile_f, tile_out, tile_in,
        total, total_north, total_south, side_out, side_in,
        load_sem, own_sem, blk_send, blk_recv, part_send, part_recv,
        band_send, band_recv, tile_send, tile_recv, row_send, row_recv, side_send, side_recv, store_sem,
    ) = refs if packed else refs[3:]
    lat, lon = lax.axis_index("lat"), lax.axis_index("lon")
    height, cells = sums.shape
    comps = jac_in.shape[0]
    chunks, extent, wide, _ = field.shape
    rows = extent - 2 * STEPS
    width = wide - 2 * EDGE
    area = planes * rows
    step_rows = LANES * rows
    slots = n_lon * CAP

    def plane_of(k):
        mirrored = lat >= n_lat - n_lat // 2
        z = jnp.where(mirrored, n_lat - 1 - lat, lat)
        o = jnp.where(k < n_lat - 1 - z, n_lat - 1 - k, k - (n_lat - 1 - z))
        return jnp.where(mirrored, n_lat - 1 - o, o)

    def remote(src, dst, send, recv_, to):
        return pltpu.make_async_remote_copy(
            src_ref=src, dst_ref=dst, send_sem=send, recv_sem=recv_, device_id=to, device_id_type=MESH
        )

    def around(step):
        return lax.rem(lon + step + n_lon, n_lon)

    def has(step):
        return (lat + step >= 0) & (lat + step < n_lat)

    def only(step, act):
        if step == 0:
            act()
        else:
            pl.when(has(step))(act)

    def slot_of(k):
        return plane_of(k) if packed else k

    def block_copy(k, h, i):
        lo, size = parts[h]
        return remote(
            sent.at[slot_of(k), around(i), :, pl.ds(lo, size), :], recv.at[k, i, :, pl.ds(lo, size), :],
            blk_send.at[k, h, i], blk_recv.at[k, h, i], (lat, around(i)),
        )

    def own_copy(k, h):
        lo, size = parts[h]
        return pltpu.make_async_copy(
            sent.at[slot_of(k), lon, :, pl.ds(lo, size), :],
            recv.at[k, 0, :, pl.ds(lo, size), :], own_sem.at[k, h],
        )

    def part_copy(k, h, slot, to):
        lo, size = parts[h]
        return remote(
            part_out.at[k, pl.ds(lo, size), :], part_in.at[slot, pl.ds(lo, size), :],
            part_send.at[k, h], part_recv.at[slot, h], (to, lon),
        )

    def part_sent(k, h):
        o = plane_of(k)
        north = o < lat
        slot = jnp.where(north & (o == lat - 1), n_lat, o)
        return part_copy(k, h, slot, jnp.where(north, lat - 1, lat + 1))

    def band_copy(a, s):
        return remote(
            band_out.at[a, 1 - s], band_in.at[a, s],
            band_send.at[a, s], band_recv.at[a, s], (lat + (1 - 2 * s), lon),
        )

    def peer(k):
        return (lat - SIDES[k][0], around(-SIDES[k][1]))

    def tile_copy(a, k):
        return remote(tile_out.at[a, 1 - k], tile_in.at[a, k], tile_send.at[a, k], tile_recv.at[a, k], peer(k))

    def row_copy(h, s):
        lo, size = parts[h]
        span = STEPS * width
        return remote(
            total.at[pl.ds(lo, size), pl.ds((1 - s) * (rows * width - span), span)],
            (total_north if s == 0 else total_south).at[pl.ds(lo, size), :],
            row_send.at[h, s], row_recv.at[h, s], (lat + (1 - 2 * s), lon),
        )

    def side_copy(k):
        step, side = SIDES[k]
        span = pl.ds((rows - STEPS) * STEPS if step < 0 else 0, (STEPS if step else rows) * STEPS)
        return remote(
            side_out.at[(1 - side) // 2, span, :], side_in.at[k, span, :],
            side_send.at[k], side_recv.at[k], peer(k),
        )

    loads = [
        pltpu.make_async_copy(ref, raw.at[a, pl.ds(0, area), :], load_sem.at[a])
        for a, ref in enumerate((control, kappa))
    ]
    small_loads = [
        pltpu.make_async_copy(ref, to, load_sem.at[3 + n]) for n, (ref, to) in enumerate(zip(small_in, small))
    ]
    loads[1].start()
    loads[0].start()
    for load in small_loads[1:]:
        load.start()
    if not packed:
        obs_load = pltpu.make_async_copy(source, obs, load_sem.at[2])
        obs_load.start()
    small_loads[0].start()

    barrier = pltpu.get_barrier_semaphore()

    @pl.loop(1, n_lon)
    def _(i):
        pl.semaphore_signal(barrier, inc=1, device_id=(lat, around(i)), device_id_type=MESH)

    for step in (-1, 1):
        def greet():
            for side in (-1, 0, 1):
                pl.semaphore_signal(
                    barrier, inc=1, device_id=(lat + step, around(side)), device_id_type=MESH
                )

        only(step, greet)

    sub = iota((EDGE, LANES), 0)
    for a in (1, 0):
        loads[a].wait()
        if chunks * step_rows > area:
            raw[a, area:, :] = jnp.zeros((chunks * step_rows - area, width), F32)
        pairs = raw[a, 0:area, :].reshape(planes // 2, 2, rows, width)
        even, odd = pairs[:, 0], pairs[:, 1]
        upper = iota(even.shape, 1) < STEPS
        band_out[a, 0] = jnp.where(upper, even, pltpu.roll(odd, STEPS, 1)).reshape(area // 2, width).astype(BF16)
        band_out[a, 1] = jnp.where(upper, pltpu.roll(even, STEPS, 1), odd).reshape(area // 2, width).astype(BF16)
        if a == 1:
            pl.semaphore_wait(
                barrier, n_lon - 1 + 3 * (has(-1).astype(jnp.int32) + has(1).astype(jnp.int32))
            )
        for s in range(2):
            only(1 - 2 * s, lambda: band_copy(a, s).start())

    for load in small_loads[1:]:
        load.wait()

    if not packed:
        blocks = columns.shape[0]
        names = owner[...].astype(F32)
        square = (blocks, blocks)
        before = (to_column(names, blocks) == names) & (iota(square, 0) < iota(square, 1))
        place = names * CAP + jnp.sum(jnp.where(before, 1.0, 0.0), axis=0, keepdims=True)
        lined = (blocks, GROUP * blocks)
        comb = jnp.where(lax.rem(iota(lined, 1), blocks) == iota(lined, 0), 1.0, 0.0).astype(BF16)
        place = jnp.broadcast_to(place, (16, blocks)).astype(BF16)
        place = jnp.dot(place, comb, preferred_element_type=F32)[0:1].astype(jnp.int32)
        code = digits(columns[...], to_column(counts[...].astype(F32), blocks))
        codes[...] = jnp.concatenate(code, axis=0).astype(BF16)

    def pack_round(k, h):
        shape = (slots * GROUP, GROUP * blocks)
        at = plane_of(k) * slots + jnp.right_shift(iota(shape, 0), 4)
        hit = (place == at) & (jnp.bitwise_and(iota(shape, 0), GROUP - 1) == iota(shape, 1) // blocks)
        pick = jnp.where(hit, 1.0, 0.0).astype(BF16)
        lo, size = parts[h]
        span = GROUP * blocks

        def put(first, values):
            for t in range(slots):
                part = values[t * GROUP : (t + 1) * GROUP].astype(BF16)
                sent[k, t // CAP, t % CAP, pl.ds(first, GROUP), :] = part

        pairs = (min(lo + size, height - GROUP) - lo) // (2 * GROUP)

        @pl.loop(0, pairs)
        def _(p):
            first = pl.multiple_of(lo + p * 2 * GROUP, GROUP)
            start = pl.multiple_of(first * blocks, span)
            both = jnp.concatenate([obs[pl.ds(start, span), :], obs[pl.ds(start + span, span), :]], axis=1)
            values = jnp.dot(pick, both, preferred_element_type=F32)
            put(first, values[:, :LANES])
            put(pl.multiple_of(first + GROUP, GROUP), values[:, LANES:])

        if lo + size == height:
            last = jnp.concatenate([obs[(height - GROUP) * blocks :, :], codes[...]], axis=0)
            put(height - GROUP, jnp.dot(pick, last, preferred_element_type=F32))

    def send_round(k, h):
        if not packed:
            pack_round(k, h)

        @pl.loop(1, n_lon)
        def _(i):
            block_copy(k, h, i).start()

        own_copy(k, h).start()

    if not packed:
        obs_load.wait()
    for h in range(len(parts)):
        send_round(0, h)

    for a, grid in ((1, coef), (0, field)):
        @pl.loop(0, rows)
        def _(r):
            for j in range(chunks):
                turned = jnp.transpose(raw[a, pl.ds(j * step_rows + r, LANES, stride=rows), :])
                grid[j, STEPS + r, EDGE : EDGE + width, :] = turned

    for k in range(1, n_lat):
        for h in range(len(parts)):
            send_round(k, h)

    small_loads[0].wait()
    matrix = jac_in[...].astype(F32)
    matrix = jnp.concatenate([matrix, jnp.zeros((height - comps, planes), F32)], axis=0)
    if chunks * LANES > planes:
        matrix = jnp.concatenate([matrix, jnp.zeros((height, chunks * LANES - planes), F32)], axis=1)
    jac[...] = matrix.astype(BF16)
    scale[...] = jnp.broadcast_to(to_column(weight_in[...].reshape(1, comps), height), scale.shape)

    def pad_line(h):
        return comps - parts[h][0]

    def lanes(n):
        return pl.ds(pl.multiple_of(n * TILE, TILE), TILE)

    def reduce(k, h):
        lo, size = parts[h]

        @pl.loop(1, n_lon)
        def _(i):
            block_copy(k, h, i).wait_recv()

        own_copy(k, h).wait()
        base = height - GROUP
        first = comps - base
        heads = [recv[k, i, c, base:height, :].astype(F32) for i in range(n_lon) for c in range(CAP)]
        code = jnp.concatenate(
            [(x[first + 1 : first + 2] - 1.0) * 32.0 + x[first + 2 : first + 3] for x in heads], axis=1
        ).astype(jnp.int32)

        @pl.loop(0, cells // TILE)
        def _(n):
            values = jnp.concatenate(
                [recv[k, i, c, lo : lo + size, :] for i in range(n_lon) for c in range(CAP)], axis=1
            )
            hot = jnp.where(iota((TILE, code.shape[1]), 0) == code - n * TILE, 1.0, 0.0).astype(BF16)
            part = lax.dot_general(values, hot, (((1,), (1,)), ((), ())), preferred_element_type=F32)
            if k == n_lat - 1:
                sums[lo : lo + size, lanes(n)] = part
                if h == 0:
                    line = pad_line(h)
                    number[:, lanes(n)] = jnp.broadcast_to(part[line : line + 1], (8, TILE))
            else:
                ring[k % 2, lo : lo + size, lanes(n)] = part

        if k < n_lat - 1:
            pl.when(jnp.logical_not(has(-1) & has(1)))(lambda: emit(k, h, False))

    def emit(k, h, joined):
        lo, size = parts[h]
        o = plane_of(k)
        if joined:
            part_copy(k, h, o, lat).wait_recv()

        @pl.loop(0, cells // TILE)
        def _(n):
            value = ring[k % 2, lo : lo + size, lanes(n)]
            if h == 0:
                line = pad_line(h)
                count = value[line : line + 1]
            if joined:
                more = part_in[o, lo : lo + size, lanes(n)].astype(F32)
                value = value + more
                if h == 0:
                    count = count + more[line : line + 1] + more[line + 1 : line + 2] * COUNT_BASE
            if h == 0:
                high = jnp.floor(count * (1.0 / COUNT_BASE))
                at = iota(value.shape, 0)
                value = jnp.where(at == line, count - high * COUNT_BASE, jnp.where(at == line + 1, high, value))
            part_out[k, lo : lo + size, lanes(n)] = value.astype(BF16)

        part_sent(k, h).start()

    def join(k, h):
        pl.when(has(-1) & has(1))(lambda: emit(k, h, True))

    def fill_rows(a, grid):
        def band(s):
            first = (rows + STEPS) * s

            def arrived():
                band_copy(a, s).wait_recv()
                band_f[0 : area // 2, :] = band_in[a, s].astype(F32)

                @pl.loop(0, STEPS)
                def _(r):
                    for j in range(chunks):
                        piece = band_f[pl.ds(j * STEPS * LANES + r, LANES, stride=STEPS), :]
                        grid[j, first + r, EDGE : EDGE + width, :] = jnp.transpose(piece)

            def closed():
                for r in range(STEPS):
                    for j in range(chunks):
                        grid[j, first + r] = jnp.zeros((wide, LANES), F32)

            pl.when(has(2 * s - 1))(arrived)
            pl.when(jnp.logical_not(has(2 * s - 1)))(closed)

        for s in range(2):
            band(s)

        @pl.loop(0, extent // 2)
        def _(p):
            for j in range(chunks):
                left = [grid[j, 2 * p + q, EDGE : 2 * EDGE, :] for q in range(2)]
                right = [grid[j, 2 * p + q, width : width + EDGE, :] for q in range(2)]
                tile_f[0, j, p] = jnp.where(sub < STEPS, left[0], pltpu.roll(left[1], STEPS, 0))
                tile_f[1, j, p] = jnp.where(sub < STEPS, pltpu.roll(right[0], STEPS, 0), right[1])

        tile_out[a] = tile_f[...].reshape(2, chunks, extent * STEPS, LANES).astype(BF16)
        for k in range(2):
            tile_copy(a, k).start()

    def put_sides(grid, j, p, west, east_):
        pair = (
            jnp.where(sub < STEPS, east_, pltpu.roll(west, STEPS, 0)),
            jnp.where(sub < STEPS, pltpu.roll(east_, STEPS, 0), west),
        )
        for q in range(2):
            grid[j, 2 * p + q, 0:EDGE, :] = pair[q]
            grid[j, 2 * p + q, EDGE + width :, :] = pair[q]

    def fill_columns(a, grid):
        for k in range(2):
            tile_copy(a, k).wait_recv()
        west, east_ = (
            tile_in[a, k].astype(F32).reshape(chunks, extent // 2, EDGE, LANES) for k in range(2)
        )
        for j in range(chunks):
            for p in range(extent // 2):
                put_sides(grid, j, p, west[j, p], east_[j, p])

    def spread(j):
        for step in range(STEPS):
            first, last = step + 1, extent - 1 - step
            here = field[j, first]
            above = coef[j, first - 1] * (here - field[j, first - 1])

            def line(r, carry):
                here, above = carry
                below = field[j, r + 1]
                down = coef[j, r] * (below - here)
                along = east[j, r] * (pltpu.roll(here, wide - 1, 0) - here)
                field[j, r] = here + (down - above) + (along - pltpu.roll(along, 1, 0))
                return below, down

            lax.fori_loop(first, last, line, (here, above), unroll=2)

    def take_kappa():
        if chunks * LANES > planes:
            band_f[area // 2 :, :] = jnp.zeros((chunks * LANES * STEPS - area // 2, width), F32)
        fill_rows(1, coef)

    def take_control():
        fill_rows(0, field)

    def make_state():
        fill_columns(1, coef)

        @pl.loop(0, chunks)
        def _(j):
            @pl.loop(0, extent - 1)
            def _(r):
                here = coef[j, r]
                east[j, r] = here * pltpu.roll(here, wide - 1, 0)
                coef[j, r] = here * coef[j, r + 1]

        fill_columns(0, field)
        pl.loop(0, chunks)(spread)

    def make_model():
        @pl.loop(0, rows)
        def _(r):
            state = jnp.concatenate(
                [field[j, STEPS + r, EDGE : EDGE + width, :].astype(BF16) for j in range(chunks)], axis=1
            )
            model[:, pl.ds(pl.multiple_of(r * width, width), width)] = lax.dot_general(
                jac[...], state, (((1,), (1,)), ((), ())), preferred_element_type=F32
            )

    stages = [take_kappa, take_control, make_state, make_model]
    for k in range(n_lat - 1):
        for h in range(len(parts)):
            reduce(k, h)
            if k > 0:
                join(k - 1, h)
            if k == n_lat - 2:
                join(k, h)
            if stages and k * len(parts) + h > 0:
                stages.pop(0)()
    for stage in stages:
        stage()
    for h in range(len(parts)):
        reduce(n_lat - 1, h)

    for s, ref in enumerate((total_north, total_south)):
        def blank():
            ref[...] = jnp.zeros(ref.shape, BF16)
            side_in[2 + 2 * s] = jnp.zeros(side_in.shape[1:], BF16)
            side_in[3 + 2 * s] = jnp.zeros(side_in.shape[1:], BF16)

        pl.when(jnp.logical_not(has(2 * s - 1)))(blank)

    def add_part(slot, h):
        lo, size = parts[h]
        part_copy(0, h, slot, lat).wait_recv()

        @pl.loop(0, cells // TILE)
        def _(n):
            more = part_in[slot, lo : lo + size, lanes(n)].astype(F32)
            sums[lo : lo + size, lanes(n)] = sums[lo : lo + size, lanes(n)] + more
            if h == 0:
                line = pad_line(h)
                count = more[line : line + 1] + more[line + 1 : line + 2] * COUNT_BASE
                number[:, lanes(n)] = number[:, lanes(n)] + count

    for h, (lo, size) in enumerate(parts):
        only(-1, lambda: add_part(lat, h))
        only(1, lambda: add_part(n_lat, h))
        for r in range(rows):
            at = slice(r * width, (r + 1) * width)
            value = number[0:1, at] * model[lo : lo + size, at] - sums[lo : lo + size, at]
            total[lo : lo + size, at] = (value * scale[lo : lo + size, :]).astype(BF16)
        for s in range(2):
            only(1 - 2 * s, lambda: row_copy(h, s).start())

    ends = (2 * rows * STEPS, cells)
    line = iota(ends, 0)
    spot = lax.rem(line, rows * STEPS)
    spot = (spot // STEPS) * width + lax.rem(spot, STEPS)
    spot = spot + jnp.where(line < rows * STEPS, 0, width - STEPS)
    ends = jnp.where(iota(ends, 1) == spot, 1.0, 0.0).astype(BF16)
    side_out[...] = lax.dot_general(
        ends, total[...], (((1,), (1,)), ((), ())), preferred_element_type=F32
    ).reshape(2, rows * STEPS, height).astype(BF16)
    for k in range(len(SIDES)):
        only(-SIDES[k][0], lambda: side_copy(k).start())

    def put_row(values, r):
        result = lax.dot_general(values, jac[...], (((0,), (0,)), ((), ())), preferred_element_type=F32)
        for j in range(chunks):
            field[j, r, EDGE : EDGE + width, :] = result[:, j * LANES : (j + 1) * LANES]

    @pl.loop(0, rows)
    def _(r):
        put_row(total[:, pl.ds(pl.multiple_of(r * width, width), width)], STEPS + r)

    for k in range(len(SIDES)):
        only(SIDES[k][0], lambda: side_copy(k).wait_recv())

    side = jnp.concatenate(
        [
            side_in[k, lines, :]
            for ks in ((2, 0, 4), (3, 1, 5))
            for k, lines in zip(ks, (slice((rows - STEPS) * STEPS, rows * STEPS), slice(None), slice(0, STEPS * STEPS)))
        ],
        axis=0,
    )
    result = jnp.dot(side, jac[...], preferred_element_type=F32)
    for j in range(chunks):
        for p in range(extent // 2):
            west, east_ = (
                result[first + p * EDGE : first + (p + 1) * EDGE, j * LANES : (j + 1) * LANES]
                for first in (0, extent * STEPS)
            )
            put_sides(field, j, p, west, east_)

    for h in range(len(parts)):
        for s in range(2):
            only(2 * s - 1, lambda: row_copy(h, s).wait_recv())

    @pl.loop(0, STEPS)
    def _(r):
        at = pl.ds(pl.multiple_of(r * width, width), width)
        put_row(total_north[:, at], r)
        put_row(total_south[:, at], STEPS + rows + r)

    stores = []
    for j in range(chunks):
        spread(j)

        @pl.loop(0, rows)
        def _(r):
            at = pl.ds(j * step_rows + r, LANES, stride=rows)
            raw[0, at, :] = raw[0, at, :] + jnp.transpose(field[j, STEPS + r, EDGE : EDGE + width, :])

        span = pl.ds(j * step_rows, min(step_rows, area - j * step_rows))
        stores.append(pltpu.make_async_copy(raw.at[0, span, :], out.at[span, :], store_sem.at[j]))
        stores[-1].start()

    for k in range(n_lat):
        for h in range(len(parts)):
            @pl.loop(1, n_lon)
            def _(i):
                block_copy(k, h, i).wait_send()
    for h in range(len(parts)):
        for k in range(n_lat - 1):
            part_sent(k, h).wait_send()
        for s in range(2):
            only(1 - 2 * s, lambda: row_copy(h, s).wait_send())
    for k in range(len(SIDES)):
        only(-SIDES[k][0], lambda: side_copy(k).wait_send())
    for a in range(2):
        for s in range(2):
            only(1 - 2 * s, lambda: band_copy(a, s).wait_send())
        for k in range(2):
            tile_copy(a, k).wait_send()
    for store in stores:
        store.wait()


def per_device(control, kappa, pc_obs, owner, columns, counts, jacobian, obs_weight):
    n_lat, n_lon = lax.axis_size("lat"), lax.axis_size("lon")
    fields, levels, rows, width = control.shape
    blocks, soundings, comps = pc_obs.shape
    planes = fields * levels
    cells = rows * width
    height = comps + TAIL
    chunks = -(-planes // LANES)
    extent, wide = rows + 2 * STEPS, width + 2 * EDGE
    half = -(-height // 64) * 32
    parts = ((half, height - half), (0, half))
    obs = jnp.transpose(pc_obs, (2, 0, 1))
    slots_shape = (n_lat, n_lon, CAP, height, soundings)
    packed = blocks * GROUP > 1024
    if packed:
        source = pack(obs, owner, columns, counts, n_lat * n_lon, height).reshape(slots_shape)
        extra = []
    else:
        source = obs.reshape(comps * blocks, soundings)
        extra = [
            pltpu.VMEM(slots_shape, BF16),
            pltpu.VMEM(source.shape, BF16),
            pltpu.VMEM((TAIL * blocks, soundings), BF16),
        ]
    small = (jnp.transpose(jacobian), obs_weight, owner.reshape(1, blocks), counts[None, :], columns)
    n_parts, n_sides = len(parts), len(SIDES)
    grid = pltpu.VMEM((chunks, extent, wide, LANES), F32)
    dma = pltpu.SemaphoreType.DMA
    result = pl.pallas_call(
        functools.partial(main_kernel, n_lat, n_lon, planes, parts, packed),
        out_shape=jax.ShapeDtypeStruct((planes * rows, width), F32),
        in_specs=[pl.BlockSpec(memory_space=pl.ANY)] * (3 + len(small)),
        out_specs=pl.BlockSpec(memory_space=pl.ANY),
        scratch_shapes=[pltpu.VMEM(x.shape, x.dtype) for x in small]
        + extra
        + [
            pltpu.VMEM(slots_shape, BF16),
            pltpu.VMEM((2, height, cells), F32),
            pltpu.VMEM((n_lat - 1, height, cells), BF16),
            pltpu.VMEM((n_lat + 1, height, cells), BF16),
            pltpu.VMEM((height, cells), F32),
            pltpu.VMEM((8, cells), F32),
            pltpu.VMEM((height, cells), F32),
            pltpu.VMEM((height, chunks * LANES), BF16),
            pltpu.VMEM((height, LANES), F32),
            grid, grid, grid,
            pltpu.VMEM((2, chunks * LANES * rows, width), F32),
            pltpu.VMEM((2, 2, planes * STEPS, width), BF16),
            pltpu.VMEM((2, 2, planes * STEPS, width), BF16),
            pltpu.VMEM((chunks * LANES * STEPS, width), F32),
            pltpu.VMEM((2, chunks, extent // 2, EDGE, LANES), F32),
            pltpu.VMEM((2, 2, chunks, extent * STEPS, LANES), BF16),
            pltpu.VMEM((2, 2, chunks, extent * STEPS, LANES), BF16),
            pltpu.VMEM((height, cells), BF16),
            pltpu.VMEM((height, STEPS * width), BF16),
            pltpu.VMEM((height, STEPS * width), BF16),
            pltpu.VMEM((2, rows * STEPS, height), BF16),
            pltpu.VMEM((n_sides, rows * STEPS, height), BF16),
            dma((3 + len(small),)), dma((n_lat, n_parts)),
            dma((n_lat, n_parts, n_lon)), dma((n_lat, n_parts, n_lon)),
            dma((n_lat, n_parts)), dma((n_lat + 1, n_parts)),
            dma((2, 2)), dma((2, 2)), dma((2, 2)), dma((2, 2)),
            dma((n_parts, 2)), dma((n_parts, 2)), dma((n_sides,)), dma((n_sides,)),
            dma((chunks,)),
        ],
        compiler_params=pltpu.CompilerParams(
            vmem_limit_bytes=62 * 2**20, has_side_effects=True, collective_id=0
        ),
    )(
        source, control.reshape(planes * rows, width), kappa.reshape(planes * rows, width),
        *small,
    )
    return result.reshape(control.shape)


def solution(mesh):
    placed = (
        P(None, None, "lat", "lon"),
        P(None, None, "lat", "lon"),
        P(("lat", "lon"), None, None),
        P(("lat", "lon"), None),
        P(("lat", "lon"), None),
        P(("lat", "lon")),
        P(),
        P(),
    )
    return jax.shard_map(
        per_device,
        mesh=mesh,
        in_specs=placed,
        out_specs=P(None, None, "lat", "lon"),
        check_vma=False,
    )
```

```python
import functools

import jax
import jax.numpy as jnp
from jax import lax
from jax.experimental import pallas as pl
from jax.experimental.pallas import tpu as pltpu
from jax.sharding import PartitionSpec as P

CAP = 2
STEPS = 4
LANES = 128
GROUP = 16
EDGE = 8
TAIL = 4
COUNT_BASE = 64
TILE = 256
MESH = pl.DeviceIdType.MESH
F32 = jnp.float32
BF16 = jnp.bfloat16
SIDES = ((0, -1), (0, 1), (-1, -1), (-1, 1), (1, -1), (1, 1))


def iota(shape, dim):
    return lax.broadcasted_iota(jnp.int32, shape, dim)


def to_column(row, size):
    shape = (size, row.shape[1])
    return jnp.sum(jnp.where(iota(shape, 0) == iota(shape, 1), row, 0.0), axis=1, keepdims=True)


def digits(columns, counts):
    low = jnp.bitwise_and(columns, 31)
    valid = iota(columns.shape, 1).astype(F32) < counts
    high = jnp.where(valid, jnp.right_shift(columns - low, 5) + 1, 0)
    zero = jnp.zeros(columns.shape, F32)
    return [zero + 1.0, high.astype(F32), low.astype(F32), zero]


def pack_kernel(group, owner_ref, obs_ref, columns_ref, counts_ref, out_ref, wide, source):
    blocks = columns_ref.shape[0]
    comps = obs_ref.shape[0]
    height = out_ref.shape[1]
    slots = source.shape[0]

    @pl.when(pl.program_id(0) == 0)
    def _():
        @pl.loop(0, slots)
        def _(t):
            source[t] = -1

        @pl.loop(0, blocks)
        def _(b):
            first = owner_ref[b] * CAP
            source[jnp.where(source[first] < 0, first, first + 1)] = b

        @pl.loop(0, comps, unroll=4)
        def _(c):
            wide[pl.ds(pl.multiple_of(c * blocks, blocks), blocks), :] = obs_ref[c].astype(F32)

        for k, row in enumerate(digits(columns_ref[...], to_column(counts_ref[...].astype(F32), blocks))):
            wide[(comps + k) * blocks : (comps + k + 1) * blocks, :] = row

    for g in range(group):
        block = source[pl.program_id(0) * group + g]
        rows = wide[pl.ds(jnp.maximum(block, 0), height, stride=blocks), :]
        out_ref[g] = jnp.where(block < 0, 0.0, rows).astype(BF16)


def pack(obs, owner, columns, counts, peers, height):
    comps, blocks, soundings = obs.shape
    slots = peers * CAP
    group = 8
    return pl.pallas_call(
        functools.partial(pack_kernel, group),
        out_shape=jax.ShapeDtypeStruct((slots, height, soundings), BF16),
        grid_spec=pltpu.PrefetchScalarGridSpec(
            num_scalar_prefetch=1,
            grid=(slots // group,),
            in_specs=[
                pl.BlockSpec((comps, blocks, soundings), lambda i, s: (0, 0, 0)),
                pl.BlockSpec((blocks, soundings), lambda i, s: (0, 0)),
                pl.BlockSpec((1, blocks), lambda i, s: (0, 0)),
            ],
            out_specs=pl.BlockSpec((group, height, soundings), lambda i, s: (i, 0, 0)),
            scratch_shapes=[
                pltpu.VMEM((height * blocks, soundings), F32),
                pltpu.SMEM((slots,), jnp.int32),
            ],
        ),
        compiler_params=pltpu.CompilerParams(vmem_limit_bytes=56 * 2**20),
    )(owner[:, 0], obs, columns, counts[None, :])


def main_kernel(n_lat, n_lon, planes, parts, packed, *refs):
    source, control, kappa, *small_in, out = refs[:9]
    small, refs = refs[9:14], refs[14:]
    jac_in, weight_in, owner, counts, columns = small
    sent, obs, codes = (source, None, None) if packed else refs[:3]
    (
        recv, ring, part_out, part_in, sums, number, model, jac, scale,
        field, coef, east, raw, band_out, band_in, band_f, tile_f, tile_out, tile_in,
        total, total_north, total_south, side_out, side_in,
        load_sem, own_sem, blk_send, blk_recv, part_send, part_recv,
        band_send, band_recv, tile_send, tile_recv, row_send, row_recv, side_send, side_recv, store_sem,
    ) = refs if packed else refs[3:]
    lat, lon = lax.axis_index("lat"), lax.axis_index("lon")
    height, cells = sums.shape
    comps = jac_in.shape[0]
    chunks, extent, wide, _ = field.shape
    rows = extent - 2 * STEPS
    width = wide - 2 * EDGE
    area = planes * rows
    step_rows = LANES * rows
    slots = n_lon * CAP

    def plane_of(k):
        mirrored = lat >= n_lat - n_lat // 2
        z = jnp.where(mirrored, n_lat - 1 - lat, lat)
        o = jnp.where(k < n_lat - 1 - z, n_lat - 1 - k, k - (n_lat - 1 - z))
        return jnp.where(mirrored, n_lat - 1 - o, o)

    def remote(src, dst, send, recv_, to):
        return pltpu.make_async_remote_copy(
            src_ref=src, dst_ref=dst, send_sem=send, recv_sem=recv_, device_id=to, device_id_type=MESH
        )

    def around(step):
        return lax.rem(lon + step + n_lon, n_lon)

    def has(step):
        return (lat + step >= 0) & (lat + step < n_lat)

    def only(step, act):
        if step == 0:
            act()
        else:
            pl.when(has(step))(act)

    def slot_of(k):
        return plane_of(k) if packed else k

    def block_copy(k, h, i):
        lo, size = parts[h]
        return remote(
            sent.at[slot_of(k), around(i), :, pl.ds(lo, size), :], recv.at[k, i, :, pl.ds(lo, size), :],
            blk_send.at[k, h, i], blk_recv.at[k, h, i], (lat, around(i)),
        )

    def own_copy(k, h):
        lo, size = parts[h]
        return pltpu.make_async_copy(
            sent.at[slot_of(k), lon, :, pl.ds(lo, size), :],
            recv.at[k, 0, :, pl.ds(lo, size), :], own_sem.at[k, h],
        )

    def part_copy(k, h, slot, to):
        lo, size = parts[h]
        return remote(
            part_out.at[k, pl.ds(lo, size), :], part_in.at[slot, pl.ds(lo, size), :],
            part_send.at[k, h], part_recv.at[slot, h], (to, lon),
        )

    def part_sent(k, h):
        o = plane_of(k)
        north = o < lat
        slot = jnp.where(north & (o == lat - 1), n_lat, o)
        return part_copy(k, h, slot, jnp.where(north, lat - 1, lat + 1))

    def band_copy(a, s):
        return remote(
            band_out.at[a, 1 - s], band_in.at[a, s],
            band_send.at[a, s], band_recv.at[a, s], (lat + (1 - 2 * s), lon),
        )

    def peer(k):
        return (lat - SIDES[k][0], around(-SIDES[k][1]))

    def side_span(k):
        step = SIDES[k][0]
        return pl.ds((rows - STEPS) * STEPS if step < 0 else 0, (STEPS if step else rows) * STEPS)

    def side_of(k):
        return (1 - SIDES[k][1]) // 2

    def tile_copy(a, k):
        span = side_span(k)
        return remote(
            tile_out.at[a, side_of(k), :, span, :], tile_in.at[a, k, :, span, :],
            tile_send.at[a, k], tile_recv.at[a, k], peer(k),
        )

    def row_copy(h, s):
        lo, size = parts[h]
        span = STEPS * width
        return remote(
            total.at[pl.ds(lo, size), pl.ds((1 - s) * (rows * width - span), span)],
            (total_north if s == 0 else total_south).at[pl.ds(lo, size), :],
            row_send.at[h, s], row_recv.at[h, s], (lat + (1 - 2 * s), lon),
        )

    def side_copy(k):
        span = side_span(k)
        return remote(
            side_out.at[side_of(k), span, :], side_in.at[k, span, :], side_send.at[k], side_recv.at[k], peer(k)
        )

    loads = [
        pltpu.make_async_copy(ref, raw.at[a, pl.ds(0, area), :], load_sem.at[a])
        for a, ref in enumerate((control, kappa))
    ]
    small_loads = [
        pltpu.make_async_copy(ref, to, load_sem.at[3 + n]) for n, (ref, to) in enumerate(zip(small_in, small))
    ]
    loads[1].start()
    loads[0].start()
    for load in small_loads[1:]:
        load.start()
    if not packed:
        obs_load = pltpu.make_async_copy(source, obs, load_sem.at[2])
        obs_load.start()
    small_loads[0].start()

    barrier = pltpu.get_barrier_semaphore()

    @pl.loop(1, n_lon)
    def _(i):
        pl.semaphore_signal(barrier, inc=1, device_id=(lat, around(i)), device_id_type=MESH)

    for step in (-1, 1):
        def greet():
            for side in (-1, 0, 1):
                pl.semaphore_signal(
                    barrier, inc=1, device_id=(lat + step, around(side)), device_id_type=MESH
                )

        only(step, greet)

    sub = iota((EDGE, LANES), 0)
    for a in (1, 0):
        loads[a].wait()
        if chunks * step_rows > area:
            raw[a, area:, :] = jnp.zeros((chunks * step_rows - area, width), F32)
        pairs = raw[a, 0:area, :].reshape(planes // 2, 2, rows, width)
        even, odd = pairs[:, 0], pairs[:, 1]
        upper = iota(even.shape, 1) < STEPS
        band_out[a, 0] = jnp.where(upper, even, pltpu.roll(odd, STEPS, 1)).reshape(area // 2, width).astype(BF16)
        band_out[a, 1] = jnp.where(upper, pltpu.roll(even, STEPS, 1), odd).reshape(area // 2, width).astype(BF16)
        if a == 1:
            pl.semaphore_wait(
                barrier, n_lon - 1 + 3 * (has(-1).astype(jnp.int32) + has(1).astype(jnp.int32))
            )
        for s in range(2):
            only(1 - 2 * s, lambda: band_copy(a, s).start())

    for load in small_loads[1:]:
        load.wait()

    if not packed:
        blocks = columns.shape[0]
        names = owner[...].astype(F32)
        square = (blocks, blocks)
        before = (to_column(names, blocks) == names) & (iota(square, 0) < iota(square, 1))
        place = names * CAP + jnp.sum(jnp.where(before, 1.0, 0.0), axis=0, keepdims=True)
        lined = (blocks, GROUP * blocks)
        comb = jnp.where(lax.rem(iota(lined, 1), blocks) == iota(lined, 0), 1.0, 0.0).astype(BF16)
        place = jnp.broadcast_to(place, (16, blocks)).astype(BF16)
        place = jnp.dot(place, comb, preferred_element_type=F32)[0:1].astype(jnp.int32)
        code = digits(columns[...], to_column(counts[...].astype(F32), blocks))
        codes[...] = jnp.concatenate(code, axis=0).astype(BF16)

    def pack_round(k, h):
        shape = (slots * GROUP, GROUP * blocks)
        at = plane_of(k) * slots + jnp.right_shift(iota(shape, 0), 4)
        hit = (place == at) & (jnp.bitwise_and(iota(shape, 0), GROUP - 1) == iota(shape, 1) // blocks)
        pick = jnp.where(hit, 1.0, 0.0).astype(BF16)
        lo, size = parts[h]
        span = GROUP * blocks

        def put(first, values):
            for t in range(slots):
                part = values[t * GROUP : (t + 1) * GROUP].astype(BF16)
                sent[k, t // CAP, t % CAP, pl.ds(first, GROUP), :] = part

        pairs = (min(lo + size, height - GROUP) - lo) // (2 * GROUP)

        @pl.loop(0, pairs)
        def _(p):
            first = pl.multiple_of(lo + p * 2 * GROUP, GROUP)
            start = pl.multiple_of(first * blocks, span)
            both = jnp.concatenate([obs[pl.ds(start, span), :], obs[pl.ds(start + span, span), :]], axis=1)
            values = jnp.dot(pick, both, preferred_element_type=F32)
            put(first, values[:, :LANES])
            put(pl.multiple_of(first + GROUP, GROUP), values[:, LANES:])

        if lo + size == height:
            last = jnp.concatenate([obs[(height - GROUP) * blocks :, :], codes[...]], axis=0)
            put(height - GROUP, jnp.dot(pick, last, preferred_element_type=F32))

    def send_round(k, h):
        if not packed:
            pack_round(k, h)

        @pl.loop(1, n_lon)
        def _(i):
            block_copy(k, h, i).start()

        own_copy(k, h).start()

    if not packed:
        obs_load.wait()
    for h in range(len(parts)):
        send_round(0, h)

    for a, grid in ((1, coef), (0, field)):
        @pl.loop(0, rows)
        def _(r):
            for j in range(chunks):
                turned = jnp.transpose(raw[a, pl.ds(j * step_rows + r, LANES, stride=rows), :])
                grid[j, STEPS + r, EDGE : EDGE + width, :] = turned

        @pl.loop(0, rows // 2)
        def _(p):
            for j in range(chunks):
                pair = [STEPS + 2 * p + q for q in range(2)]
                left = [grid[j, r, EDGE : 2 * EDGE, :] for r in pair]
                right = [grid[j, r, width : width + EDGE, :] for r in pair]
                tile_f[0, j, p] = jnp.where(sub < STEPS, left[0], pltpu.roll(left[1], STEPS, 0))
                tile_f[1, j, p] = jnp.where(sub < STEPS, pltpu.roll(right[0], STEPS, 0), right[1])

        tile_out[a] = tile_f[...].reshape(2, chunks, rows * STEPS, LANES).astype(BF16)
        for k in range(len(SIDES)):
            only(-SIDES[k][0], lambda: tile_copy(a, k).start())

    for k in range(1, n_lat):
        for h in range(len(parts)):
            send_round(k, h)

    small_loads[0].wait()
    matrix = jac_in[...].astype(F32)
    matrix = jnp.concatenate([matrix, jnp.zeros((height - comps, planes), F32)], axis=0)
    if chunks * LANES > planes:
        matrix = jnp.concatenate([matrix, jnp.zeros((height, chunks * LANES - planes), F32)], axis=1)
    jac[...] = matrix.astype(BF16)
    scale[...] = jnp.broadcast_to(to_column(weight_in[...].reshape(1, comps), height), scale.shape)

    def pad_line(h):
        return comps - parts[h][0]

    def lanes(n):
        return pl.ds(pl.multiple_of(n * TILE, TILE), TILE)

    def reduce(k, h):
        lo, size = parts[h]

        @pl.loop(1, n_lon)
        def _(i):
            block_copy(k, h, i).wait_recv()

        own_copy(k, h).wait()
        base = height - GROUP
        first = comps - base
        heads = [recv[k, i, c, base:height, :].astype(F32) for i in range(n_lon) for c in range(CAP)]
        code = jnp.concatenate(
            [(x[first + 1 : first + 2] - 1.0) * 32.0 + x[first + 2 : first + 3] for x in heads], axis=1
        ).astype(jnp.int32)

        @pl.loop(0, cells // TILE)
        def _(n):
            values = jnp.concatenate(
                [recv[k, i, c, lo : lo + size, :] for i in range(n_lon) for c in range(CAP)], axis=1
            )
            hot = jnp.where(iota((TILE, code.shape[1]), 0) == code - n * TILE, 1.0, 0.0).astype(BF16)
            part = lax.dot_general(values, hot, (((1,), (1,)), ((), ())), preferred_element_type=F32)
            if k == n_lat - 1:
                sums[lo : lo + size, lanes(n)] = part
                if h == 0:
                    line = pad_line(h)
                    number[:, lanes(n)] = jnp.broadcast_to(part[line : line + 1], (8, TILE))
            else:
                ring[k % 2, lo : lo + size, lanes(n)] = part

        if k < n_lat - 1:
            pl.when(jnp.logical_not(has(-1) & has(1)))(lambda: emit(k, h, False))

    def emit(k, h, joined):
        lo, size = parts[h]
        o = plane_of(k)
        if joined:
            part_copy(k, h, o, lat).wait_recv()

        @pl.loop(0, cells // TILE)
        def _(n):
            value = ring[k % 2, lo : lo + size, lanes(n)]
            if h == 0:
                line = pad_line(h)
                count = value[line : line + 1]
            if joined:
                more = part_in[o, lo : lo + size, lanes(n)].astype(F32)
                value = value + more
                if h == 0:
                    count = count + more[line : line + 1] + more[line + 1 : line + 2] * COUNT_BASE
            if h == 0:
                high = jnp.floor(count * (1.0 / COUNT_BASE))
                at = iota(value.shape, 0)
                value = jnp.where(at == line, count - high * COUNT_BASE, jnp.where(at == line + 1, high, value))
            part_out[k, lo : lo + size, lanes(n)] = value.astype(BF16)

        part_sent(k, h).start()

    def join(k, h):
        pl.when(has(-1) & has(1))(lambda: emit(k, h, True))

    def fill_rows(a, grid):
        def band(s):
            first = (rows + STEPS) * s

            def arrived():
                band_copy(a, s).wait_recv()
                band_f[0 : area // 2, :] = band_in[a, s].astype(F32)

                @pl.loop(0, STEPS)
                def _(r):
                    for j in range(chunks):
                        piece = band_f[pl.ds(j * STEPS * LANES + r, LANES, stride=STEPS), :]
                        grid[j, first + r, EDGE : EDGE + width, :] = jnp.transpose(piece)

            def closed():
                for r in range(STEPS):
                    for j in range(chunks):
                        grid[j, first + r] = jnp.zeros((wide, LANES), F32)

            pl.when(has(2 * s - 1))(arrived)
            pl.when(jnp.logical_not(has(2 * s - 1)))(closed)

        for s in range(2):
            band(s)

    def put_sides(grid, j, p, west, east_):
        pair = (
            jnp.where(sub < STEPS, east_, pltpu.roll(west, STEPS, 0)),
            jnp.where(sub < STEPS, pltpu.roll(east_, STEPS, 0), west),
        )
        for q in range(2):
            grid[j, 2 * p + q, 0:EDGE, :] = pair[q]
            grid[j, 2 * p + q, EDGE + width :, :] = pair[q]

    def fill_columns(a, grid):
        def sides(k, place, source_row, count):
            for side in (k, k + 1):
                tile_copy(a, side).wait_recv()
            span = slice(source_row * STEPS, (source_row + count) * STEPS)
            west, east_ = (
                tile_in[a, side, :, span, :].astype(F32).reshape(chunks, count // 2, EDGE, LANES)
                for side in (k, k + 1)
            )
            for j in range(chunks):
                for p in range(count // 2):
                    put_sides(grid, j, place // 2 + p, west[j, p], east_[j, p])

        sides(0, STEPS, 0, rows)
        only(-1, lambda: sides(2, 0, rows - STEPS, STEPS))
        only(1, lambda: sides(4, STEPS + rows, 0, STEPS))

    def spread(j):
        for step in range(STEPS):
            first, last = step + 1, extent - 1 - step
            here = field[j, first]
            above = coef[j, first - 1] * (here - field[j, first - 1])

            def line(r, carry):
                here, above = carry
                below = field[j, r + 1]
                down = coef[j, r] * (below - here)
                along = east[j, r] * (pltpu.roll(here, wide - 1, 0) - here)
                field[j, r] = here + (down - above) + (along - pltpu.roll(along, 1, 0))
                return below, down

            lax.fori_loop(first, last, line, (here, above), unroll=2)

    def take_kappa():
        if chunks * LANES > planes:
            band_f[area // 2 :, :] = jnp.zeros((chunks * LANES * STEPS - area // 2, width), F32)
        fill_rows(1, coef)

    def take_control():
        fill_rows(0, field)

    def make_state():
        fill_columns(1, coef)

        @pl.loop(0, chunks)
        def _(j):
            @pl.loop(0, extent - 1)
            def _(r):
                here = coef[j, r]
                east[j, r] = here * pltpu.roll(here, wide - 1, 0)
                coef[j, r] = here * coef[j, r + 1]

        fill_columns(0, field)
        pl.loop(0, chunks)(spread)

    def make_model():
        @pl.loop(0, rows)
        def _(r):
            state = jnp.concatenate(
                [field[j, STEPS + r, EDGE : EDGE + width, :].astype(BF16) for j in range(chunks)], axis=1
            )
            model[:, pl.ds(pl.multiple_of(r * width, width), width)] = lax.dot_general(
                jac[...], state, (((1,), (1,)), ((), ())), preferred_element_type=F32
            )

    stages = [take_kappa, take_control, make_state, make_model]
    for k in range(n_lat - 1):
        for h in range(len(parts)):
            reduce(k, h)
            if k > 0:
                join(k - 1, h)
            if k == n_lat - 2:
                join(k, h)
            if stages and k * len(parts) + h > 0:
                stages.pop(0)()
    for stage in stages:
        stage()
    for h in range(len(parts)):
        reduce(n_lat - 1, h)

    for s, ref in enumerate((total_north, total_south)):
        def blank():
            ref[...] = jnp.zeros(ref.shape, BF16)
            side_in[2 + 2 * s] = jnp.zeros(side_in.shape[1:], BF16)
            side_in[3 + 2 * s] = jnp.zeros(side_in.shape[1:], BF16)

        pl.when(jnp.logical_not(has(2 * s - 1)))(blank)

    def add_part(slot, h):
        lo, size = parts[h]
        part_copy(0, h, slot, lat).wait_recv()

        @pl.loop(0, cells // TILE)
        def _(n):
            more = part_in[slot, lo : lo + size, lanes(n)].astype(F32)
            sums[lo : lo + size, lanes(n)] = sums[lo : lo + size, lanes(n)] + more
            if h == 0:
                line = pad_line(h)
                count = more[line : line + 1] + more[line + 1 : line + 2] * COUNT_BASE
                number[:, lanes(n)] = number[:, lanes(n)] + count

    for h, (lo, size) in enumerate(parts):
        only(-1, lambda: add_part(lat, h))
        only(1, lambda: add_part(n_lat, h))
        for r in range(rows):
            at = slice(r * width, (r + 1) * width)
            value = number[0:1, at] * model[lo : lo + size, at] - sums[lo : lo + size, at]
            total[lo : lo + size, at] = (value * scale[lo : lo + size, :]).astype(BF16)
        for s in range(2):
            only(1 - 2 * s, lambda: row_copy(h, s).start())

    ends = (2 * rows * STEPS, cells)
    line = iota(ends, 0)
    spot = lax.rem(line, rows * STEPS)
    spot = (spot // STEPS) * width + lax.rem(spot, STEPS)
    spot = spot + jnp.where(line < rows * STEPS, 0, width - STEPS)
    ends = jnp.where(iota(ends, 1) == spot, 1.0, 0.0).astype(BF16)
    side_out[...] = lax.dot_general(
        ends, total[...], (((1,), (1,)), ((), ())), preferred_element_type=F32
    ).reshape(2, rows * STEPS, height).astype(BF16)
    for k in range(len(SIDES)):
        only(-SIDES[k][0], lambda: side_copy(k).start())

    def put_row(values, r):
        result = lax.dot_general(values, jac[...], (((0,), (0,)), ((), ())), preferred_element_type=F32)
        for j in range(chunks):
            field[j, r, EDGE : EDGE + width, :] = result[:, j * LANES : (j + 1) * LANES]

    @pl.loop(0, rows)
    def _(r):
        put_row(total[:, pl.ds(pl.multiple_of(r * width, width), width)], STEPS + r)

    for k in range(len(SIDES)):
        only(SIDES[k][0], lambda: side_copy(k).wait_recv())

    side = jnp.concatenate(
        [
            side_in[k, lines, :]
            for ks in ((2, 0, 4), (3, 1, 5))
            for k, lines in zip(ks, (slice((rows - STEPS) * STEPS, rows * STEPS), slice(None), slice(0, STEPS * STEPS)))
        ],
        axis=0,
    )
    result = jnp.dot(side, jac[...], preferred_element_type=F32)
    for j in range(chunks):
        for p in range(extent // 2):
            west, east_ = (
                result[first + p * EDGE : first + (p + 1) * EDGE, j * LANES : (j + 1) * LANES]
                for first in (0, extent * STEPS)
            )
            put_sides(field, j, p, west, east_)

    for h in range(len(parts)):
        for s in range(2):
            only(2 * s - 1, lambda: row_copy(h, s).wait_recv())

    @pl.loop(0, STEPS)
    def _(r):
        at = pl.ds(pl.multiple_of(r * width, width), width)
        put_row(total_north[:, at], r)
        put_row(total_south[:, at], STEPS + rows + r)

    stores = []
    for j in range(chunks):
        spread(j)

        @pl.loop(0, rows)
        def _(r):
            at = pl.ds(j * step_rows + r, LANES, stride=rows)
            raw[0, at, :] = raw[0, at, :] + jnp.transpose(field[j, STEPS + r, EDGE : EDGE + width, :])

        span = pl.ds(j * step_rows, min(step_rows, area - j * step_rows))
        stores.append(pltpu.make_async_copy(raw.at[0, span, :], out.at[span, :], store_sem.at[j]))
        stores[-1].start()

    for k in range(n_lat):
        for h in range(len(parts)):
            @pl.loop(1, n_lon)
            def _(i):
                block_copy(k, h, i).wait_send()
    for h in range(len(parts)):
        for k in range(n_lat - 1):
            part_sent(k, h).wait_send()
        for s in range(2):
            only(1 - 2 * s, lambda: row_copy(h, s).wait_send())
    for k in range(len(SIDES)):
        only(-SIDES[k][0], lambda: side_copy(k).wait_send())
    for a in range(2):
        for s in range(2):
            only(1 - 2 * s, lambda: band_copy(a, s).wait_send())
        for k in range(len(SIDES)):
            only(-SIDES[k][0], lambda: tile_copy(a, k).wait_send())
    for store in stores:
        store.wait()


def per_device(control, kappa, pc_obs, owner, columns, counts, jacobian, obs_weight):
    n_lat, n_lon = lax.axis_size("lat"), lax.axis_size("lon")
    fields, levels, rows, width = control.shape
    blocks, soundings, comps = pc_obs.shape
    planes = fields * levels
    cells = rows * width
    height = comps + TAIL
    chunks = -(-planes // LANES)
    extent, wide = rows + 2 * STEPS, width + 2 * EDGE
    half = -(-height // 64) * 32
    parts = ((half, height - half), (0, half))
    obs = jnp.transpose(pc_obs, (2, 0, 1))
    slots_shape = (n_lat, n_lon, CAP, height, soundings)
    packed = blocks * GROUP > 1024
    if packed:
        source = pack(obs, owner, columns, counts, n_lat * n_lon, height).reshape(slots_shape)
        extra = []
    else:
        source = obs.reshape(comps * blocks, soundings)
        extra = [
            pltpu.VMEM(slots_shape, BF16),
            pltpu.VMEM(source.shape, BF16),
            pltpu.VMEM((TAIL * blocks, soundings), BF16),
        ]
    small = (jnp.transpose(jacobian), obs_weight, owner.reshape(1, blocks), counts[None, :], columns)
    n_parts, n_sides = len(parts), len(SIDES)
    grid = pltpu.VMEM((chunks, extent, wide, LANES), F32)
    dma = pltpu.SemaphoreType.DMA
    result = pl.pallas_call(
        functools.partial(main_kernel, n_lat, n_lon, planes, parts, packed),
        out_shape=jax.ShapeDtypeStruct((planes * rows, width), F32),
        in_specs=[pl.BlockSpec(memory_space=pl.ANY)] * (3 + len(small)),
        out_specs=pl.BlockSpec(memory_space=pl.ANY),
        scratch_shapes=[pltpu.VMEM(x.shape, x.dtype) for x in small]
        + extra
        + [
            pltpu.VMEM(slots_shape, BF16),
            pltpu.VMEM((2, height, cells), F32),
            pltpu.VMEM((n_lat - 1, height, cells), BF16),
            pltpu.VMEM((n_lat + 1, height, cells), BF16),
            pltpu.VMEM((height, cells), F32),
            pltpu.VMEM((8, cells), F32),
            pltpu.VMEM((height, cells), F32),
            pltpu.VMEM((height, chunks * LANES), BF16),
            pltpu.VMEM((height, LANES), F32),
            grid, grid, grid,
            pltpu.VMEM((2, chunks * LANES * rows, width), F32),
            pltpu.VMEM((2, 2, planes * STEPS, width), BF16),
            pltpu.VMEM((2, 2, planes * STEPS, width), BF16),
            pltpu.VMEM((chunks * LANES * STEPS, width), F32),
            pltpu.VMEM((2, chunks, rows // 2, EDGE, LANES), F32),
            pltpu.VMEM((2, 2, chunks, rows * STEPS, LANES), BF16),
            pltpu.VMEM((2, n_sides, chunks, rows * STEPS, LANES), BF16),
            pltpu.VMEM((height, cells), BF16),
            pltpu.VMEM((height, STEPS * width), BF16),
            pltpu.VMEM((height, STEPS * width), BF16),
            pltpu.VMEM((2, rows * STEPS, height), BF16),
            pltpu.VMEM((n_sides, rows * STEPS, height), BF16),
            dma((3 + len(small),)), dma((n_lat, n_parts)),
            dma((n_lat, n_parts, n_lon)), dma((n_lat, n_parts, n_lon)),
            dma((n_lat, n_parts)), dma((n_lat + 1, n_parts)),
            dma((2, 2)), dma((2, 2)), dma((2, n_sides)), dma((2, n_sides)),
            dma((n_parts, 2)), dma((n_parts, 2)), dma((n_sides,)), dma((n_sides,)),
            dma((chunks,)),
        ],
        compiler_params=pltpu.CompilerParams(
            vmem_limit_bytes=62 * 2**20, has_side_effects=True, collective_id=0
        ),
    )(
        source, control.reshape(planes * rows, width), kappa.reshape(planes * rows, width),
        *small,
    )
    return result.reshape(control.shape)


def solution(mesh):
    placed = (
        P(None, None, "lat", "lon"),
        P(None, None, "lat", "lon"),
        P(("lat", "lon"), None, None),
        P(("lat", "lon"), None),
        P(("lat", "lon"), None),
        P(("lat", "lon")),
        P(),
        P(),
    )
    return jax.shard_map(
        per_device,
        mesh=mesh,
        in_specs=placed,
        out_specs=P(None, None, "lat", "lon"),
        check_vma=False,
    )
```

```python
import functools

import jax
import jax.numpy as jnp
from jax import lax
from jax.experimental import pallas as pl
from jax.experimental.pallas import tpu as pltpu
from jax.sharding import PartitionSpec as P

CAP = 2
STEPS = 4
LANES = 128
GROUP = 16
EDGE = 8
TAIL = 4
COUNT_BASE = 64
TILE = 256
MESH = pl.DeviceIdType.MESH
F32 = jnp.float32
BF16 = jnp.bfloat16
SIDES = ((0, -1), (0, 1), (-1, -1), (-1, 1), (1, -1), (1, 1))


def iota(shape, dim):
    return lax.broadcasted_iota(jnp.int32, shape, dim)


def to_column(row, size):
    shape = (size, row.shape[1])
    return jnp.sum(jnp.where(iota(shape, 0) == iota(shape, 1), row, 0.0), axis=1, keepdims=True)


def digits(columns, counts):
    low = jnp.bitwise_and(columns, 31)
    valid = iota(columns.shape, 1).astype(F32) < counts
    high = jnp.where(valid, jnp.right_shift(columns - low, 5) + 1, 0)
    zero = jnp.zeros(columns.shape, F32)
    return [zero + 1.0, high.astype(F32), low.astype(F32), zero]


def pack_kernel(group, owner_ref, obs_ref, columns_ref, counts_ref, out_ref, wide, source):
    blocks = columns_ref.shape[0]
    comps = obs_ref.shape[0]
    height = out_ref.shape[1]
    slots = source.shape[0]

    @pl.when(pl.program_id(0) == 0)
    def _():
        @pl.loop(0, slots)
        def _(t):
            source[t] = -1

        @pl.loop(0, blocks)
        def _(b):
            first = owner_ref[b] * CAP
            source[jnp.where(source[first] < 0, first, first + 1)] = b

        @pl.loop(0, comps, unroll=4)
        def _(c):
            wide[pl.ds(pl.multiple_of(c * blocks, blocks), blocks), :] = obs_ref[c].astype(F32)

        for k, row in enumerate(digits(columns_ref[...], to_column(counts_ref[...].astype(F32), blocks))):
            wide[(comps + k) * blocks : (comps + k + 1) * blocks, :] = row

    for g in range(group):
        block = source[pl.program_id(0) * group + g]
        rows = wide[pl.ds(jnp.maximum(block, 0), height, stride=blocks), :]
        out_ref[g] = jnp.where(block < 0, 0.0, rows).astype(BF16)


def pack(obs, owner, columns, counts, peers, height):
    comps, blocks, soundings = obs.shape
    slots = peers * CAP
    group = 8
    return pl.pallas_call(
        functools.partial(pack_kernel, group),
        out_shape=jax.ShapeDtypeStruct((slots, height, soundings), BF16),
        grid_spec=pltpu.PrefetchScalarGridSpec(
            num_scalar_prefetch=1,
            grid=(slots // group,),
            in_specs=[
                pl.BlockSpec((comps, blocks, soundings), lambda i, s: (0, 0, 0)),
                pl.BlockSpec((blocks, soundings), lambda i, s: (0, 0)),
                pl.BlockSpec((1, blocks), lambda i, s: (0, 0)),
            ],
            out_specs=pl.BlockSpec((group, height, soundings), lambda i, s: (i, 0, 0)),
            scratch_shapes=[
                pltpu.VMEM((height * blocks, soundings), F32),
                pltpu.SMEM((slots,), jnp.int32),
            ],
        ),
        compiler_params=pltpu.CompilerParams(vmem_limit_bytes=56 * 2**20),
    )(owner[:, 0], obs, columns, counts[None, :])


def main_kernel(n_lat, n_lon, planes, parts, packed, *refs):
    source, control, kappa, *small_in, out = refs[:9]
    small, refs = refs[9:14], refs[14:]
    jac_in, weight_in, owner, counts, columns = small
    sent, obs, codes = (source, None, None) if packed else refs[:3]
    (
        recv, ring, part_out, part_in, sums, number, model, jac, scale,
        field, coef, east, raw, band_out, band_in, band_f, tile_f, tile_out, tile_in,
        total, total_north, total_south, side_out, side_in,
        load_sem, own_sem, blk_send, blk_recv, part_send, part_recv,
        band_send, band_recv, tile_send, tile_recv, row_send, row_recv, side_send, side_recv, store_sem,
    ) = refs if packed else refs[3:]
    lat, lon = lax.axis_index("lat"), lax.axis_index("lon")
    height, cells = sums.shape
    comps = jac_in.shape[0]
    chunks, extent, wide, _ = field.shape
    rows = extent - 2 * STEPS
    width = wide - 2 * EDGE
    area = planes * rows
    step_rows = LANES * rows
    slots = n_lon * CAP

    def plane_of(k):
        mirrored = lat >= n_lat - n_lat // 2
        z = jnp.where(mirrored, n_lat - 1 - lat, lat)
        o = jnp.where(k < n_lat - 1 - z, n_lat - 1 - k, k - (n_lat - 1 - z))
        return jnp.where(mirrored, n_lat - 1 - o, o)

    def remote(src, dst, send, recv_, to):
        return pltpu.make_async_remote_copy(
            src_ref=src, dst_ref=dst, send_sem=send, recv_sem=recv_, device_id=to, device_id_type=MESH
        )

    def around(step):
        return lax.rem(lon + step + n_lon, n_lon)

    def has(step):
        return (lat + step >= 0) & (lat + step < n_lat)

    def only(step, act):
        if step == 0:
            act()
        else:
            pl.when(has(step))(act)

    def slot_of(k):
        return plane_of(k) if packed else k

    def block_copy(k, h, i):
        lo, size = parts[h]
        return remote(
            sent.at[slot_of(k), around(i), :, pl.ds(lo, size), :], recv.at[k, i, :, pl.ds(lo, size), :],
            blk_send.at[k, h, i], blk_recv.at[k, h, i], (lat, around(i)),
        )

    def own_copy(k, h):
        lo, size = parts[h]
        return pltpu.make_async_copy(
            sent.at[slot_of(k), lon, :, pl.ds(lo, size), :],
            recv.at[k, 0, :, pl.ds(lo, size), :], own_sem.at[k, h],
        )

    def part_copy(k, h, slot, to):
        lo, size = parts[h]
        return remote(
            part_out.at[k, pl.ds(lo, size), :], part_in.at[slot, pl.ds(lo, size), :],
            part_send.at[k, h], part_recv.at[slot, h], (to, lon),
        )

    def part_sent(k, h):
        o = plane_of(k)
        north = o < lat
        slot = jnp.where(north & (o == lat - 1), n_lat, o)
        return part_copy(k, h, slot, jnp.where(north, lat - 1, lat + 1))

    def band_copy(a, s):
        return remote(
            band_out.at[a, 1 - s], band_in.at[a, s],
            band_send.at[a, s], band_recv.at[a, s], (lat + (1 - 2 * s), lon),
        )

    def peer(k):
        return (lat - SIDES[k][0], around(-SIDES[k][1]))

    def side_span(k):
        step = SIDES[k][0]
        return pl.ds((rows - STEPS) * STEPS if step < 0 else 0, (STEPS if step else rows) * STEPS)

    def side_of(k):
        return (1 - SIDES[k][1]) // 2

    def tile_copy(a, k):
        span = side_span(k)
        return remote(
            tile_out.at[a, side_of(k), :, span, :], tile_in.at[a, k, :, span, :],
            tile_send.at[a, k], tile_recv.at[a, k], peer(k),
        )

    def row_copy(h, s):
        lo, size = parts[h]
        span = STEPS * width
        return remote(
            total.at[pl.ds(lo, size), pl.ds((1 - s) * (rows * width - span), span)],
            (total_north if s == 0 else total_south).at[pl.ds(lo, size), :],
            row_send.at[h, s], row_recv.at[h, s], (lat + (1 - 2 * s), lon),
        )

    def side_copy(k):
        span = side_span(k)
        return remote(
            side_out.at[side_of(k), span, :], side_in.at[k, span, :], side_send.at[k], side_recv.at[k], peer(k)
        )

    loads = [
        pltpu.make_async_copy(ref, raw.at[a, pl.ds(0, area), :], load_sem.at[a])
        for a, ref in enumerate((control, kappa))
    ]
    small_loads = [
        pltpu.make_async_copy(ref, to, load_sem.at[3 + n]) for n, (ref, to) in enumerate(zip(small_in, small))
    ]
    loads[1].start()
    for load in small_loads[1:]:
        load.start()
    if not packed:
        obs_load = pltpu.make_async_copy(source, obs, load_sem.at[2])
        obs_load.start()
    loads[0].start()
    small_loads[0].start()

    barrier = pltpu.get_barrier_semaphore()

    @pl.loop(1, n_lon)
    def _(i):
        pl.semaphore_signal(barrier, inc=1, device_id=(lat, around(i)), device_id_type=MESH)

    for step in (-1, 1):
        def greet():
            for side in (-1, 0, 1):
                pl.semaphore_signal(
                    barrier, inc=1, device_id=(lat + step, around(side)), device_id_type=MESH
                )

        only(step, greet)

    sub = iota((EDGE, LANES), 0)

    def send_bands(a):
        loads[a].wait()
        if chunks * step_rows > area:
            raw[a, area:, :] = jnp.zeros((chunks * step_rows - area, width), F32)
        pairs = raw[a, 0:area, :].reshape(planes // 2, 2, rows, width)
        even, odd = pairs[:, 0], pairs[:, 1]
        upper = iota(even.shape, 1) < STEPS
        band_out[a, 0] = jnp.where(upper, even, pltpu.roll(odd, STEPS, 1)).reshape(area // 2, width).astype(BF16)
        band_out[a, 1] = jnp.where(upper, pltpu.roll(even, STEPS, 1), odd).reshape(area // 2, width).astype(BF16)
        if a == 1:
            pl.semaphore_wait(
                barrier, n_lon - 1 + 3 * (has(-1).astype(jnp.int32) + has(1).astype(jnp.int32))
            )
        for s in range(2):
            only(1 - 2 * s, lambda: band_copy(a, s).start())

    send_bands(1)
    for load in small_loads[1:]:
        load.wait()

    if not packed:
        blocks = columns.shape[0]
        names = owner[...].astype(F32)
        square = (blocks, blocks)
        before = (to_column(names, blocks) == names) & (iota(square, 0) < iota(square, 1))
        place = names * CAP + jnp.sum(jnp.where(before, 1.0, 0.0), axis=0, keepdims=True)
        lined = (blocks, GROUP * blocks)
        comb = jnp.where(lax.rem(iota(lined, 1), blocks) == iota(lined, 0), 1.0, 0.0).astype(BF16)
        place = jnp.broadcast_to(place, (16, blocks)).astype(BF16)
        place = jnp.dot(place, comb, preferred_element_type=F32)[0:1].astype(jnp.int32)
        code = digits(columns[...], to_column(counts[...].astype(F32), blocks))
        codes[...] = jnp.concatenate(code, axis=0).astype(BF16)

    def pack_round(k, h):
        shape = (slots * GROUP, GROUP * blocks)
        at = plane_of(k) * slots + jnp.right_shift(iota(shape, 0), 4)
        hit = (place == at) & (jnp.bitwise_and(iota(shape, 0), GROUP - 1) == iota(shape, 1) // blocks)
        pick = jnp.where(hit, 1.0, 0.0).astype(BF16)
        lo, size = parts[h]
        span = GROUP * blocks

        def put(first, values):
            for t in range(slots):
                part = values[t * GROUP : (t + 1) * GROUP].astype(BF16)
                sent[k, t // CAP, t % CAP, pl.ds(first, GROUP), :] = part

        pairs = (min(lo + size, height - GROUP) - lo) // (2 * GROUP)

        @pl.loop(0, pairs)
        def _(p):
            first = pl.multiple_of(lo + p * 2 * GROUP, GROUP)
            start = pl.multiple_of(first * blocks, span)
            both = jnp.concatenate([obs[pl.ds(start, span), :], obs[pl.ds(start + span, span), :]], axis=1)
            values = jnp.dot(pick, both, preferred_element_type=F32)
            put(first, values[:, :LANES])
            put(pl.multiple_of(first + GROUP, GROUP), values[:, LANES:])

        if lo + size == height:
            last = jnp.concatenate([obs[(height - GROUP) * blocks :, :], codes[...]], axis=0)
            put(height - GROUP, jnp.dot(pick, last, preferred_element_type=F32))

    def send_round(k, h):
        if not packed:
            pack_round(k, h)

        @pl.loop(1, n_lon)
        def _(i):
            block_copy(k, h, i).start()

        own_copy(k, h).start()

    if not packed:
        obs_load.wait()
    for h in range(len(parts)):
        send_round(0, h)
        if h == 0:
            send_bands(0)

    for a, grid in ((1, coef), (0, field)):
        @pl.loop(0, rows)
        def _(r):
            for j in range(chunks):
                turned = jnp.transpose(raw[a, pl.ds(j * step_rows + r, LANES, stride=rows), :])
                grid[j, STEPS + r, EDGE : EDGE + width, :] = turned

        @pl.loop(0, rows // 2)
        def _(p):
            for j in range(chunks):
                pair = [STEPS + 2 * p + q for q in range(2)]
                left = [grid[j, r, EDGE : 2 * EDGE, :] for r in pair]
                right = [grid[j, r, width : width + EDGE, :] for r in pair]
                tile_f[0, j, p] = jnp.where(sub < STEPS, left[0], pltpu.roll(left[1], STEPS, 0))
                tile_f[1, j, p] = jnp.where(sub < STEPS, pltpu.roll(right[0], STEPS, 0), right[1])

        tile_out[a] = tile_f[...].reshape(2, chunks, rows * STEPS, LANES).astype(BF16)
        for k in range(len(SIDES)):
            only(-SIDES[k][0], lambda: tile_copy(a, k).start())

    for k in range(1, n_lat):
        for h in range(len(parts)):
            send_round(k, h)

    small_loads[0].wait()
    matrix = jac_in[...].astype(F32)
    matrix = jnp.concatenate([matrix, jnp.zeros((height - comps, planes), F32)], axis=0)
    if chunks * LANES > planes:
        matrix = jnp.concatenate([matrix, jnp.zeros((height, chunks * LANES - planes), F32)], axis=1)
    jac[...] = matrix.astype(BF16)
    scale[...] = jnp.broadcast_to(to_column(weight_in[...].reshape(1, comps), height), scale.shape)

    def pad_line(h):
        return comps - parts[h][0]

    def lanes(n):
        return pl.ds(pl.multiple_of(n * TILE, TILE), TILE)

    def reduce_peers(k, h, start, stop):
        lo, size = parts[h]

        @pl.loop(max(start, 1), stop)
        def _(i):
            block_copy(k, h, i).wait_recv()

        base = height - GROUP
        first = comps - base
        heads = [recv[k, i, c, base:height, :].astype(F32) for i in range(start, stop) for c in range(CAP)]
        code = jnp.concatenate(
            [(x[first + 1 : first + 2] - 1.0) * 32.0 + x[first + 2 : first + 3] for x in heads], axis=1
        ).astype(jnp.int32)

        @pl.loop(0, cells // TILE)
        def _(n):
            values = jnp.concatenate(
                [recv[k, i, c, lo : lo + size, :] for i in range(start, stop) for c in range(CAP)], axis=1
            )
            hot = jnp.where(iota((TILE, code.shape[1]), 0) == code - n * TILE, 1.0, 0.0).astype(BF16)
            part = lax.dot_general(values, hot, (((1,), (1,)), ((), ())), preferred_element_type=F32)
            target = sums.at[lo : lo + size, lanes(n)]
            if k < n_lat - 1:
                target = ring.at[k % 2, lo : lo + size, lanes(n)]
            target[...] = part if start == 0 else target[...] + part
            if k == n_lat - 1 and h == 0:
                line = pad_line(h)
                number[:, lanes(n)] = jnp.broadcast_to(part[line : line + 1], (8, TILE))

    def reduce(k, h, groups=1):
        own_copy(k, h).wait()
        for g in range(groups):
            peers = n_lon // groups
            reduce_peers(k, h, g * peers, (g + 1) * peers)
        if k < n_lat - 1:
            pl.when(jnp.logical_not(has(-1) & has(1)))(lambda: emit(k, h, False))

    def emit(k, h, joined):
        lo, size = parts[h]
        o = plane_of(k)
        if joined:
            part_copy(k, h, o, lat).wait_recv()

        @pl.loop(0, cells // TILE)
        def _(n):
            value = ring[k % 2, lo : lo + size, lanes(n)]
            if h == 0:
                line = pad_line(h)
                count = value[line : line + 1]
            if joined:
                more = part_in[o, lo : lo + size, lanes(n)].astype(F32)
                value = value + more
                if h == 0:
                    count = count + more[line : line + 1] + more[line + 1 : line + 2] * COUNT_BASE
            if h == 0:
                high = jnp.floor(count * (1.0 / COUNT_BASE))
                at = iota(value.shape, 0)
                value = jnp.where(at == line, count - high * COUNT_BASE, jnp.where(at == line + 1, high, value))
            part_out[k, lo : lo + size, lanes(n)] = value.astype(BF16)

        part_sent(k, h).start()

    def join(k, h):
        pl.when(has(-1) & has(1))(lambda: emit(k, h, True))

    def fill_rows(a, grid):
        def band(s):
            first = (rows + STEPS) * s

            def arrived():
                band_copy(a, s).wait_recv()
                band_f[0 : area // 2, :] = band_in[a, s].astype(F32)

                @pl.loop(0, STEPS)
                def _(r):
                    for j in range(chunks):
                        piece = band_f[pl.ds(j * STEPS * LANES + r, LANES, stride=STEPS), :]
                        grid[j, first + r, EDGE : EDGE + width, :] = jnp.transpose(piece)

            def closed():
                for r in range(STEPS):
                    for j in range(chunks):
                        grid[j, first + r] = jnp.zeros((wide, LANES), F32)

            pl.when(has(2 * s - 1))(arrived)
            pl.when(jnp.logical_not(has(2 * s - 1)))(closed)

        for s in range(2):
            band(s)

    def put_sides(grid, j, p, west, east_):
        pair = (
            jnp.where(sub < STEPS, east_, pltpu.roll(west, STEPS, 0)),
            jnp.where(sub < STEPS, pltpu.roll(east_, STEPS, 0), west),
        )
        for q in range(2):
            grid[j, 2 * p + q, 0:EDGE, :] = pair[q]
            grid[j, 2 * p + q, EDGE + width :, :] = pair[q]

    def fill_columns(a, grid):
        def sides(k, place, source_row, count):
            for side in (k, k + 1):
                tile_copy(a, side).wait_recv()
            span = slice(source_row * STEPS, (source_row + count) * STEPS)
            west, east_ = (
                tile_in[a, side, :, span, :].astype(F32).reshape(chunks, count // 2, EDGE, LANES)
                for side in (k, k + 1)
            )
            for j in range(chunks):
                for p in range(count // 2):
                    put_sides(grid, j, place // 2 + p, west[j, p], east_[j, p])

        sides(0, STEPS, 0, rows)
        only(-1, lambda: sides(2, 0, rows - STEPS, STEPS))
        only(1, lambda: sides(4, STEPS + rows, 0, STEPS))

    def spread(j):
        for step in range(STEPS):
            first, last = step + 1, extent - 1 - step
            above = coef[j, first - 1] * (field[j, first] - field[j, first - 1])

            def line(r, above):
                here = field[j, r]
                down = coef[j, r] * (field[j, r + 1] - here)
                along = east[j, r] * (pltpu.roll(here, wide - 1, 0) - here)
                field[j, r] = here + (down - above) + (along - pltpu.roll(along, 1, 0))
                return down

            lax.fori_loop(first, last, line, above, unroll=2)

    def take_kappa():
        if chunks * LANES > planes:
            band_f[area // 2 :, :] = jnp.zeros((chunks * LANES * STEPS - area // 2, width), F32)
        fill_rows(1, coef)

    def take_control():
        fill_rows(0, field)

    def make_state():
        fill_columns(1, coef)

        @pl.loop(0, chunks)
        def _(j):
            @pl.loop(0, extent - 1)
            def _(r):
                here = coef[j, r]
                east[j, r] = here * pltpu.roll(here, wide - 1, 0)
                coef[j, r] = here * coef[j, r + 1]

        fill_columns(0, field)
        pl.loop(0, chunks)(spread)

    def make_model():
        @pl.loop(0, rows)
        def _(r):
            state = jnp.concatenate(
                [field[j, STEPS + r, EDGE : EDGE + width, :].astype(BF16) for j in range(chunks)], axis=1
            )
            model[:, pl.ds(pl.multiple_of(r * width, width), width)] = lax.dot_general(
                jac[...], state, (((1,), (1,)), ((), ())), preferred_element_type=F32
            )

    stages = [take_kappa, take_control, make_state, make_model]
    for k in range(n_lat - 1):
        for h in range(len(parts)):
            reduce(k, h)
            if k > 0:
                join(k - 1, h)
            if k == n_lat - 2:
                join(k, h)
            if stages and k * len(parts) + h > 0:
                stages.pop(0)()
    for stage in stages:
        stage()

    for s, ref in enumerate((total_north, total_south)):
        def blank():
            ref[...] = jnp.zeros(ref.shape, BF16)
            side_in[2 + 2 * s] = jnp.zeros(side_in.shape[1:], BF16)
            side_in[3 + 2 * s] = jnp.zeros(side_in.shape[1:], BF16)

        pl.when(jnp.logical_not(has(2 * s - 1)))(blank)

    def add_part(slot, h):
        lo, size = parts[h]
        part_copy(0, h, slot, lat).wait_recv()

        @pl.loop(0, cells // TILE)
        def _(n):
            more = part_in[slot, lo : lo + size, lanes(n)].astype(F32)
            sums[lo : lo + size, lanes(n)] = sums[lo : lo + size, lanes(n)] + more
            if h == 0:
                line = pad_line(h)
                count = more[line : line + 1] + more[line + 1 : line + 2] * COUNT_BASE
                number[:, lanes(n)] = number[:, lanes(n)] + count

    for h, (lo, size) in enumerate(parts):
        reduce(n_lat - 1, h, groups=2 if h == len(parts) - 1 else 1)
        only(-1, lambda: add_part(lat, h))
        only(1, lambda: add_part(n_lat, h))
        for r in range(rows):
            at = slice(r * width, (r + 1) * width)
            value = number[0:1, at] * model[lo : lo + size, at] - sums[lo : lo + size, at]
            total[lo : lo + size, at] = (value * scale[lo : lo + size, :]).astype(BF16)
        for s in range(2):
            only(1 - 2 * s, lambda: row_copy(h, s).start())

    ends = (2 * rows * STEPS, cells)
    line = iota(ends, 0)
    spot = lax.rem(line, rows * STEPS)
    spot = (spot // STEPS) * width + lax.rem(spot, STEPS)
    spot = spot + jnp.where(line < rows * STEPS, 0, width - STEPS)
    ends = jnp.where(iota(ends, 1) == spot, 1.0, 0.0).astype(BF16)
    side_out[...] = lax.dot_general(
        ends, total[...], (((1,), (1,)), ((), ())), preferred_element_type=F32
    ).reshape(2, rows * STEPS, height).astype(BF16)
    for k in range(len(SIDES)):
        only(-SIDES[k][0], lambda: side_copy(k).start())

    def put_row(values, r):
        result = lax.dot_general(values, jac[...], (((0,), (0,)), ((), ())), preferred_element_type=F32)
        for j in range(chunks):
            field[j, r, EDGE : EDGE + width, :] = result[:, j * LANES : (j + 1) * LANES]

    @pl.loop(0, rows)
    def _(r):
        put_row(total[:, pl.ds(pl.multiple_of(r * width, width), width)], STEPS + r)

    for k in range(len(SIDES)):
        only(SIDES[k][0], lambda: side_copy(k).wait_recv())

    side = jnp.concatenate(
        [
            side_in[k, lines, :]
            for ks in ((2, 0, 4), (3, 1, 5))
            for k, lines in zip(ks, (slice((rows - STEPS) * STEPS, rows * STEPS), slice(None), slice(0, STEPS * STEPS)))
        ],
        axis=0,
    )
    result = jnp.dot(side, jac[...], preferred_element_type=F32)
    for j in range(chunks):
        for p in range(extent // 2):
            west, east_ = (
                result[first + p * EDGE : first + (p + 1) * EDGE, j * LANES : (j + 1) * LANES]
                for first in (0, extent * STEPS)
            )
            put_sides(field, j, p, west, east_)

    for h in range(len(parts)):
        for s in range(2):
            only(2 * s - 1, lambda: row_copy(h, s).wait_recv())

    @pl.loop(0, STEPS)
    def _(r):
        at = pl.ds(pl.multiple_of(r * width, width), width)
        put_row(total_north[:, at], r)
        put_row(total_south[:, at], STEPS + rows + r)

    stores = []
    for j in range(chunks):
        spread(j)

        @pl.loop(0, rows)
        def _(r):
            at = pl.ds(j * step_rows + r, LANES, stride=rows)
            raw[0, at, :] = raw[0, at, :] + jnp.transpose(field[j, STEPS + r, EDGE : EDGE + width, :])

        span = pl.ds(j * step_rows, min(step_rows, area - j * step_rows))
        stores.append(pltpu.make_async_copy(raw.at[0, span, :], out.at[span, :], store_sem.at[j]))
        stores[-1].start()

    for k in range(n_lat):
        for h in range(len(parts)):
            @pl.loop(1, n_lon)
            def _(i):
                block_copy(k, h, i).wait_send()
    for h in range(len(parts)):
        for k in range(n_lat - 1):
            part_sent(k, h).wait_send()
        for s in range(2):
            only(1 - 2 * s, lambda: row_copy(h, s).wait_send())
    for k in range(len(SIDES)):
        only(-SIDES[k][0], lambda: side_copy(k).wait_send())
    for a in range(2):
        for s in range(2):
            only(1 - 2 * s, lambda: band_copy(a, s).wait_send())
        for k in range(len(SIDES)):
            only(-SIDES[k][0], lambda: tile_copy(a, k).wait_send())
    for store in stores:
        store.wait()


def per_device(control, kappa, pc_obs, owner, columns, counts, jacobian, obs_weight):
    n_lat, n_lon = lax.axis_size("lat"), lax.axis_size("lon")
    fields, levels, rows, width = control.shape
    blocks, soundings, comps = pc_obs.shape
    planes = fields * levels
    cells = rows * width
    height = comps + TAIL
    chunks = -(-planes // LANES)
    extent, wide = rows + 2 * STEPS, width + 2 * EDGE
    half = height // 96 * 32
    parts = ((half, height - half), (0, half))
    obs = jnp.transpose(pc_obs, (2, 0, 1))
    slots_shape = (n_lat, n_lon, CAP, height, soundings)
    packed = blocks * GROUP > 1024
    if packed:
        source = pack(obs, owner, columns, counts, n_lat * n_lon, height).reshape(slots_shape)
        extra = []
    else:
        source = obs.reshape(comps * blocks, soundings)
        extra = [
            pltpu.VMEM(slots_shape, BF16),
            pltpu.VMEM(source.shape, BF16),
            pltpu.VMEM((TAIL * blocks, soundings), BF16),
        ]
    small = (jnp.transpose(jacobian), obs_weight, owner.reshape(1, blocks), counts[None, :], columns)
    n_parts, n_sides = len(parts), len(SIDES)
    grid = pltpu.VMEM((chunks, extent, wide, LANES), F32)
    dma = pltpu.SemaphoreType.DMA
    result = pl.pallas_call(
        functools.partial(main_kernel, n_lat, n_lon, planes, parts, packed),
        out_shape=jax.ShapeDtypeStruct((planes * rows, width), F32),
        in_specs=[pl.BlockSpec(memory_space=pl.ANY)] * (3 + len(small)),
        out_specs=pl.BlockSpec(memory_space=pl.ANY),
        scratch_shapes=[pltpu.VMEM(x.shape, x.dtype) for x in small]
        + extra
        + [
            pltpu.VMEM(slots_shape, BF16),
            pltpu.VMEM((2, height, cells), F32),
            pltpu.VMEM((n_lat - 1, height, cells), BF16),
            pltpu.VMEM((n_lat + 1, height, cells), BF16),
            pltpu.VMEM((height, cells), F32),
            pltpu.VMEM((8, cells), F32),
            pltpu.VMEM((height, cells), F32),
            pltpu.VMEM((height, chunks * LANES), BF16),
            pltpu.VMEM((height, LANES), F32),
            grid, grid, grid,
            pltpu.VMEM((2, chunks * LANES * rows, width), F32),
            pltpu.VMEM((2, 2, planes * STEPS, width), BF16),
            pltpu.VMEM((2, 2, planes * STEPS, width), BF16),
            pltpu.VMEM((chunks * LANES * STEPS, width), F32),
            pltpu.VMEM((2, chunks, rows // 2, EDGE, LANES), F32),
            pltpu.VMEM((2, 2, chunks, rows * STEPS, LANES), BF16),
            pltpu.VMEM((2, n_sides, chunks, rows * STEPS, LANES), BF16),
            pltpu.VMEM((height, cells), BF16),
            pltpu.VMEM((height, STEPS * width), BF16),
            pltpu.VMEM((height, STEPS * width), BF16),
            pltpu.VMEM((2, rows * STEPS, height), BF16),
            pltpu.VMEM((n_sides, rows * STEPS, height), BF16),
            dma((3 + len(small),)), dma((n_lat, n_parts)),
            dma((n_lat, n_parts, n_lon)), dma((n_lat, n_parts, n_lon)),
            dma((n_lat, n_parts)), dma((n_lat + 1, n_parts)),
            dma((2, 2)), dma((2, 2)), dma((2, n_sides)), dma((2, n_sides)),
            dma((n_parts, 2)), dma((n_parts, 2)), dma((n_sides,)), dma((n_sides,)),
            dma((chunks,)),
        ],
        compiler_params=pltpu.CompilerParams(
            vmem_limit_bytes=62 * 2**20, has_side_effects=True, collective_id=0
        ),
    )(
        source, control.reshape(planes * rows, width), kappa.reshape(planes * rows, width),
        *small,
    )
    return result.reshape(control.shape)


def solution(mesh):
    placed = (
        P(None, None, "lat", "lon"),
        P(None, None, "lat", "lon"),
        P(("lat", "lon"), None, None),
        P(("lat", "lon"), None),
        P(("lat", "lon"), None),
        P(("lat", "lon")),
        P(),
        P(),
    )
    return jax.shard_map(
        per_device,
        mesh=mesh,
        in_specs=placed,
        out_specs=P(None, None, "lat", "lon"),
        check_vma=False,
    )
```

```python
import functools

import jax
import jax.numpy as jnp
from jax import lax
from jax.experimental import pallas as pl
from jax.experimental.pallas import tpu as pltpu
from jax.sharding import PartitionSpec as P

CAP = 2
STEPS = 4
LANES = 128
GROUP = 16
EDGE = 8
TAIL = 4
COUNT_BASE = 64
TILE = 256
MESH = pl.DeviceIdType.MESH
F32 = jnp.float32
BF16 = jnp.bfloat16
SIDES = ((0, -1), (0, 1), (-1, -1), (-1, 1), (1, -1), (1, 1))


def iota(shape, dim):
    return lax.broadcasted_iota(jnp.int32, shape, dim)


def to_column(row, size):
    shape = (size, row.shape[1])
    return jnp.sum(jnp.where(iota(shape, 0) == iota(shape, 1), row, 0.0), axis=1, keepdims=True)


def digits(columns, counts):
    low = jnp.bitwise_and(columns, 31)
    valid = iota(columns.shape, 1).astype(F32) < counts
    high = jnp.where(valid, jnp.right_shift(columns - low, 5) + 1, 0)
    zero = jnp.zeros(columns.shape, F32)
    return [zero + 1.0, high.astype(F32), low.astype(F32), zero]


def pack_kernel(group, owner_ref, obs_ref, columns_ref, counts_ref, out_ref, wide, source):
    blocks = columns_ref.shape[0]
    comps = obs_ref.shape[0]
    height = out_ref.shape[1]
    slots = source.shape[0]

    @pl.when(pl.program_id(0) == 0)
    def _():
        @pl.loop(0, slots)
        def _(t):
            source[t] = -1

        @pl.loop(0, blocks)
        def _(b):
            first = owner_ref[b] * CAP
            source[jnp.where(source[first] < 0, first, first + 1)] = b

        @pl.loop(0, comps, unroll=4)
        def _(c):
            wide[pl.ds(pl.multiple_of(c * blocks, blocks), blocks), :] = obs_ref[c].astype(F32)

        for k, row in enumerate(digits(columns_ref[...], to_column(counts_ref[...].astype(F32), blocks))):
            wide[(comps + k) * blocks : (comps + k + 1) * blocks, :] = row

    for g in range(group):
        block = source[pl.program_id(0) * group + g]
        rows = wide[pl.ds(jnp.maximum(block, 0), height, stride=blocks), :]
        out_ref[g] = jnp.where(block < 0, 0.0, rows).astype(BF16)


def pack(obs, owner, columns, counts, peers, height):
    comps, blocks, soundings = obs.shape
    slots = peers * CAP
    group = 8
    return pl.pallas_call(
        functools.partial(pack_kernel, group),
        out_shape=jax.ShapeDtypeStruct((slots, height, soundings), BF16),
        grid_spec=pltpu.PrefetchScalarGridSpec(
            num_scalar_prefetch=1,
            grid=(slots // group,),
            in_specs=[
                pl.BlockSpec((comps, blocks, soundings), lambda i, s: (0, 0, 0)),
                pl.BlockSpec((blocks, soundings), lambda i, s: (0, 0)),
                pl.BlockSpec((1, blocks), lambda i, s: (0, 0)),
            ],
            out_specs=pl.BlockSpec((group, height, soundings), lambda i, s: (i, 0, 0)),
            scratch_shapes=[
                pltpu.VMEM((height * blocks, soundings), F32),
                pltpu.SMEM((slots,), jnp.int32),
            ],
        ),
        compiler_params=pltpu.CompilerParams(vmem_limit_bytes=56 * 2**20),
    )(owner[:, 0], obs, columns, counts[None, :])


def main_kernel(n_lat, n_lon, planes, parts, packed, *refs):
    source, control, kappa, *small_in, out = refs[:9]
    small, refs = refs[9:14], refs[14:]
    jac_in, weight_in, owner, counts, columns = small
    sent, obs, codes = (source, None, None) if packed else refs[:3]
    (
        recv, ring, part_out, part_in, sums, number, model, jac, scale,
        field, coef, east, raw, band_out, band_in, band_f, tile_f, tile_out, tile_in,
        total, total_north, total_south, side_out, side_in,
        load_sem, own_sem, blk_send, blk_recv, part_send, part_recv,
        band_send, band_recv, tile_send, tile_recv, row_send, row_recv, side_send, side_recv, store_sem,
    ) = refs if packed else refs[3:]
    lat, lon = lax.axis_index("lat"), lax.axis_index("lon")
    height, cells = sums.shape
    comps = jac_in.shape[0]
    chunks, extent, wide, _ = field.shape
    rows = extent - 2 * STEPS
    width = wide - 2 * EDGE
    area = planes * rows
    step_rows = LANES * rows
    slots = n_lon * CAP

    def plane_of(k):
        mirrored = lat >= n_lat - n_lat // 2
        z = jnp.where(mirrored, n_lat - 1 - lat, lat)
        o = jnp.where(k < n_lat - 1 - z, n_lat - 1 - k, k - (n_lat - 1 - z))
        return jnp.where(mirrored, n_lat - 1 - o, o)

    def remote(src, dst, send, recv_, to):
        return pltpu.make_async_remote_copy(
            src_ref=src, dst_ref=dst, send_sem=send, recv_sem=recv_, device_id=to, device_id_type=MESH
        )

    def around(step):
        return lax.rem(lon + step + n_lon, n_lon)

    def has(step):
        return (lat + step >= 0) & (lat + step < n_lat)

    def only(step, act):
        if step == 0:
            act()
        else:
            pl.when(has(step))(act)

    def slot_of(k):
        return plane_of(k) if packed else k

    def block_copy(k, h, i):
        lo, size = parts[h]
        return remote(
            sent.at[slot_of(k), around(i), :, pl.ds(lo, size), :], recv.at[k, i, :, pl.ds(lo, size), :],
            blk_send.at[k, h, i], blk_recv.at[k, h, i], (lat, around(i)),
        )

    def own_copy(k, h):
        lo, size = parts[h]
        return pltpu.make_async_copy(
            sent.at[slot_of(k), lon, :, pl.ds(lo, size), :],
            recv.at[k, 0, :, pl.ds(lo, size), :], own_sem.at[k, h],
        )

    def part_copy(k, h, slot, to):
        lo, size = parts[h]
        return remote(
            part_out.at[k, pl.ds(lo, size), :], part_in.at[slot, pl.ds(lo, size), :],
            part_send.at[k, h], part_recv.at[slot, h], (to, lon),
        )

    def part_sent(k, h):
        o = plane_of(k)
        north = o < lat
        slot = jnp.where(north & (o == lat - 1), n_lat, o)
        return part_copy(k, h, slot, jnp.where(north, lat - 1, lat + 1))

    def band_copy(a, s):
        return remote(
            band_out.at[a, 1 - s], band_in.at[a, s],
            band_send.at[a, s], band_recv.at[a, s], (lat + (1 - 2 * s), lon),
        )

    def peer(k):
        return (lat - SIDES[k][0], around(-SIDES[k][1]))

    def side_span(k):
        step = SIDES[k][0]
        return pl.ds((rows - STEPS) * STEPS if step < 0 else 0, (STEPS if step else rows) * STEPS)

    def side_of(k):
        return (1 - SIDES[k][1]) // 2

    def tile_copy(a, k):
        span = side_span(k)
        return remote(
            tile_out.at[a, side_of(k), :, span, :], tile_in.at[a, k, :, span, :],
            tile_send.at[a, k], tile_recv.at[a, k], peer(k),
        )

    def row_copy(h, s):
        lo, size = parts[h]
        span = STEPS * width
        return remote(
            total.at[pl.ds(lo, size), pl.ds((1 - s) * (rows * width - span), span)],
            (total_north if s == 0 else total_south).at[pl.ds(lo, size), :],
            row_send.at[h, s], row_recv.at[h, s], (lat + (1 - 2 * s), lon),
        )

    def side_copy(k):
        span = side_span(k)
        return remote(
            side_out.at[side_of(k), span, :], side_in.at[k, span, :], side_send.at[k], side_recv.at[k], peer(k)
        )

    loads = [
        pltpu.make_async_copy(ref, raw.at[a, pl.ds(0, area), :], load_sem.at[a])
        for a, ref in enumerate((control, kappa))
    ]
    small_loads = [
        pltpu.make_async_copy(ref, to, load_sem.at[3 + n]) for n, (ref, to) in enumerate(zip(small_in, small))
    ]
    loads[1].start()
    for load in small_loads[1:]:
        load.start()
    if not packed:
        obs_load = pltpu.make_async_copy(source, obs, load_sem.at[2])
        obs_load.start()
    loads[0].start()
    small_loads[0].start()

    barrier = pltpu.get_barrier_semaphore()

    @pl.loop(1, n_lon)
    def _(i):
        pl.semaphore_signal(barrier, inc=1, device_id=(lat, around(i)), device_id_type=MESH)

    for step in (-1, 1):
        def greet():
            for side in (-1, 0, 1):
                pl.semaphore_signal(
                    barrier, inc=1, device_id=(lat + step, around(side)), device_id_type=MESH
                )

        only(step, greet)

    sub = iota((EDGE, LANES), 0)

    def send_bands(a):
        loads[a].wait()
        if chunks * step_rows > area:
            raw[a, area:, :] = jnp.zeros((chunks * step_rows - area, width), F32)
        pairs = raw[a, 0:area, :].reshape(planes // 2, 2, rows, width)
        even, odd = pairs[:, 0], pairs[:, 1]
        upper = iota(even.shape, 1) < STEPS
        band_out[a, 0] = jnp.where(upper, even, pltpu.roll(odd, STEPS, 1)).reshape(area // 2, width).astype(BF16)
        band_out[a, 1] = jnp.where(upper, pltpu.roll(even, STEPS, 1), odd).reshape(area // 2, width).astype(BF16)
        if a == 1:
            pl.semaphore_wait(
                barrier, n_lon - 1 + 3 * (has(-1).astype(jnp.int32) + has(1).astype(jnp.int32))
            )
        for s in range(2):
            only(1 - 2 * s, lambda: band_copy(a, s).start())

    send_bands(1)
    for load in small_loads[1:]:
        load.wait()

    if not packed:
        blocks = columns.shape[0]
        names = owner[...].astype(F32)
        square = (blocks, blocks)
        before = (to_column(names, blocks) == names) & (iota(square, 0) < iota(square, 1))
        place = names * CAP + jnp.sum(jnp.where(before, 1.0, 0.0), axis=0, keepdims=True)
        lined = (blocks, GROUP * blocks)
        comb = jnp.where(lax.rem(iota(lined, 1), blocks) == iota(lined, 0), 1.0, 0.0).astype(BF16)
        place = jnp.broadcast_to(place, (16, blocks)).astype(BF16)
        place = jnp.dot(place, comb, preferred_element_type=F32)[0:1].astype(jnp.int32)
        code = digits(columns[...], to_column(counts[...].astype(F32), blocks))
        codes[...] = jnp.concatenate(code, axis=0).astype(BF16)

    def pack_round(k, h):
        shape = (slots * GROUP, GROUP * blocks)
        at = plane_of(k) * slots + jnp.right_shift(iota(shape, 0), 4)
        hit = (place == at) & (jnp.bitwise_and(iota(shape, 0), GROUP - 1) == iota(shape, 1) // blocks)
        pick = jnp.where(hit, 1.0, 0.0).astype(BF16)
        lo, size = parts[h]
        span = GROUP * blocks

        def put(first, values):
            for t in range(slots):
                part = values[t * GROUP : (t + 1) * GROUP].astype(BF16)
                sent[k, t // CAP, t % CAP, pl.ds(first, GROUP), :] = part

        pairs = (min(lo + size, height - GROUP) - lo) // (2 * GROUP)

        @pl.loop(0, pairs)
        def _(p):
            first = pl.multiple_of(lo + p * 2 * GROUP, GROUP)
            start = pl.multiple_of(first * blocks, span)
            both = jnp.concatenate([obs[pl.ds(start, span), :], obs[pl.ds(start + span, span), :]], axis=1)
            values = jnp.dot(pick, both, preferred_element_type=F32)
            put(first, values[:, :LANES])
            put(pl.multiple_of(first + GROUP, GROUP), values[:, LANES:])

        if lo + size == height:
            last = jnp.concatenate([obs[(height - GROUP) * blocks :, :], codes[...]], axis=0)
            put(height - GROUP, jnp.dot(pick, last, preferred_element_type=F32))

    def send_round(k, h):
        if not packed:
            pack_round(k, h)

        @pl.loop(1, n_lon)
        def _(i):
            block_copy(k, h, i).start()

        own_copy(k, h).start()

    if not packed:
        obs_load.wait()
    for h in range(len(parts)):
        send_round(0, h)
        if h == 0:
            send_bands(0)

    for a, grid in ((1, coef), (0, field)):
        @pl.loop(0, rows)
        def _(r):
            for j in range(chunks):
                turned = jnp.transpose(raw[a, pl.ds(j * step_rows + r, LANES, stride=rows), :])
                grid[j, STEPS + r, EDGE : EDGE + width, :] = turned

        @pl.loop(0, rows // 2)
        def _(p):
            for j in range(chunks):
                pair = [STEPS + 2 * p + q for q in range(2)]
                left = [grid[j, r, EDGE : 2 * EDGE, :] for r in pair]
                right = [grid[j, r, width : width + EDGE, :] for r in pair]
                tile_f[0, j, p] = jnp.where(sub < STEPS, left[0], pltpu.roll(left[1], STEPS, 0))
                tile_f[1, j, p] = jnp.where(sub < STEPS, pltpu.roll(right[0], STEPS, 0), right[1])

        tile_out[a] = tile_f[...].reshape(2, chunks, rows * STEPS, LANES).astype(BF16)
        for k in range(len(SIDES)):
            only(-SIDES[k][0], lambda: tile_copy(a, k).start())

    for k in range(1, n_lat):
        for h in range(len(parts)):
            send_round(k, h)

    small_loads[0].wait()
    matrix = jac_in[...].astype(F32)
    matrix = jnp.concatenate([matrix, jnp.zeros((height - comps, planes), F32)], axis=0)
    if chunks * LANES > planes:
        matrix = jnp.concatenate([matrix, jnp.zeros((height, chunks * LANES - planes), F32)], axis=1)
    jac[...] = matrix.astype(BF16)
    scale[...] = jnp.broadcast_to(to_column(weight_in[...].reshape(1, comps), height), scale.shape)

    def pad_line(h):
        return comps - parts[h][0]

    def lanes(n):
        return pl.ds(pl.multiple_of(n * TILE, TILE), TILE)

    def reduce_peers(k, h, start, stop):
        lo, size = parts[h]

        @pl.loop(max(start, 1), stop)
        def _(i):
            block_copy(k, h, i).wait_recv()

        base = height - GROUP
        first = comps - base
        heads = [recv[k, i, c, base:height, :].astype(F32) for i in range(start, stop) for c in range(CAP)]
        code = jnp.concatenate(
            [(x[first + 1 : first + 2] - 1.0) * 32.0 + x[first + 2 : first + 3] for x in heads], axis=1
        ).astype(jnp.int32)

        @pl.loop(0, cells // TILE)
        def _(n):
            values = jnp.concatenate(
                [recv[k, i, c, lo : lo + size, :] for i in range(start, stop) for c in range(CAP)], axis=1
            )
            hot = jnp.where(iota((TILE, code.shape[1]), 0) == code - n * TILE, 1.0, 0.0).astype(BF16)
            part = lax.dot_general(values, hot, (((1,), (1,)), ((), ())), preferred_element_type=F32)
            target = sums.at[lo : lo + size, lanes(n)]
            if k < n_lat - 1:
                target = ring.at[k % 2, lo : lo + size, lanes(n)]
            target[...] = part if start == 0 else target[...] + part
            if k == n_lat - 1 and h == 0:
                line = pad_line(h)
                number[:, lanes(n)] = jnp.broadcast_to(part[line : line + 1], (8, TILE))

    def reduce(k, h, groups=1):
        own_copy(k, h).wait()
        for g in range(groups):
            peers = n_lon // groups
            reduce_peers(k, h, g * peers, (g + 1) * peers)
        if k < n_lat - 1:
            pl.when(jnp.logical_not(has(-1) & has(1)))(lambda: emit(k, h, False))

    def emit(k, h, joined):
        lo, size = parts[h]
        o = plane_of(k)
        if joined:
            part_copy(k, h, o, lat).wait_recv()

        @pl.loop(0, cells // TILE)
        def _(n):
            value = ring[k % 2, lo : lo + size, lanes(n)]
            if h == 0:
                line = pad_line(h)
                count = value[line : line + 1]
            if joined:
                more = part_in[o, lo : lo + size, lanes(n)].astype(F32)
                value = value + more
                if h == 0:
                    count = count + more[line : line + 1] + more[line + 1 : line + 2] * COUNT_BASE
            if h == 0:
                high = jnp.floor(count * (1.0 / COUNT_BASE))
                at = iota(value.shape, 0)
                value = jnp.where(at == line, count - high * COUNT_BASE, jnp.where(at == line + 1, high, value))
            part_out[k, lo : lo + size, lanes(n)] = value.astype(BF16)

        part_sent(k, h).start()

    def join(k, h):
        pl.when(has(-1) & has(1))(lambda: emit(k, h, True))

    def fill_rows(a, grid):
        def band(s):
            first = (rows + STEPS) * s

            def arrived():
                band_copy(a, s).wait_recv()
                band_f[0 : area // 2, :] = band_in[a, s].astype(F32)

                @pl.loop(0, STEPS)
                def _(r):
                    for j in range(chunks):
                        piece = band_f[pl.ds(j * STEPS * LANES + r, LANES, stride=STEPS), :]
                        grid[j, first + r, EDGE : EDGE + width, :] = jnp.transpose(piece)

            def closed():
                for r in range(STEPS):
                    for j in range(chunks):
                        grid[j, first + r] = jnp.zeros((wide, LANES), F32)

            pl.when(has(2 * s - 1))(arrived)
            pl.when(jnp.logical_not(has(2 * s - 1)))(closed)

        for s in range(2):
            band(s)

    def put_sides(grid, j, p, west, east_):
        pair = (
            jnp.where(sub < STEPS, east_, pltpu.roll(west, STEPS, 0)),
            jnp.where(sub < STEPS, pltpu.roll(east_, STEPS, 0), west),
        )
        for q in range(2):
            grid[j, 2 * p + q, 0:EDGE, :] = pair[q]
            grid[j, 2 * p + q, EDGE + width :, :] = pair[q]

    def fill_columns(a, grid):
        def sides(k, place, source_row, count):
            for side in (k, k + 1):
                tile_copy(a, side).wait_recv()
            span = slice(source_row * STEPS, (source_row + count) * STEPS)
            west, east_ = (
                tile_in[a, side, :, span, :].astype(F32).reshape(chunks, count // 2, EDGE, LANES)
                for side in (k, k + 1)
            )
            for j in range(chunks):
                for p in range(count // 2):
                    put_sides(grid, j, place // 2 + p, west[j, p], east_[j, p])

        sides(0, STEPS, 0, rows)
        only(-1, lambda: sides(2, 0, rows - STEPS, STEPS))
        only(1, lambda: sides(4, STEPS + rows, 0, STEPS))

    def spread(j, finish=None):
        for step in range(STEPS):
            first, last = step + 1, extent - 1 - step
            above = coef[j, first - 1] * (field[j, first] - field[j, first - 1])

            def line(r, above):
                here = field[j, r]
                down = coef[j, r] * (field[j, r + 1] - here)
                along = east[j, r] * (pltpu.roll(here, wide - 1, 0) - here)
                result = here + (down - above) + (along - pltpu.roll(along, 1, 0))
                if finish is not None and step == STEPS - 1:
                    finish(r - STEPS, result[EDGE : EDGE + width])
                else:
                    field[j, r] = result
                return down

            lax.fori_loop(first, last, line, above, unroll=2)

    def take_kappa():
        if chunks * LANES > planes:
            band_f[area // 2 :, :] = jnp.zeros((chunks * LANES * STEPS - area // 2, width), F32)
        fill_rows(1, coef)

    def take_control():
        fill_rows(0, field)

    def make_products():
        fill_columns(1, coef)

        @pl.loop(0, chunks)
        def _(j):
            @pl.loop(0, extent - 1)
            def _(r):
                here = coef[j, r]
                east[j, r] = here * pltpu.roll(here, wide - 1, 0)
                coef[j, r] = here * coef[j, r + 1]

    def make_state():
        fill_columns(0, field)
        pl.loop(0, chunks)(spread)

    def make_model():
        @pl.loop(0, rows)
        def _(r):
            state = jnp.concatenate(
                [field[j, STEPS + r, EDGE : EDGE + width, :].astype(BF16) for j in range(chunks)], axis=1
            )
            model[:, pl.ds(pl.multiple_of(r * width, width), width)] = lax.dot_general(
                jac[...], state, (((1,), (1,)), ((), ())), preferred_element_type=F32
            )

    stages = {1: [make_products, take_control], 3: [make_state, make_model]}
    take_kappa()
    for k in range(n_lat - 1):
        for h in range(len(parts)):
            reduce(k, h)
            if k > 0:
                join(k - 1, h)
            if k == n_lat - 2:
                join(k, h)
            for stage in stages.get(k * len(parts) + h, []):
                stage()

    for s, ref in enumerate((total_north, total_south)):
        def blank():
            ref[...] = jnp.zeros(ref.shape, BF16)
            side_in[2 + 2 * s] = jnp.zeros(side_in.shape[1:], BF16)
            side_in[3 + 2 * s] = jnp.zeros(side_in.shape[1:], BF16)

        pl.when(jnp.logical_not(has(2 * s - 1)))(blank)

    def add_part(slot, h):
        lo, size = parts[h]
        part_copy(0, h, slot, lat).wait_recv()

        @pl.loop(0, cells // TILE)
        def _(n):
            more = part_in[slot, lo : lo + size, lanes(n)].astype(F32)
            sums[lo : lo + size, lanes(n)] = sums[lo : lo + size, lanes(n)] + more
            if h == 0:
                line = pad_line(h)
                count = more[line : line + 1] + more[line + 1 : line + 2] * COUNT_BASE
                number[:, lanes(n)] = number[:, lanes(n)] + count

    for h, (lo, size) in enumerate(parts):
        reduce(n_lat - 1, h, groups=2 if h == len(parts) - 1 else 1)
        only(-1, lambda: add_part(lat, h))
        only(1, lambda: add_part(n_lat, h))
        for r in range(rows):
            at = slice(r * width, (r + 1) * width)
            value = number[0:1, at] * model[lo : lo + size, at] - sums[lo : lo + size, at]
            total[lo : lo + size, at] = (value * scale[lo : lo + size, :]).astype(BF16)
        for s in range(2):
            only(1 - 2 * s, lambda: row_copy(h, s).start())

    ends = (2 * rows * STEPS, cells)
    line = iota(ends, 0)
    spot = lax.rem(line, rows * STEPS)
    spot = (spot // STEPS) * width + lax.rem(spot, STEPS)
    spot = spot + jnp.where(line < rows * STEPS, 0, width - STEPS)
    ends = jnp.where(iota(ends, 1) == spot, 1.0, 0.0).astype(BF16)
    side_out[...] = lax.dot_general(
        ends, total[...], (((1,), (1,)), ((), ())), preferred_element_type=F32
    ).reshape(2, rows * STEPS, height).astype(BF16)
    for k in range(len(SIDES)):
        only(-SIDES[k][0], lambda: side_copy(k).start())

    def put_row(values, r):
        result = lax.dot_general(values, jac[...], (((0,), (0,)), ((), ())), preferred_element_type=F32)
        for j in range(chunks):
            field[j, r, EDGE : EDGE + width, :] = result[:, j * LANES : (j + 1) * LANES]

    @pl.loop(0, rows)
    def _(r):
        put_row(total[:, pl.ds(pl.multiple_of(r * width, width), width)], STEPS + r)

    for k in range(len(SIDES)):
        only(SIDES[k][0], lambda: side_copy(k).wait_recv())

    side = jnp.concatenate(
        [
            side_in[k, lines, :]
            for ks in ((2, 0, 4), (3, 1, 5))
            for k, lines in zip(ks, (slice((rows - STEPS) * STEPS, rows * STEPS), slice(None), slice(0, STEPS * STEPS)))
        ],
        axis=0,
    )
    result = jnp.dot(side, jac[...], preferred_element_type=F32)
    for j in range(chunks):
        for p in range(extent // 2):
            west, east_ = (
                result[first + p * EDGE : first + (p + 1) * EDGE, j * LANES : (j + 1) * LANES]
                for first in (0, extent * STEPS)
            )
            put_sides(field, j, p, west, east_)

    for h in range(len(parts)):
        for s in range(2):
            only(2 * s - 1, lambda: row_copy(h, s).wait_recv())

    @pl.loop(0, STEPS)
    def _(r):
        at = pl.ds(pl.multiple_of(r * width, width), width)
        put_row(total_north[:, at], r)
        put_row(total_south[:, at], STEPS + rows + r)

    stores = []
    for j in range(chunks):
        def add_row(r, values):
            at = pl.ds(j * step_rows + r, LANES, stride=rows)
            raw[0, at, :] = raw[0, at, :] + jnp.transpose(values)

        spread(j, add_row)
        span = pl.ds(j * step_rows, min(step_rows, area - j * step_rows))
        stores.append(pltpu.make_async_copy(raw.at[0, span, :], out.at[span, :], store_sem.at[j]))
        stores[-1].start()

    for k in range(n_lat):
        for h in range(len(parts)):
            @pl.loop(1, n_lon)
            def _(i):
                block_copy(k, h, i).wait_send()
    for h in range(len(parts)):
        for k in range(n_lat - 1):
            part_sent(k, h).wait_send()
        for s in range(2):
            only(1 - 2 * s, lambda: row_copy(h, s).wait_send())
    for k in range(len(SIDES)):
        only(-SIDES[k][0], lambda: side_copy(k).wait_send())
    for a in range(2):
        for s in range(2):
            only(1 - 2 * s, lambda: band_copy(a, s).wait_send())
        for k in range(len(SIDES)):
            only(-SIDES[k][0], lambda: tile_copy(a, k).wait_send())
    for store in stores:
        store.wait()


def per_device(control, kappa, pc_obs, owner, columns, counts, jacobian, obs_weight):
    n_lat, n_lon = lax.axis_size("lat"), lax.axis_size("lon")
    fields, levels, rows, width = control.shape
    blocks, soundings, comps = pc_obs.shape
    planes = fields * levels
    cells = rows * width
    height = comps + TAIL
    chunks = -(-planes // LANES)
    extent, wide = rows + 2 * STEPS, width + 2 * EDGE
    half = height // 96 * 32
    parts = ((half, height - half), (0, half))
    obs = jnp.transpose(pc_obs, (2, 0, 1))
    slots_shape = (n_lat, n_lon, CAP, height, soundings)
    packed = blocks * GROUP > 1024
    if packed:
        source = pack(obs, owner, columns, counts, n_lat * n_lon, height).reshape(slots_shape)
        extra = []
    else:
        source = obs.reshape(comps * blocks, soundings)
        extra = [
            pltpu.VMEM(slots_shape, BF16),
            pltpu.VMEM(source.shape, BF16),
            pltpu.VMEM((TAIL * blocks, soundings), BF16),
        ]
    small = (jnp.transpose(jacobian), obs_weight, owner.reshape(1, blocks), counts[None, :], columns)
    n_parts, n_sides = len(parts), len(SIDES)
    grid = pltpu.VMEM((chunks, extent, wide, LANES), F32)
    dma = pltpu.SemaphoreType.DMA
    result = pl.pallas_call(
        functools.partial(main_kernel, n_lat, n_lon, planes, parts, packed),
        out_shape=jax.ShapeDtypeStruct((planes * rows, width), F32),
        in_specs=[pl.BlockSpec(memory_space=pl.ANY)] * (3 + len(small)),
        out_specs=pl.BlockSpec(memory_space=pl.ANY),
        scratch_shapes=[pltpu.VMEM(x.shape, x.dtype) for x in small]
        + extra
        + [
            pltpu.VMEM(slots_shape, BF16),
            pltpu.VMEM((2, height, cells), F32),
            pltpu.VMEM((n_lat - 1, height, cells), BF16),
            pltpu.VMEM((n_lat + 1, height, cells), BF16),
            pltpu.VMEM((height, cells), F32),
            pltpu.VMEM((8, cells), F32),
            pltpu.VMEM((height, cells), F32),
            pltpu.VMEM((height, chunks * LANES), BF16),
            pltpu.VMEM((height, LANES), F32),
            grid, grid, grid,
            pltpu.VMEM((2, chunks * LANES * rows, width), F32),
            pltpu.VMEM((2, 2, planes * STEPS, width), BF16),
            pltpu.VMEM((2, 2, planes * STEPS, width), BF16),
            pltpu.VMEM((chunks * LANES * STEPS, width), F32),
            pltpu.VMEM((2, chunks, rows // 2, EDGE, LANES), F32),
            pltpu.VMEM((2, 2, chunks, rows * STEPS, LANES), BF16),
            pltpu.VMEM((2, n_sides, chunks, rows * STEPS, LANES), BF16),
            pltpu.VMEM((height, cells), BF16),
            pltpu.VMEM((height, STEPS * width), BF16),
            pltpu.VMEM((height, STEPS * width), BF16),
            pltpu.VMEM((2, rows * STEPS, height), BF16),
            pltpu.VMEM((n_sides, rows * STEPS, height), BF16),
            dma((3 + len(small),)), dma((n_lat, n_parts)),
            dma((n_lat, n_parts, n_lon)), dma((n_lat, n_parts, n_lon)),
            dma((n_lat, n_parts)), dma((n_lat + 1, n_parts)),
            dma((2, 2)), dma((2, 2)), dma((2, n_sides)), dma((2, n_sides)),
            dma((n_parts, 2)), dma((n_parts, 2)), dma((n_sides,)), dma((n_sides,)),
            dma((chunks,)),
        ],
        compiler_params=pltpu.CompilerParams(
            vmem_limit_bytes=62 * 2**20, has_side_effects=True, collective_id=0
        ),
    )(
        source, control.reshape(planes * rows, width), kappa.reshape(planes * rows, width),
        *small,
    )
    return result.reshape(control.shape)


def solution(mesh):
    placed = (
        P(None, None, "lat", "lon"),
        P(None, None, "lat", "lon"),
        P(("lat", "lon"), None, None),
        P(("lat", "lon"), None),
        P(("lat", "lon"), None),
        P(("lat", "lon")),
        P(),
        P(),
    )
    return jax.shard_map(
        per_device,
        mesh=mesh,
        in_specs=placed,
        out_specs=P(None, None, "lat", "lon"),
        check_vma=False,
    )
```

```python
import functools

import jax
import jax.numpy as jnp
from jax import lax
from jax.experimental import pallas as pl
from jax.experimental.pallas import tpu as pltpu
from jax.sharding import PartitionSpec as P

CAP = 2
STEPS = 4
LANES = 128
GROUP = 16
EDGE = 8
TAIL = 4
COUNT_BASE = 64
TILE = 256
MESH = pl.DeviceIdType.MESH
F32 = jnp.float32
BF16 = jnp.bfloat16
SIDES = ((0, -1), (0, 1), (-1, -1), (-1, 1), (1, -1), (1, 1))


def iota(shape, dim):
    return lax.broadcasted_iota(jnp.int32, shape, dim)


def to_column(row, size):
    shape = (size, row.shape[1])
    return jnp.sum(jnp.where(iota(shape, 0) == iota(shape, 1), row, 0.0), axis=1, keepdims=True)


def digits(columns, counts):
    low = jnp.bitwise_and(columns, 31)
    valid = iota(columns.shape, 1).astype(F32) < counts
    high = jnp.where(valid, jnp.right_shift(columns - low, 5) + 1, 0)
    zero = jnp.zeros(columns.shape, F32)
    return [zero + 1.0, high.astype(F32), low.astype(F32), zero]


def pack_kernel(group, owner_ref, obs_ref, columns_ref, counts_ref, out_ref, wide, source):
    blocks = columns_ref.shape[0]
    comps = obs_ref.shape[0]
    height = out_ref.shape[1]
    slots = source.shape[0]

    @pl.when(pl.program_id(0) == 0)
    def _():
        @pl.loop(0, slots)
        def _(t):
            source[t] = -1

        @pl.loop(0, blocks)
        def _(b):
            first = owner_ref[b] * CAP
            source[jnp.where(source[first] < 0, first, first + 1)] = b

        @pl.loop(0, comps, unroll=4)
        def _(c):
            wide[pl.ds(pl.multiple_of(c * blocks, blocks), blocks), :] = obs_ref[c].astype(F32)

        for k, row in enumerate(digits(columns_ref[...], to_column(counts_ref[...].astype(F32), blocks))):
            wide[(comps + k) * blocks : (comps + k + 1) * blocks, :] = row

    for g in range(group):
        block = source[pl.program_id(0) * group + g]
        rows = wide[pl.ds(jnp.maximum(block, 0), height, stride=blocks), :]
        out_ref[g] = jnp.where(block < 0, 0.0, rows).astype(BF16)


def pack(obs, owner, columns, counts, peers, height):
    comps, blocks, soundings = obs.shape
    slots = peers * CAP
    group = 8
    return pl.pallas_call(
        functools.partial(pack_kernel, group),
        out_shape=jax.ShapeDtypeStruct((slots, height, soundings), BF16),
        grid_spec=pltpu.PrefetchScalarGridSpec(
            num_scalar_prefetch=1,
            grid=(slots // group,),
            in_specs=[
                pl.BlockSpec((comps, blocks, soundings), lambda i, s: (0, 0, 0)),
                pl.BlockSpec((blocks, soundings), lambda i, s: (0, 0)),
                pl.BlockSpec((1, blocks), lambda i, s: (0, 0)),
            ],
            out_specs=pl.BlockSpec((group, height, soundings), lambda i, s: (i, 0, 0)),
            scratch_shapes=[
                pltpu.VMEM((height * blocks, soundings), F32),
                pltpu.SMEM((slots,), jnp.int32),
            ],
        ),
        compiler_params=pltpu.CompilerParams(vmem_limit_bytes=56 * 2**20),
    )(owner[:, 0], obs, columns, counts[None, :])


def main_kernel(n_lat, n_lon, planes, parts, packed, *refs):
    source, control, kappa, *small_in, out = refs[:9]
    small, refs = refs[9:14], refs[14:]
    jac_in, weight_in, owner, counts, columns = small
    sent, obs, codes = (source, None, None) if packed else refs[:3]
    (
        recv, ring, part_out, part_in, sums, number, model, jac, scale,
        field, coef, east, raw, band_out, band_in, band_f, tile_f, tile_out, tile_in,
        total, total_north, total_south, side_out, side_in,
        load_sem, own_sem, blk_send, blk_recv, part_send, part_recv,
        band_send, band_recv, tile_send, tile_recv, row_send, row_recv, side_send, side_recv, store_sem,
    ) = refs if packed else refs[3:]
    lat, lon = lax.axis_index("lat"), lax.axis_index("lon")
    height, cells = sums.shape
    comps = jac_in.shape[0]
    chunks, extent, wide, _ = field.shape
    rows = extent - 2 * STEPS
    width = wide - 2 * EDGE
    area = planes * rows
    step_rows = LANES * rows
    slots = n_lon * CAP

    def plane_of(k):
        mirrored = lat >= n_lat - n_lat // 2
        z = jnp.where(mirrored, n_lat - 1 - lat, lat)
        o = jnp.where(k < n_lat - 1 - z, n_lat - 1 - k, k - (n_lat - 1 - z))
        return jnp.where(mirrored, n_lat - 1 - o, o)

    def remote(src, dst, send, recv_, to):
        return pltpu.make_async_remote_copy(
            src_ref=src, dst_ref=dst, send_sem=send, recv_sem=recv_, device_id=to, device_id_type=MESH
        )

    def around(step):
        return lax.rem(lon + step + n_lon, n_lon)

    def has(step):
        return (lat + step >= 0) & (lat + step < n_lat)

    def only(step, act):
        if step == 0:
            act()
        else:
            pl.when(has(step))(act)

    def slot_of(k):
        return plane_of(k) if packed else k

    def block_copy(k, h, i):
        lo, size = parts[h]
        return remote(
            sent.at[slot_of(k), around(i), :, pl.ds(lo, size), :], recv.at[k, i, :, pl.ds(lo, size), :],
            blk_send.at[k, h, i], blk_recv.at[k, h, i], (lat, around(i)),
        )

    def own_copy(k, h):
        lo, size = parts[h]
        return pltpu.make_async_copy(
            sent.at[slot_of(k), lon, :, pl.ds(lo, size), :],
            recv.at[k, 0, :, pl.ds(lo, size), :], own_sem.at[k, h],
        )

    def part_copy(k, h, slot, to):
        lo, size = parts[h]
        return remote(
            part_out.at[k, pl.ds(lo, size), :], part_in.at[slot, pl.ds(lo, size), :],
            part_send.at[k, h], part_recv.at[slot, h], (to, lon),
        )

    def part_sent(k, h):
        o = plane_of(k)
        north = o < lat
        slot = jnp.where(north & (o == lat - 1), n_lat, o)
        return part_copy(k, h, slot, jnp.where(north, lat - 1, lat + 1))

    def band_copy(a, s):
        return remote(
            band_out.at[a, 1 - s], band_in.at[a, s],
            band_send.at[a, s], band_recv.at[a, s], (lat + (1 - 2 * s), lon),
        )

    def peer(k):
        return (lat - SIDES[k][0], around(-SIDES[k][1]))

    def side_span(k):
        step = SIDES[k][0]
        return pl.ds((rows - STEPS) * STEPS if step < 0 else 0, (STEPS if step else rows) * STEPS)

    def side_of(k):
        return (1 - SIDES[k][1]) // 2

    def tile_copy(a, k):
        span = side_span(k)
        return remote(
            tile_out.at[a, side_of(k), :, span, :], tile_in.at[a, k, :, span, :],
            tile_send.at[a, k], tile_recv.at[a, k], peer(k),
        )

    def row_copy(h, s):
        lo, size = parts[h]
        span = STEPS * width
        return remote(
            total.at[pl.ds(lo, size), pl.ds((1 - s) * (rows * width - span), span)],
            (total_north if s == 0 else total_south).at[pl.ds(lo, size), :],
            row_send.at[h, s], row_recv.at[h, s], (lat + (1 - 2 * s), lon),
        )

    def side_copy(k):
        span = side_span(k)
        return remote(
            side_out.at[side_of(k), span, :], side_in.at[k, span, :], side_send.at[k], side_recv.at[k], peer(k)
        )

    loads = [
        pltpu.make_async_copy(ref, raw.at[a, pl.ds(0, area), :], load_sem.at[a])
        for a, ref in enumerate((control, kappa))
    ]
    small_loads = [
        pltpu.make_async_copy(ref, to, load_sem.at[3 + n]) for n, (ref, to) in enumerate(zip(small_in, small))
    ]
    for load in small_loads[1:]:
        load.start()
    if not packed:
        obs_load = pltpu.make_async_copy(source, obs, load_sem.at[2])
        obs_load.start()
    loads[1].start()
    loads[0].start()
    small_loads[0].start()

    barrier = pltpu.get_barrier_semaphore()

    @pl.loop(1, n_lon)
    def _(i):
        pl.semaphore_signal(barrier, inc=1, device_id=(lat, around(i)), device_id_type=MESH)

    for step in (-1, 1):
        def greet():
            for side in (-1, 0, 1):
                pl.semaphore_signal(
                    barrier, inc=1, device_id=(lat + step, around(side)), device_id_type=MESH
                )

        only(step, greet)

    sub = iota((EDGE, LANES), 0)

    def send_bands(a):
        loads[a].wait()
        if chunks * step_rows > area:
            raw[a, area:, :] = jnp.zeros((chunks * step_rows - area, width), F32)
        pairs = raw[a, 0:area, :].reshape(planes // 2, 2, rows, width)
        even, odd = pairs[:, 0], pairs[:, 1]
        upper = iota(even.shape, 1) < STEPS
        band_out[a, 0] = jnp.where(upper, even, pltpu.roll(odd, STEPS, 1)).reshape(area // 2, width).astype(BF16)
        band_out[a, 1] = jnp.where(upper, pltpu.roll(even, STEPS, 1), odd).reshape(area // 2, width).astype(BF16)
        for s in range(2):
            only(1 - 2 * s, lambda: band_copy(a, s).start())

    for load in small_loads[1:]:
        load.wait()

    if not packed:
        blocks = columns.shape[0]
        names = owner[...].astype(F32)
        square = (blocks, blocks)
        before = (to_column(names, blocks) == names) & (iota(square, 0) < iota(square, 1))
        place = names * CAP + jnp.sum(jnp.where(before, 1.0, 0.0), axis=0, keepdims=True)
        lined = (blocks, GROUP * blocks)
        comb = jnp.where(lax.rem(iota(lined, 1), blocks) == iota(lined, 0), 1.0, 0.0).astype(BF16)
        place = jnp.broadcast_to(place, (16, blocks)).astype(BF16)
        place = jnp.dot(place, comb, preferred_element_type=F32)[0:1].astype(jnp.int32)
        code = digits(columns[...], to_column(counts[...].astype(F32), blocks))
        codes[...] = jnp.concatenate(code, axis=0).astype(BF16)

    def pack_round(k, h):
        shape = (slots * GROUP, GROUP * blocks)
        at = plane_of(k) * slots + jnp.right_shift(iota(shape, 0), 4)
        hit = (place == at) & (jnp.bitwise_and(iota(shape, 0), GROUP - 1) == iota(shape, 1) // blocks)
        pick = jnp.where(hit, 1.0, 0.0).astype(BF16)
        lo, size = parts[h]
        span = GROUP * blocks

        def put(first, values):
            for t in range(slots):
                part = values[t * GROUP : (t + 1) * GROUP].astype(BF16)
                sent[k, t // CAP, t % CAP, pl.ds(first, GROUP), :] = part

        pairs = (min(lo + size, height - GROUP) - lo) // (2 * GROUP)

        @pl.loop(0, pairs)
        def _(p):
            first = pl.multiple_of(lo + p * 2 * GROUP, GROUP)
            start = pl.multiple_of(first * blocks, span)
            both = jnp.concatenate([obs[pl.ds(start, span), :], obs[pl.ds(start + span, span), :]], axis=1)
            values = jnp.dot(pick, both, preferred_element_type=F32)
            put(first, values[:, :LANES])
            put(pl.multiple_of(first + GROUP, GROUP), values[:, LANES:])

        if lo + size == height:
            last = jnp.concatenate([obs[(height - GROUP) * blocks :, :], codes[...]], axis=0)
            put(height - GROUP, jnp.dot(pick, last, preferred_element_type=F32))

    def send_round(k, h):
        if not packed:
            pack_round(k, h)
        if k == 0 and h == 0:
            pl.semaphore_wait(
                barrier, n_lon - 1 + 3 * (has(-1).astype(jnp.int32) + has(1).astype(jnp.int32))
            )

        @pl.loop(1, n_lon)
        def _(i):
            block_copy(k, h, i).start()

        own_copy(k, h).start()

    if not packed:
        obs_load.wait()
    for h in range(len(parts)):
        send_round(0, h)
        if h == 0:
            send_bands(1)
            send_bands(0)

    for a, grid in ((1, coef), (0, field)):
        @pl.loop(0, rows)
        def _(r):
            for j in range(chunks):
                turned = jnp.transpose(raw[a, pl.ds(j * step_rows + r, LANES, stride=rows), :])
                grid[j, STEPS + r, EDGE : EDGE + width, :] = turned

        @pl.loop(0, rows // 2)
        def _(p):
            for j in range(chunks):
                pair = [STEPS + 2 * p + q for q in range(2)]
                left = [grid[j, r, EDGE : 2 * EDGE, :] for r in pair]
                right = [grid[j, r, width : width + EDGE, :] for r in pair]
                tile_f[0, j, p] = jnp.where(sub < STEPS, left[0], pltpu.roll(left[1], STEPS, 0))
                tile_f[1, j, p] = jnp.where(sub < STEPS, pltpu.roll(right[0], STEPS, 0), right[1])

        tile_out[a] = tile_f[...].reshape(2, chunks, rows * STEPS, LANES).astype(BF16)
        for k in range(len(SIDES)):
            only(-SIDES[k][0], lambda: tile_copy(a, k).start())

    for k in range(1, n_lat):
        for h in range(len(parts)):
            send_round(k, h)

    small_loads[0].wait()
    matrix = jac_in[...].astype(F32)
    matrix = jnp.concatenate([matrix, jnp.zeros((height - comps, planes), F32)], axis=0)
    if chunks * LANES > planes:
        matrix = jnp.concatenate([matrix, jnp.zeros((height, chunks * LANES - planes), F32)], axis=1)
    jac[...] = matrix.astype(BF16)
    scale[...] = jnp.broadcast_to(to_column(weight_in[...].reshape(1, comps), height), scale.shape)

    def pad_line(h):
        return comps - parts[h][0]

    def lanes(n):
        return pl.ds(pl.multiple_of(n * TILE, TILE), TILE)

    def reduce_peers(k, h, start, stop):
        lo, size = parts[h]

        @pl.loop(max(start, 1), stop)
        def _(i):
            block_copy(k, h, i).wait_recv()

        base = height - GROUP
        first = comps - base
        heads = [recv[k, i, c, base:height, :].astype(F32) for i in range(start, stop) for c in range(CAP)]
        code = jnp.concatenate(
            [(x[first + 1 : first + 2] - 1.0) * 32.0 + x[first + 2 : first + 3] for x in heads], axis=1
        ).astype(jnp.int32)

        @pl.loop(0, cells // TILE)
        def _(n):
            values = jnp.concatenate(
                [recv[k, i, c, lo : lo + size, :] for i in range(start, stop) for c in range(CAP)], axis=1
            )
            hot = jnp.where(iota((TILE, code.shape[1]), 0) == code - n * TILE, 1.0, 0.0).astype(BF16)
            part = lax.dot_general(values, hot, (((1,), (1,)), ((), ())), preferred_element_type=F32)
            target = sums.at[lo : lo + size, lanes(n)]
            if k < n_lat - 1:
                target = ring.at[k % 2, lo : lo + size, lanes(n)]
            target[...] = part if start == 0 else target[...] + part
            if k == n_lat - 1 and h == 0:
                line = pad_line(h)
                number[:, lanes(n)] = jnp.broadcast_to(part[line : line + 1], (8, TILE))

    def reduce(k, h, groups=1):
        own_copy(k, h).wait()
        for g in range(groups):
            peers = n_lon // groups
            reduce_peers(k, h, g * peers, (g + 1) * peers)
        if k < n_lat - 1:
            pl.when(jnp.logical_not(has(-1) & has(1)))(lambda: emit(k, h, False))

    def emit(k, h, joined):
        lo, size = parts[h]
        o = plane_of(k)
        if joined:
            part_copy(k, h, o, lat).wait_recv()

        @pl.loop(0, cells // TILE)
        def _(n):
            value = ring[k % 2, lo : lo + size, lanes(n)]
            if h == 0:
                line = pad_line(h)
                count = value[line : line + 1]
            if joined:
                more = part_in[o, lo : lo + size, lanes(n)].astype(F32)
                value = value + more
                if h == 0:
                    count = count + more[line : line + 1] + more[line + 1 : line + 2] * COUNT_BASE
            if h == 0:
                high = jnp.floor(count * (1.0 / COUNT_BASE))
                at = iota(value.shape, 0)
                value = jnp.where(at == line, count - high * COUNT_BASE, jnp.where(at == line + 1, high, value))
            part_out[k, lo : lo + size, lanes(n)] = value.astype(BF16)

        part_sent(k, h).start()

    def join(k, h):
        pl.when(has(-1) & has(1))(lambda: emit(k, h, True))

    def fill_rows(a, grid):
        def band(s):
            first = (rows + STEPS) * s

            def arrived():
                band_copy(a, s).wait_recv()
                band_f[0 : area // 2, :] = band_in[a, s].astype(F32)

                @pl.loop(0, STEPS)
                def _(r):
                    for j in range(chunks):
                        piece = band_f[pl.ds(j * STEPS * LANES + r, LANES, stride=STEPS), :]
                        grid[j, first + r, EDGE : EDGE + width, :] = jnp.transpose(piece)

            def closed():
                for r in range(STEPS):
                    for j in range(chunks):
                        grid[j, first + r] = jnp.zeros((wide, LANES), F32)

            pl.when(has(2 * s - 1))(arrived)
            pl.when(jnp.logical_not(has(2 * s - 1)))(closed)

        for s in range(2):
            band(s)

    def put_sides(grid, j, p, west, east_):
        pair = (
            jnp.where(sub < STEPS, east_, pltpu.roll(west, STEPS, 0)),
            jnp.where(sub < STEPS, pltpu.roll(east_, STEPS, 0), west),
        )
        for q in range(2):
            grid[j, 2 * p + q, 0:EDGE, :] = pair[q]
            grid[j, 2 * p + q, EDGE + width :, :] = pair[q]

    def fill_columns(a, grid):
        def sides(k, place, source_row, count):
            for side in (k, k + 1):
                tile_copy(a, side).wait_recv()
            span = slice(source_row * STEPS, (source_row + count) * STEPS)
            west, east_ = (
                tile_in[a, side, :, span, :].astype(F32).reshape(chunks, count // 2, EDGE, LANES)
                for side in (k, k + 1)
            )
            for j in range(chunks):
                for p in range(count // 2):
                    put_sides(grid, j, place // 2 + p, west[j, p], east_[j, p])

        sides(0, STEPS, 0, rows)
        only(-1, lambda: sides(2, 0, rows - STEPS, STEPS))
        only(1, lambda: sides(4, STEPS + rows, 0, STEPS))

    def spread(j, finish=None):
        for step in range(STEPS):
            first, last = step + 1, extent - 1 - step
            above = coef[j, first - 1] * (field[j, first] - field[j, first - 1])

            def line(r, above):
                here = field[j, r]
                down = coef[j, r] * (field[j, r + 1] - here)
                along = east[j, r] * (pltpu.roll(here, wide - 1, 0) - here)
                result = here + (down - above) + (along - pltpu.roll(along, 1, 0))
                if finish is not None and step == STEPS - 1:
                    finish(r - STEPS, result[EDGE : EDGE + width])
                else:
                    field[j, r] = result
                return down

            lax.fori_loop(first, last, line, above, unroll=2)

    def take_kappa():
        if chunks * LANES > planes:
            band_f[area // 2 :, :] = jnp.zeros((chunks * LANES * STEPS - area // 2, width), F32)
        fill_rows(1, coef)

    def take_control():
        fill_rows(0, field)

    def make_products():
        fill_columns(1, coef)

        @pl.loop(0, chunks)
        def _(j):
            @pl.loop(0, extent - 1)
            def _(r):
                here = coef[j, r]
                east[j, r] = here * pltpu.roll(here, wide - 1, 0)
                coef[j, r] = here * coef[j, r + 1]

    def make_state():
        fill_columns(0, field)
        pl.loop(0, chunks)(spread)

    def make_model():
        @pl.loop(0, rows)
        def _(r):
            state = jnp.concatenate(
                [field[j, STEPS + r, EDGE : EDGE + width, :].astype(BF16) for j in range(chunks)], axis=1
            )
            model[:, pl.ds(pl.multiple_of(r * width, width), width)] = lax.dot_general(
                jac[...], state, (((1,), (1,)), ((), ())), preferred_element_type=F32
            )

    stages = {1: [make_products, take_control], 3: [make_state, make_model]}
    take_kappa()
    for k in range(n_lat - 1):
        for h in range(len(parts)):
            reduce(k, h)
            if k > 0:
                join(k - 1, h)
            if k == n_lat - 2:
                join(k, h)
            for stage in stages.get(k * len(parts) + h, []):
                stage()

    for s, ref in enumerate((total_north, total_south)):
        def blank():
            ref[...] = jnp.zeros(ref.shape, BF16)
            side_in[2 + 2 * s] = jnp.zeros(side_in.shape[1:], BF16)
            side_in[3 + 2 * s] = jnp.zeros(side_in.shape[1:], BF16)

        pl.when(jnp.logical_not(has(2 * s - 1)))(blank)

    def add_part(slot, h):
        lo, size = parts[h]
        part_copy(0, h, slot, lat).wait_recv()

        @pl.loop(0, cells // TILE)
        def _(n):
            more = part_in[slot, lo : lo + size, lanes(n)].astype(F32)
            sums[lo : lo + size, lanes(n)] = sums[lo : lo + size, lanes(n)] + more
            if h == 0:
                line = pad_line(h)
                count = more[line : line + 1] + more[line + 1 : line + 2] * COUNT_BASE
                number[:, lanes(n)] = number[:, lanes(n)] + count

    for h, (lo, size) in enumerate(parts):
        reduce(n_lat - 1, h, groups=2 if h == len(parts) - 1 else 1)
        only(-1, lambda: add_part(lat, h))
        only(1, lambda: add_part(n_lat, h))
        for r in range(rows):
            at = slice(r * width, (r + 1) * width)
            value = number[0:1, at] * model[lo : lo + size, at] - sums[lo : lo + size, at]
            total[lo : lo + size, at] = (value * scale[lo : lo + size, :]).astype(BF16)
        for s in range(2):
            only(1 - 2 * s, lambda: row_copy(h, s).start())

    ends = (2 * rows * STEPS, cells)
    line = iota(ends, 0)
    spot = lax.rem(line, rows * STEPS)
    spot = (spot // STEPS) * width + lax.rem(spot, STEPS)
    spot = spot + jnp.where(line < rows * STEPS, 0, width - STEPS)
    ends = jnp.where(iota(ends, 1) == spot, 1.0, 0.0).astype(BF16)
    side_out[...] = lax.dot_general(
        ends, total[...], (((1,), (1,)), ((), ())), preferred_element_type=F32
    ).reshape(2, rows * STEPS, height).astype(BF16)
    for k in range(len(SIDES)):
        only(-SIDES[k][0], lambda: side_copy(k).start())

    def put_row(values, r):
        result = lax.dot_general(values, jac[...], (((0,), (0,)), ((), ())), preferred_element_type=F32)
        for j in range(chunks):
            field[j, r, EDGE : EDGE + width, :] = result[:, j * LANES : (j + 1) * LANES]

    @pl.loop(0, rows)
    def _(r):
        put_row(total[:, pl.ds(pl.multiple_of(r * width, width), width)], STEPS + r)

    for k in range(len(SIDES)):
        only(SIDES[k][0], lambda: side_copy(k).wait_recv())

    side = jnp.concatenate(
        [
            side_in[k, lines, :]
            for ks in ((2, 0, 4), (3, 1, 5))
            for k, lines in zip(ks, (slice((rows - STEPS) * STEPS, rows * STEPS), slice(None), slice(0, STEPS * STEPS)))
        ],
        axis=0,
    )
    result = jnp.dot(side, jac[...], preferred_element_type=F32)
    for j in range(chunks):
        for p in range(extent // 2):
            west, east_ = (
                result[first + p * EDGE : first + (p + 1) * EDGE, j * LANES : (j + 1) * LANES]
                for first in (0, extent * STEPS)
            )
            put_sides(field, j, p, west, east_)

    for h in range(len(parts)):
        for s in range(2):
            only(2 * s - 1, lambda: row_copy(h, s).wait_recv())

    @pl.loop(0, STEPS)
    def _(r):
        at = pl.ds(pl.multiple_of(r * width, width), width)
        put_row(total_north[:, at], r)
        put_row(total_south[:, at], STEPS + rows + r)

    stores = []
    for j in range(chunks):
        def add_row(r, values):
            at = pl.ds(j * step_rows + r, LANES, stride=rows)
            raw[0, at, :] = raw[0, at, :] + jnp.transpose(values)

        spread(j, add_row)
        span = pl.ds(j * step_rows, min(step_rows, area - j * step_rows))
        stores.append(pltpu.make_async_copy(raw.at[0, span, :], out.at[span, :], store_sem.at[j]))
        stores[-1].start()

    for k in range(n_lat):
        for h in range(len(parts)):
            @pl.loop(1, n_lon)
            def _(i):
                block_copy(k, h, i).wait_send()
    for h in range(len(parts)):
        for k in range(n_lat - 1):
            part_sent(k, h).wait_send()
        for s in range(2):
            only(1 - 2 * s, lambda: row_copy(h, s).wait_send())
    for k in range(len(SIDES)):
        only(-SIDES[k][0], lambda: side_copy(k).wait_send())
    for a in range(2):
        for s in range(2):
            only(1 - 2 * s, lambda: band_copy(a, s).wait_send())
        for k in range(len(SIDES)):
            only(-SIDES[k][0], lambda: tile_copy(a, k).wait_send())
    for store in stores:
        store.wait()


def per_device(control, kappa, pc_obs, owner, columns, counts, jacobian, obs_weight):
    n_lat, n_lon = lax.axis_size("lat"), lax.axis_size("lon")
    fields, levels, rows, width = control.shape
    blocks, soundings, comps = pc_obs.shape
    planes = fields * levels
    cells = rows * width
    height = comps + TAIL
    chunks = -(-planes // LANES)
    extent, wide = rows + 2 * STEPS, width + 2 * EDGE
    half = height // 64 * 32
    parts = ((half, height - half), (0, half))
    obs = jnp.transpose(pc_obs, (2, 0, 1))
    slots_shape = (n_lat, n_lon, CAP, height, soundings)
    packed = blocks * GROUP > 1024
    if packed:
        source = pack(obs, owner, columns, counts, n_lat * n_lon, height).reshape(slots_shape)
        extra = []
    else:
        source = obs.reshape(comps * blocks, soundings)
        extra = [
            pltpu.VMEM(slots_shape, BF16),
            pltpu.VMEM(source.shape, BF16),
            pltpu.VMEM((TAIL * blocks, soundings), BF16),
        ]
    small = (jnp.transpose(jacobian), obs_weight, owner.reshape(1, blocks), counts[None, :], columns)
    n_parts, n_sides = len(parts), len(SIDES)
    grid = pltpu.VMEM((chunks, extent, wide, LANES), F32)
    dma = pltpu.SemaphoreType.DMA
    result = pl.pallas_call(
        functools.partial(main_kernel, n_lat, n_lon, planes, parts, packed),
        out_shape=jax.ShapeDtypeStruct((planes * rows, width), F32),
        in_specs=[pl.BlockSpec(memory_space=pl.ANY)] * (3 + len(small)),
        out_specs=pl.BlockSpec(memory_space=pl.ANY),
        scratch_shapes=[pltpu.VMEM(x.shape, x.dtype) for x in small]
        + extra
        + [
            pltpu.VMEM(slots_shape, BF16),
            pltpu.VMEM((2, height, cells), F32),
            pltpu.VMEM((n_lat - 1, height, cells), BF16),
            pltpu.VMEM((n_lat + 1, height, cells), BF16),
            pltpu.VMEM((height, cells), F32),
            pltpu.VMEM((8, cells), F32),
            pltpu.VMEM((height, cells), F32),
            pltpu.VMEM((height, chunks * LANES), BF16),
            pltpu.VMEM((height, LANES), F32),
            grid, grid, grid,
            pltpu.VMEM((2, chunks * LANES * rows, width), F32),
            pltpu.VMEM((2, 2, planes * STEPS, width), BF16),
            pltpu.VMEM((2, 2, planes * STEPS, width), BF16),
            pltpu.VMEM((chunks * LANES * STEPS, width), F32),
            pltpu.VMEM((2, chunks, rows // 2, EDGE, LANES), F32),
            pltpu.VMEM((2, 2, chunks, rows * STEPS, LANES), BF16),
            pltpu.VMEM((2, n_sides, chunks, rows * STEPS, LANES), BF16),
            pltpu.VMEM((height, cells), BF16),
            pltpu.VMEM((height, STEPS * width), BF16),
            pltpu.VMEM((height, STEPS * width), BF16),
            pltpu.VMEM((2, rows * STEPS, height), BF16),
            pltpu.VMEM((n_sides, rows * STEPS, height), BF16),
            dma((3 + len(small),)), dma((n_lat, n_parts)),
            dma((n_lat, n_parts, n_lon)), dma((n_lat, n_parts, n_lon)),
            dma((n_lat, n_parts)), dma((n_lat + 1, n_parts)),
            dma((2, 2)), dma((2, 2)), dma((2, n_sides)), dma((2, n_sides)),
            dma((n_parts, 2)), dma((n_parts, 2)), dma((n_sides,)), dma((n_sides,)),
            dma((chunks,)),
        ],
        compiler_params=pltpu.CompilerParams(
            vmem_limit_bytes=62 * 2**20, has_side_effects=True, collective_id=0
        ),
    )(
        source, control.reshape(planes * rows, width), kappa.reshape(planes * rows, width),
        *small,
    )
    return result.reshape(control.shape)


def solution(mesh):
    placed = (
        P(None, None, "lat", "lon"),
        P(None, None, "lat", "lon"),
        P(("lat", "lon"), None, None),
        P(("lat", "lon"), None),
        P(("lat", "lon"), None),
        P(("lat", "lon")),
        P(),
        P(),
    )
    return jax.shard_map(
        per_device,
        mesh=mesh,
        in_specs=placed,
        out_specs=P(None, None, "lat", "lon"),
        check_vma=False,
    )
```

```python
import functools

import jax
import jax.numpy as jnp
from jax import lax
from jax.experimental import pallas as pl
from jax.experimental.pallas import tpu as pltpu
from jax.sharding import PartitionSpec as P

CAP = 2
STEPS = 4
LANES = 128
GROUP = 16
EDGE = 8
TAIL = 4
COUNT_BASE = 64
TILE = 512
MESH = pl.DeviceIdType.MESH
F32 = jnp.float32
BF16 = jnp.bfloat16
SIDES = ((0, -1), (0, 1), (-1, -1), (-1, 1), (1, -1), (1, 1))


def iota(shape, dim):
    return lax.broadcasted_iota(jnp.int32, shape, dim)


def to_column(row, size):
    shape = (size, row.shape[1])
    return jnp.sum(jnp.where(iota(shape, 0) == iota(shape, 1), row, 0.0), axis=1, keepdims=True)


def digits(columns, counts):
    low = jnp.bitwise_and(columns, 31)
    valid = iota(columns.shape, 1).astype(F32) < counts
    high = jnp.where(valid, jnp.right_shift(columns - low, 5) + 1, 0)
    zero = jnp.zeros(columns.shape, F32)
    return [zero + 1.0, high.astype(F32), low.astype(F32), zero]


def pack_kernel(group, owner_ref, obs_ref, columns_ref, counts_ref, out_ref, wide, source):
    blocks = columns_ref.shape[0]
    comps = obs_ref.shape[0]
    height = out_ref.shape[1]
    slots = source.shape[0]

    @pl.when(pl.program_id(0) == 0)
    def _():
        @pl.loop(0, slots)
        def _(t):
            source[t] = -1

        @pl.loop(0, blocks)
        def _(b):
            first = owner_ref[b] * CAP
            source[jnp.where(source[first] < 0, first, first + 1)] = b

        @pl.loop(0, comps, unroll=4)
        def _(c):
            wide[pl.ds(pl.multiple_of(c * blocks, blocks), blocks), :] = obs_ref[c].astype(F32)

        for k, row in enumerate(digits(columns_ref[...], to_column(counts_ref[...].astype(F32), blocks))):
            wide[(comps + k) * blocks : (comps + k + 1) * blocks, :] = row

    for g in range(group):
        block = source[pl.program_id(0) * group + g]
        rows = wide[pl.ds(jnp.maximum(block, 0), height, stride=blocks), :]
        out_ref[g] = jnp.where(block < 0, 0.0, rows).astype(BF16)


def pack(obs, owner, columns, counts, peers, height):
    comps, blocks, soundings = obs.shape
    slots = peers * CAP
    group = 8
    return pl.pallas_call(
        functools.partial(pack_kernel, group),
        out_shape=jax.ShapeDtypeStruct((slots, height, soundings), BF16),
        grid_spec=pltpu.PrefetchScalarGridSpec(
            num_scalar_prefetch=1,
            grid=(slots // group,),
            in_specs=[
                pl.BlockSpec((comps, blocks, soundings), lambda i, s: (0, 0, 0)),
                pl.BlockSpec((blocks, soundings), lambda i, s: (0, 0)),
                pl.BlockSpec((1, blocks), lambda i, s: (0, 0)),
            ],
            out_specs=pl.BlockSpec((group, height, soundings), lambda i, s: (i, 0, 0)),
            scratch_shapes=[
                pltpu.VMEM((height * blocks, soundings), F32),
                pltpu.SMEM((slots,), jnp.int32),
            ],
        ),
        compiler_params=pltpu.CompilerParams(vmem_limit_bytes=56 * 2**20),
    )(owner[:, 0], obs, columns, counts[None, :])


def main_kernel(n_lat, n_lon, planes, parts, packed, *refs):
    source, control, kappa, *small_in, out = refs[:9]
    small, refs = refs[9:14], refs[14:]
    jac_in, weight_in, owner, counts, columns = small
    sent, obs, codes = (source, None, None) if packed else refs[:3]
    (
        recv, ring, part_out, part_in, sums, number, model, jac, scale,
        field, coef, east, raw, band_out, band_in, band_f, tile_f, tile_out, tile_in,
        total, total_north, total_south, side_out, side_in,
        load_sem, own_sem, blk_send, blk_recv, part_send, part_recv,
        band_send, band_recv, tile_send, tile_recv, row_send, row_recv, side_send, side_recv, store_sem,
    ) = refs if packed else refs[3:]
    lat, lon = lax.axis_index("lat"), lax.axis_index("lon")
    height, cells = sums.shape
    comps = jac_in.shape[0]
    chunks, extent, wide, _ = field.shape
    rows = extent - 2 * STEPS
    width = wide - 2 * EDGE
    area = planes * rows
    step_rows = LANES * rows
    slots = n_lon * CAP

    def plane_of(k):
        mirrored = lat >= n_lat - n_lat // 2
        z = jnp.where(mirrored, n_lat - 1 - lat, lat)
        o = jnp.where(k < n_lat - 1 - z, n_lat - 1 - k, k - (n_lat - 1 - z))
        return jnp.where(mirrored, n_lat - 1 - o, o)

    def remote(src, dst, send, recv_, to):
        return pltpu.make_async_remote_copy(
            src_ref=src, dst_ref=dst, send_sem=send, recv_sem=recv_, device_id=to, device_id_type=MESH
        )

    def around(step):
        return lax.rem(lon + step + n_lon, n_lon)

    def has(step):
        return (lat + step >= 0) & (lat + step < n_lat)

    def only(step, act):
        if step == 0:
            act()
        else:
            pl.when(has(step))(act)

    def slot_of(k):
        return plane_of(k) if packed else k

    def block_copy(k, h, i):
        lo, size = parts[h]
        return remote(
            sent.at[slot_of(k), around(i), :, pl.ds(lo, size), :], recv.at[k, i, :, pl.ds(lo, size), :],
            blk_send.at[k, h, i], blk_recv.at[k, h, i], (lat, around(i)),
        )

    def own_copy(k, h):
        lo, size = parts[h]
        return pltpu.make_async_copy(
            sent.at[slot_of(k), lon, :, pl.ds(lo, size), :],
            recv.at[k, 0, :, pl.ds(lo, size), :], own_sem.at[k, h],
        )

    def part_copy(k, h, slot, to):
        lo, size = parts[h]
        return remote(
            part_out.at[k, pl.ds(lo, size), :], part_in.at[slot, pl.ds(lo, size), :],
            part_send.at[k, h], part_recv.at[slot, h], (to, lon),
        )

    def part_sent(k, h):
        o = plane_of(k)
        north = o < lat
        slot = jnp.where(north & (o == lat - 1), n_lat, o)
        return part_copy(k, h, slot, jnp.where(north, lat - 1, lat + 1))

    def band_copy(a, s):
        return remote(
            band_out.at[a, 1 - s], band_in.at[a, s],
            band_send.at[a, s], band_recv.at[a, s], (lat + (1 - 2 * s), lon),
        )

    def peer(k):
        return (lat - SIDES[k][0], around(-SIDES[k][1]))

    def side_span(k):
        step = SIDES[k][0]
        return pl.ds((rows - STEPS) * STEPS if step < 0 else 0, (STEPS if step else rows) * STEPS)

    def side_of(k):
        return (1 - SIDES[k][1]) // 2

    def tile_copy(a, k):
        span = side_span(k)
        return remote(
            tile_out.at[a, side_of(k), :, span, :], tile_in.at[a, k, :, span, :],
            tile_send.at[a, k], tile_recv.at[a, k], peer(k),
        )

    def row_copy(h, s):
        lo, size = parts[h]
        span = STEPS * width
        return remote(
            total.at[pl.ds(lo, size), pl.ds((1 - s) * (rows * width - span), span)],
            (total_north if s == 0 else total_south).at[pl.ds(lo, size), :],
            row_send.at[h, s], row_recv.at[h, s], (lat + (1 - 2 * s), lon),
        )

    def side_copy(k):
        span = side_span(k)
        return remote(
            side_out.at[side_of(k), span, :], side_in.at[k, span, :], side_send.at[k], side_recv.at[k], peer(k)
        )

    loads = [
        pltpu.make_async_copy(ref, raw.at[a, pl.ds(0, area), :], load_sem.at[a])
        for a, ref in enumerate((control, kappa))
    ]
    small_loads = [
        pltpu.make_async_copy(ref, to, load_sem.at[3 + n]) for n, (ref, to) in enumerate(zip(small_in, small))
    ]
    for load in small_loads[1:]:
        load.start()
    if not packed:
        obs_load = pltpu.make_async_copy(source, obs, load_sem.at[2])
        obs_load.start()
    loads[1].start()
    loads[0].start()
    small_loads[0].start()

    barrier = pltpu.get_barrier_semaphore()

    @pl.loop(1, n_lon)
    def _(i):
        pl.semaphore_signal(barrier, inc=1, device_id=(lat, around(i)), device_id_type=MESH)

    for step in (-1, 1):
        def greet():
            for side in (-1, 0, 1):
                pl.semaphore_signal(
                    barrier, inc=1, device_id=(lat + step, around(side)), device_id_type=MESH
                )

        only(step, greet)

    sub = iota((EDGE, LANES), 0)

    def send_bands(a):
        loads[a].wait()
        if chunks * step_rows > area:
            raw[a, area:, :] = jnp.zeros((chunks * step_rows - area, width), F32)
        pairs = raw[a, 0:area, :].reshape(planes // 2, 2, rows, width)
        even, odd = pairs[:, 0], pairs[:, 1]
        upper = iota(even.shape, 1) < STEPS
        band_out[a, 0] = jnp.where(upper, even, pltpu.roll(odd, STEPS, 1)).reshape(area // 2, width).astype(BF16)
        band_out[a, 1] = jnp.where(upper, pltpu.roll(even, STEPS, 1), odd).reshape(area // 2, width).astype(BF16)
        for s in range(2):
            only(1 - 2 * s, lambda: band_copy(a, s).start())

    for load in small_loads[1:]:
        load.wait()

    if not packed:
        blocks = columns.shape[0]
        names = owner[...].astype(F32)
        square = (blocks, blocks)
        before = (to_column(names, blocks) == names) & (iota(square, 0) < iota(square, 1))
        place = names * CAP + jnp.sum(jnp.where(before, 1.0, 0.0), axis=0, keepdims=True)
        lined = (blocks, GROUP * blocks)
        comb = jnp.where(lax.rem(iota(lined, 1), blocks) == iota(lined, 0), 1.0, 0.0).astype(BF16)
        place = jnp.broadcast_to(place, (16, blocks)).astype(BF16)
        place = jnp.dot(place, comb, preferred_element_type=F32)[0:1].astype(jnp.int32)
        code = digits(columns[...], to_column(counts[...].astype(F32), blocks))
        codes[...] = jnp.concatenate(code, axis=0).astype(BF16)

    def pack_round(k, h):
        shape = (slots * GROUP, GROUP * blocks)
        at = plane_of(k) * slots + jnp.right_shift(iota(shape, 0), 4)
        hit = (place == at) & (jnp.bitwise_and(iota(shape, 0), GROUP - 1) == iota(shape, 1) // blocks)
        pick = jnp.where(hit, 1.0, 0.0).astype(BF16)
        lo, size = parts[h]
        span = GROUP * blocks

        def put(first, values):
            for t in range(slots):
                part = values[t * GROUP : (t + 1) * GROUP].astype(BF16)
                sent[k, t // CAP, t % CAP, pl.ds(first, GROUP), :] = part

        pairs = (min(lo + size, height - GROUP) - lo) // (2 * GROUP)

        @pl.loop(0, pairs)
        def _(p):
            first = pl.multiple_of(lo + p * 2 * GROUP, GROUP)
            start = pl.multiple_of(first * blocks, span)
            both = jnp.concatenate([obs[pl.ds(start, span), :], obs[pl.ds(start + span, span), :]], axis=1)
            values = jnp.dot(pick, both, preferred_element_type=F32)
            put(first, values[:, :LANES])
            put(pl.multiple_of(first + GROUP, GROUP), values[:, LANES:])

        if lo + size == height:
            last = jnp.concatenate([obs[(height - GROUP) * blocks :, :], codes[...]], axis=0)
            put(height - GROUP, jnp.dot(pick, last, preferred_element_type=F32))

    def send_round(k, h):
        if not packed:
            pack_round(k, h)
        if k == 0 and h == 0:
            pl.semaphore_wait(
                barrier, n_lon - 1 + 3 * (has(-1).astype(jnp.int32) + has(1).astype(jnp.int32))
            )

        @pl.loop(1, n_lon)
        def _(i):
            block_copy(k, h, i).start()

        own_copy(k, h).start()

    if not packed:
        obs_load.wait()
    for h in range(len(parts)):
        send_round(0, h)
        if h == 0:
            send_bands(1)
            send_bands(0)

    for a, grid in ((1, coef), (0, field)):
        @pl.loop(0, rows)
        def _(r):
            for j in range(chunks):
                turned = jnp.transpose(raw[a, pl.ds(j * step_rows + r, LANES, stride=rows), :])
                grid[j, STEPS + r, EDGE : EDGE + width, :] = turned

        @pl.loop(0, rows // 2)
        def _(p):
            for j in range(chunks):
                pair = [STEPS + 2 * p + q for q in range(2)]
                left = [grid[j, r, EDGE : 2 * EDGE, :] for r in pair]
                right = [grid[j, r, width : width + EDGE, :] for r in pair]
                tile_f[0, j, p] = jnp.where(sub < STEPS, left[0], pltpu.roll(left[1], STEPS, 0))
                tile_f[1, j, p] = jnp.where(sub < STEPS, pltpu.roll(right[0], STEPS, 0), right[1])

        tile_out[a] = tile_f[...].reshape(2, chunks, rows * STEPS, LANES).astype(BF16)
        for k in range(len(SIDES)):
            only(-SIDES[k][0], lambda: tile_copy(a, k).start())

    for k in range(1, n_lat):
        for h in range(len(parts)):
            send_round(k, h)

    small_loads[0].wait()
    matrix = jac_in[...].astype(F32)
    matrix = jnp.concatenate([matrix, jnp.zeros((height - comps, planes), F32)], axis=0)
    if chunks * LANES > planes:
        matrix = jnp.concatenate([matrix, jnp.zeros((height, chunks * LANES - planes), F32)], axis=1)
    jac[...] = matrix.astype(BF16)
    scale[...] = jnp.broadcast_to(to_column(weight_in[...].reshape(1, comps), height), scale.shape)

    def pad_line(h):
        return comps - parts[h][0]

    def lanes(n):
        return pl.ds(pl.multiple_of(n * TILE, TILE), TILE)

    def reduce_peers(k, h, start, stop):
        lo, size = parts[h]

        @pl.loop(max(start, 1), stop)
        def _(i):
            block_copy(k, h, i).wait_recv()

        base = height - GROUP
        first = comps - base
        heads = [recv[k, i, c, base:height, :].astype(F32) for i in range(start, stop) for c in range(CAP)]
        code = jnp.concatenate(
            [(x[first + 1 : first + 2] - 1.0) * 32.0 + x[first + 2 : first + 3] for x in heads], axis=1
        ).astype(jnp.int32)

        @pl.loop(0, cells // TILE)
        def _(n):
            values = jnp.concatenate(
                [recv[k, i, c, lo : lo + size, :] for i in range(start, stop) for c in range(CAP)], axis=1
            )
            hot = jnp.where(iota((TILE, code.shape[1]), 0) == code - n * TILE, 1.0, 0.0).astype(BF16)
            part = lax.dot_general(values, hot, (((1,), (1,)), ((), ())), preferred_element_type=F32)
            target = sums.at[lo : lo + size, lanes(n)]
            if k < n_lat - 1:
                target = ring.at[k % 2, lo : lo + size, lanes(n)]
            target[...] = part if start == 0 else target[...] + part
            if k == n_lat - 1 and h == 0:
                line = pad_line(h)
                number[:, lanes(n)] = jnp.broadcast_to(part[line : line + 1], (8, TILE))

    def reduce(k, h, groups=1):
        own_copy(k, h).wait()
        for g in range(groups):
            peers = n_lon // groups
            reduce_peers(k, h, g * peers, (g + 1) * peers)
        if k < n_lat - 1:
            pl.when(jnp.logical_not(has(-1) & has(1)))(lambda: emit(k, h, False))

    def emit(k, h, joined):
        lo, size = parts[h]
        o = plane_of(k)
        if joined:
            part_copy(k, h, o, lat).wait_recv()

        @pl.loop(0, cells // TILE)
        def _(n):
            value = ring[k % 2, lo : lo + size, lanes(n)]
            if h == 0:
                line = pad_line(h)
                count = value[line : line + 1]
            if joined:
                more = part_in[o, lo : lo + size, lanes(n)].astype(F32)
                value = value + more
                if h == 0:
                    count = count + more[line : line + 1] + more[line + 1 : line + 2] * COUNT_BASE
            if h == 0:
                high = jnp.floor(count * (1.0 / COUNT_BASE))
                at = iota(value.shape, 0)
                value = jnp.where(at == line, count - high * COUNT_BASE, jnp.where(at == line + 1, high, value))
            part_out[k, lo : lo + size, lanes(n)] = value.astype(BF16)

        part_sent(k, h).start()

    def join(k, h):
        pl.when(has(-1) & has(1))(lambda: emit(k, h, True))

    def fill_rows(a, grid):
        def band(s):
            first = (rows + STEPS) * s

            def arrived():
                band_copy(a, s).wait_recv()
                band_f[0 : area // 2, :] = band_in[a, s].astype(F32)

                @pl.loop(0, STEPS)
                def _(r):
                    for j in range(chunks):
                        piece = band_f[pl.ds(j * STEPS * LANES + r, LANES, stride=STEPS), :]
                        grid[j, first + r, EDGE : EDGE + width, :] = jnp.transpose(piece)

            def closed():
                for r in range(STEPS):
                    for j in range(chunks):
                        grid[j, first + r] = jnp.zeros((wide, LANES), F32)

            pl.when(has(2 * s - 1))(arrived)
            pl.when(jnp.logical_not(has(2 * s - 1)))(closed)

        for s in range(2):
            band(s)

    def put_sides(grid, j, p, west, east_):
        pair = (
            jnp.where(sub < STEPS, east_, pltpu.roll(west, STEPS, 0)),
            jnp.where(sub < STEPS, pltpu.roll(east_, STEPS, 0), west),
        )
        for q in range(2):
            grid[j, 2 * p + q, 0:EDGE, :] = pair[q]
            grid[j, 2 * p + q, EDGE + width :, :] = pair[q]

    def fill_columns(a, grid):
        def sides(k, place, source_row, count):
            for side in (k, k + 1):
                tile_copy(a, side).wait_recv()
            span = slice(source_row * STEPS, (source_row + count) * STEPS)
            west, east_ = (
                tile_in[a, side, :, span, :].astype(F32).reshape(chunks, count // 2, EDGE, LANES)
                for side in (k, k + 1)
            )
            for j in range(chunks):
                for p in range(count // 2):
                    put_sides(grid, j, place // 2 + p, west[j, p], east_[j, p])

        sides(0, STEPS, 0, rows)
        only(-1, lambda: sides(2, 0, rows - STEPS, STEPS))
        only(1, lambda: sides(4, STEPS + rows, 0, STEPS))

    def spread(j, finish=None):
        for step in range(STEPS):
            first, last = step + 1, extent - 1 - step
            above = coef[j, first - 1] * (field[j, first] - field[j, first - 1])

            def line(r, above):
                here = field[j, r]
                down = coef[j, r] * (field[j, r + 1] - here)
                along = east[j, r] * (pltpu.roll(here, wide - 1, 0) - here)
                result = here + (down - above) + (along - pltpu.roll(along, 1, 0))
                if finish is not None and step == STEPS - 1:
                    finish(r - STEPS, result[EDGE : EDGE + width])
                else:
                    field[j, r] = result
                return down

            lax.fori_loop(first, last, line, above, unroll=2)

    def take_kappa():
        if chunks * LANES > planes:
            band_f[area // 2 :, :] = jnp.zeros((chunks * LANES * STEPS - area // 2, width), F32)
        fill_rows(1, coef)

    def take_control():
        fill_rows(0, field)

    def make_products():
        fill_columns(1, coef)

        @pl.loop(0, chunks)
        def _(j):
            @pl.loop(0, extent - 1)
            def _(r):
                here = coef[j, r]
                east[j, r] = here * pltpu.roll(here, wide - 1, 0)
                coef[j, r] = here * coef[j, r + 1]

    def make_state():
        fill_columns(0, field)
        pl.loop(0, chunks)(spread)

    def make_model():
        @pl.loop(0, rows)
        def _(r):
            state = jnp.concatenate(
                [field[j, STEPS + r, EDGE : EDGE + width, :].astype(BF16) for j in range(chunks)], axis=1
            )
            model[:, pl.ds(pl.multiple_of(r * width, width), width)] = lax.dot_general(
                jac[...], state, (((1,), (1,)), ((), ())), preferred_element_type=F32
            )

    stages = {1: [make_products, take_control], 3: [make_state, make_model]}
    take_kappa()
    for k in range(n_lat - 1):
        for h in range(len(parts)):
            reduce(k, h)
            if k > 0:
                join(k - 1, h)
            if k == n_lat - 2:
                join(k, h)
            for stage in stages.get(k * len(parts) + h, []):
                stage()

    for s, ref in enumerate((total_north, total_south)):
        def blank():
            ref[...] = jnp.zeros(ref.shape, BF16)
            side_in[2 + 2 * s] = jnp.zeros(side_in.shape[1:], BF16)
            side_in[3 + 2 * s] = jnp.zeros(side_in.shape[1:], BF16)

        pl.when(jnp.logical_not(has(2 * s - 1)))(blank)

    def add_part(slot, h):
        lo, size = parts[h]
        part_copy(0, h, slot, lat).wait_recv()

        @pl.loop(0, cells // TILE)
        def _(n):
            more = part_in[slot, lo : lo + size, lanes(n)].astype(F32)
            sums[lo : lo + size, lanes(n)] = sums[lo : lo + size, lanes(n)] + more
            if h == 0:
                line = pad_line(h)
                count = more[line : line + 1] + more[line + 1 : line + 2] * COUNT_BASE
                number[:, lanes(n)] = number[:, lanes(n)] + count

    for h, (lo, size) in enumerate(parts):
        reduce(n_lat - 1, h, groups=2 if h == len(parts) - 1 else 1)
        only(-1, lambda: add_part(lat, h))
        only(1, lambda: add_part(n_lat, h))
        for r in range(rows):
            at = slice(r * width, (r + 1) * width)
            value = number[0:1, at] * model[lo : lo + size, at] - sums[lo : lo + size, at]
            total[lo : lo + size, at] = (value * scale[lo : lo + size, :]).astype(BF16)
        for s in range(2):
            only(1 - 2 * s, lambda: row_copy(h, s).start())

    ends = (2 * rows * STEPS, cells)
    line = iota(ends, 0)
    spot = lax.rem(line, rows * STEPS)
    spot = (spot // STEPS) * width + lax.rem(spot, STEPS)
    spot = spot + jnp.where(line < rows * STEPS, 0, width - STEPS)
    ends = jnp.where(iota(ends, 1) == spot, 1.0, 0.0).astype(BF16)
    side_out[...] = lax.dot_general(
        ends, total[...], (((1,), (1,)), ((), ())), preferred_element_type=F32
    ).reshape(2, rows * STEPS, height).astype(BF16)
    for k in range(len(SIDES)):
        only(-SIDES[k][0], lambda: side_copy(k).start())

    def put_row(values, r):
        result = lax.dot_general(values, jac[...], (((0,), (0,)), ((), ())), preferred_element_type=F32)
        for j in range(chunks):
            field[j, r, EDGE : EDGE + width, :] = result[:, j * LANES : (j + 1) * LANES]

    @pl.loop(0, rows)
    def _(r):
        put_row(total[:, pl.ds(pl.multiple_of(r * width, width), width)], STEPS + r)

    for k in range(len(SIDES)):
        only(SIDES[k][0], lambda: side_copy(k).wait_recv())

    side = jnp.concatenate(
        [
            side_in[k, lines, :]
            for ks in ((2, 0, 4), (3, 1, 5))
            for k, lines in zip(ks, (slice((rows - STEPS) * STEPS, rows * STEPS), slice(None), slice(0, STEPS * STEPS)))
        ],
        axis=0,
    )
    result = jnp.dot(side, jac[...], preferred_element_type=F32)
    for j in range(chunks):
        for p in range(extent // 2):
            west, east_ = (
                result[first + p * EDGE : first + (p + 1) * EDGE, j * LANES : (j + 1) * LANES]
                for first in (0, extent * STEPS)
            )
            put_sides(field, j, p, west, east_)

    for h in range(len(parts)):
        for s in range(2):
            only(2 * s - 1, lambda: row_copy(h, s).wait_recv())

    @pl.loop(0, STEPS)
    def _(r):
        at = pl.ds(pl.multiple_of(r * width, width), width)
        put_row(total_north[:, at], r)
        put_row(total_south[:, at], STEPS + rows + r)

    stores = []
    for j in range(chunks):
        def add_row(r, values):
            at = pl.ds(j * step_rows + r, LANES, stride=rows)
            raw[0, at, :] = raw[0, at, :] + jnp.transpose(values)

        spread(j, add_row)
        span = pl.ds(j * step_rows, min(step_rows, area - j * step_rows))
        stores.append(pltpu.make_async_copy(raw.at[0, span, :], out.at[span, :], store_sem.at[j]))
        stores[-1].start()

    for k in range(n_lat):
        for h in range(len(parts)):
            @pl.loop(1, n_lon)
            def _(i):
                block_copy(k, h, i).wait_send()
    for h in range(len(parts)):
        for k in range(n_lat - 1):
            part_sent(k, h).wait_send()
        for s in range(2):
            only(1 - 2 * s, lambda: row_copy(h, s).wait_send())
    for k in range(len(SIDES)):
        only(-SIDES[k][0], lambda: side_copy(k).wait_send())
    for a in range(2):
        for s in range(2):
            only(1 - 2 * s, lambda: band_copy(a, s).wait_send())
        for k in range(len(SIDES)):
            only(-SIDES[k][0], lambda: tile_copy(a, k).wait_send())
    for store in stores:
        store.wait()


def per_device(control, kappa, pc_obs, owner, columns, counts, jacobian, obs_weight):
    n_lat, n_lon = lax.axis_size("lat"), lax.axis_size("lon")
    fields, levels, rows, width = control.shape
    blocks, soundings, comps = pc_obs.shape
    planes = fields * levels
    cells = rows * width
    height = comps + TAIL
    chunks = -(-planes // LANES)
    extent, wide = rows + 2 * STEPS, width + 2 * EDGE
    half = height // 64 * 32
    parts = ((half, height - half), (0, half))
    obs = jnp.transpose(pc_obs, (2, 0, 1))
    slots_shape = (n_lat, n_lon, CAP, height, soundings)
    packed = blocks * GROUP > 1024
    if packed:
        source = pack(obs, owner, columns, counts, n_lat * n_lon, height).reshape(slots_shape)
        extra = []
    else:
        source = obs.reshape(comps * blocks, soundings)
        extra = [
            pltpu.VMEM(slots_shape, BF16),
            pltpu.VMEM(source.shape, BF16),
            pltpu.VMEM((TAIL * blocks, soundings), BF16),
        ]
    small = (jnp.transpose(jacobian), obs_weight, owner.reshape(1, blocks), counts[None, :], columns)
    n_parts, n_sides = len(parts), len(SIDES)
    grid = pltpu.VMEM((chunks, extent, wide, LANES), F32)
    dma = pltpu.SemaphoreType.DMA
    result = pl.pallas_call(
        functools.partial(main_kernel, n_lat, n_lon, planes, parts, packed),
        out_shape=jax.ShapeDtypeStruct((planes * rows, width), F32),
        in_specs=[pl.BlockSpec(memory_space=pl.ANY)] * (3 + len(small)),
        out_specs=pl.BlockSpec(memory_space=pl.ANY),
        scratch_shapes=[pltpu.VMEM(x.shape, x.dtype) for x in small]
        + extra
        + [
            pltpu.VMEM(slots_shape, BF16),
            pltpu.VMEM((2, height, cells), F32),
            pltpu.VMEM((n_lat - 1, height, cells), BF16),
            pltpu.VMEM((n_lat + 1, height, cells), BF16),
            pltpu.VMEM((height, cells), F32),
            pltpu.VMEM((8, cells), F32),
            pltpu.VMEM((height, cells), F32),
            pltpu.VMEM((height, chunks * LANES), BF16),
            pltpu.VMEM((height, LANES), F32),
            grid, grid, grid,
            pltpu.VMEM((2, chunks * LANES * rows, width), F32),
            pltpu.VMEM((2, 2, planes * STEPS, width), BF16),
            pltpu.VMEM((2, 2, planes * STEPS, width), BF16),
            pltpu.VMEM((chunks * LANES * STEPS, width), F32),
            pltpu.VMEM((2, chunks, rows // 2, EDGE, LANES), F32),
            pltpu.VMEM((2, 2, chunks, rows * STEPS, LANES), BF16),
            pltpu.VMEM((2, n_sides, chunks, rows * STEPS, LANES), BF16),
            pltpu.VMEM((height, cells), BF16),
            pltpu.VMEM((height, STEPS * width), BF16),
            pltpu.VMEM((height, STEPS * width), BF16),
            pltpu.VMEM((2, rows * STEPS, height), BF16),
            pltpu.VMEM((n_sides, rows * STEPS, height), BF16),
            dma((3 + len(small),)), dma((n_lat, n_parts)),
            dma((n_lat, n_parts, n_lon)), dma((n_lat, n_parts, n_lon)),
            dma((n_lat, n_parts)), dma((n_lat + 1, n_parts)),
            dma((2, 2)), dma((2, 2)), dma((2, n_sides)), dma((2, n_sides)),
            dma((n_parts, 2)), dma((n_parts, 2)), dma((n_sides,)), dma((n_sides,)),
            dma((chunks,)),
        ],
        compiler_params=pltpu.CompilerParams(
            vmem_limit_bytes=62 * 2**20, has_side_effects=True, collective_id=0
        ),
    )(
        source, control.reshape(planes * rows, width), kappa.reshape(planes * rows, width),
        *small,
    )
    return result.reshape(control.shape)


def solution(mesh):
    placed = (
        P(None, None, "lat", "lon"),
        P(None, None, "lat", "lon"),
        P(("lat", "lon"), None, None),
        P(("lat", "lon"), None),
        P(("lat", "lon"), None),
        P(("lat", "lon")),
        P(),
        P(),
    )
    return jax.shard_map(
        per_device,
        mesh=mesh,
        in_specs=placed,
        out_specs=P(None, None, "lat", "lon"),
        check_vma=False,
    )
```

```python
import functools

import jax
import jax.numpy as jnp
from jax import lax
from jax.experimental import pallas as pl
from jax.experimental.pallas import tpu as pltpu
from jax.sharding import PartitionSpec as P

CAP = 2
STEPS = 4
LANES = 128
GROUP = 16
EDGE = 8
TAIL = 4
COUNT_BASE = 64
TILE = 512
MESH = pl.DeviceIdType.MESH
F32 = jnp.float32
BF16 = jnp.bfloat16
SIDES = ((0, -1), (0, 1), (-1, -1), (-1, 1), (1, -1), (1, 1))


def iota(shape, dim):
    return lax.broadcasted_iota(jnp.int32, shape, dim)


def to_column(row, size):
    shape = (size, row.shape[1])
    return jnp.sum(jnp.where(iota(shape, 0) == iota(shape, 1), row, 0.0), axis=1, keepdims=True)


def digits(columns, counts):
    low = jnp.bitwise_and(columns, 31)
    valid = iota(columns.shape, 1).astype(F32) < counts
    high = jnp.where(valid, jnp.right_shift(columns - low, 5) + 1, 0)
    zero = jnp.zeros(columns.shape, F32)
    return [zero + 1.0, high.astype(F32), low.astype(F32), zero]


def pack_kernel(group, owner_ref, obs_ref, columns_ref, counts_ref, out_ref, wide, source):
    blocks = columns_ref.shape[0]
    comps = obs_ref.shape[0]
    height = out_ref.shape[1]
    slots = source.shape[0]

    @pl.when(pl.program_id(0) == 0)
    def _():
        @pl.loop(0, slots)
        def _(t):
            source[t] = -1

        @pl.loop(0, blocks)
        def _(b):
            first = owner_ref[b] * CAP
            source[jnp.where(source[first] < 0, first, first + 1)] = b

        @pl.loop(0, comps, unroll=4)
        def _(c):
            wide[pl.ds(pl.multiple_of(c * blocks, blocks), blocks), :] = obs_ref[c].astype(F32)

        for k, row in enumerate(digits(columns_ref[...], to_column(counts_ref[...].astype(F32), blocks))):
            wide[(comps + k) * blocks : (comps + k + 1) * blocks, :] = row

    for g in range(group):
        block = source[pl.program_id(0) * group + g]
        rows = wide[pl.ds(jnp.maximum(block, 0), height, stride=blocks), :]
        out_ref[g] = jnp.where(block < 0, 0.0, rows).astype(BF16)


def pack(obs, owner, columns, counts, peers, height):
    comps, blocks, soundings = obs.shape
    slots = peers * CAP
    group = 8
    return pl.pallas_call(
        functools.partial(pack_kernel, group),
        out_shape=jax.ShapeDtypeStruct((slots, height, soundings), BF16),
        grid_spec=pltpu.PrefetchScalarGridSpec(
            num_scalar_prefetch=1,
            grid=(slots // group,),
            in_specs=[
                pl.BlockSpec((comps, blocks, soundings), lambda i, s: (0, 0, 0)),
                pl.BlockSpec((blocks, soundings), lambda i, s: (0, 0)),
                pl.BlockSpec((1, blocks), lambda i, s: (0, 0)),
            ],
            out_specs=pl.BlockSpec((group, height, soundings), lambda i, s: (i, 0, 0)),
            scratch_shapes=[
                pltpu.VMEM((height * blocks, soundings), F32),
                pltpu.SMEM((slots,), jnp.int32),
            ],
        ),
        compiler_params=pltpu.CompilerParams(vmem_limit_bytes=56 * 2**20),
    )(owner[:, 0], obs, columns, counts[None, :])


def main_kernel(n_lat, n_lon, planes, parts, packed, *refs):
    source, control, kappa, *small_in, out = refs[:9]
    small, refs = refs[9:14], refs[14:]
    jac_in, weight_in, owner, counts, columns = small
    sent, obs, codes = (source, None, None) if packed else refs[:3]
    (
        recv, ring, part_out, part_in, sums, number, model, jac, scale,
        field, coef, east, raw, band_out, band_in, band_f, tile_f, tile_out, tile_in,
        total, total_north, total_south, side_out, side_in,
        load_sem, own_sem, blk_send, blk_recv, part_send, part_recv,
        band_send, band_recv, tile_send, tile_recv, row_send, row_recv, side_send, side_recv, store_sem,
    ) = refs if packed else refs[3:]
    lat, lon = lax.axis_index("lat"), lax.axis_index("lon")
    height, cells = sums.shape
    comps = jac_in.shape[0]
    chunks, extent, wide, _ = field.shape
    rows = extent - 2 * STEPS
    width = wide - 2 * EDGE
    area = planes * rows
    step_rows = LANES * rows
    slots = n_lon * CAP

    def plane_of(k):
        mirrored = lat >= n_lat - n_lat // 2
        z = jnp.where(mirrored, n_lat - 1 - lat, lat)
        o = jnp.where(k < n_lat - 1 - z, n_lat - 1 - k, k - (n_lat - 1 - z))
        return jnp.where(mirrored, n_lat - 1 - o, o)

    def remote(src, dst, send, recv_, to):
        return pltpu.make_async_remote_copy(
            src_ref=src, dst_ref=dst, send_sem=send, recv_sem=recv_, device_id=to, device_id_type=MESH
        )

    def around(step):
        return lax.rem(lon + step + n_lon, n_lon)

    def has(step):
        return (lat + step >= 0) & (lat + step < n_lat)

    def only(step, act):
        if step == 0:
            act()
        else:
            pl.when(has(step))(act)

    def slot_of(k):
        return plane_of(k) if packed else k

    def block_copy(k, h, i):
        lo, size = parts[h]
        return remote(
            sent.at[slot_of(k), around(i), :, pl.ds(lo, size), :], recv.at[k, i, :, pl.ds(lo, size), :],
            blk_send.at[k, h, i], blk_recv.at[k, h, i], (lat, around(i)),
        )

    def own_copy(k, h):
        lo, size = parts[h]
        return pltpu.make_async_copy(
            sent.at[slot_of(k), lon, :, pl.ds(lo, size), :],
            recv.at[k, 0, :, pl.ds(lo, size), :], own_sem.at[k, h],
        )

    def part_copy(k, h, slot, to):
        lo, size = parts[h]
        return remote(
            part_out.at[k, pl.ds(lo, size), :], part_in.at[slot, pl.ds(lo, size), :],
            part_send.at[k, h], part_recv.at[slot, h], (to, lon),
        )

    def part_sent(k, h):
        o = plane_of(k)
        north = o < lat
        slot = jnp.where(north & (o == lat - 1), n_lat, o)
        return part_copy(k, h, slot, jnp.where(north, lat - 1, lat + 1))

    def band_copy(a, s):
        return remote(
            band_out.at[a, 1 - s], band_in.at[a, s],
            band_send.at[a, s], band_recv.at[a, s], (lat + (1 - 2 * s), lon),
        )

    def peer(k):
        return (lat - SIDES[k][0], around(-SIDES[k][1]))

    def side_span(k):
        step = SIDES[k][0]
        return pl.ds((rows - STEPS) * STEPS if step < 0 else 0, (STEPS if step else rows) * STEPS)

    def side_of(k):
        return (1 - SIDES[k][1]) // 2

    def tile_copy(a, k):
        span = side_span(k)
        return remote(
            tile_out.at[a, side_of(k), :, span, :], tile_in.at[a, k, :, span, :],
            tile_send.at[a, k], tile_recv.at[a, k], peer(k),
        )

    def row_copy(h, s):
        lo, size = parts[h]
        span = STEPS * width
        return remote(
            total.at[pl.ds(lo, size), pl.ds((1 - s) * (rows * width - span), span)],
            (total_north if s == 0 else total_south).at[pl.ds(lo, size), :],
            row_send.at[h, s], row_recv.at[h, s], (lat + (1 - 2 * s), lon),
        )

    def side_copy(k):
        span = side_span(k)
        return remote(
            side_out.at[side_of(k), span, :], side_in.at[k, span, :], side_send.at[k], side_recv.at[k], peer(k)
        )

    loads = [
        pltpu.make_async_copy(ref, raw.at[a, pl.ds(0, area), :], load_sem.at[a])
        for a, ref in enumerate((control, kappa))
    ]
    small_loads = [
        pltpu.make_async_copy(ref, to, load_sem.at[3 + n]) for n, (ref, to) in enumerate(zip(small_in, small))
    ]
    for load in small_loads[1:]:
        load.start()
    if not packed:
        obs_load = pltpu.make_async_copy(source, obs, load_sem.at[2])
        obs_load.start()
    loads[1].start()
    loads[0].start()
    small_loads[0].start()

    barrier = pltpu.get_barrier_semaphore()

    @pl.loop(1, n_lon)
    def _(i):
        pl.semaphore_signal(barrier, inc=1, device_id=(lat, around(i)), device_id_type=MESH)

    for step in (-1, 1):
        def greet():
            for side in (-1, 0, 1):
                pl.semaphore_signal(
                    barrier, inc=1, device_id=(lat + step, around(side)), device_id_type=MESH
                )

        only(step, greet)

    sub = iota((EDGE, LANES), 0)

    def send_bands(a):
        loads[a].wait()
        if chunks * step_rows > area:
            raw[a, area:, :] = jnp.zeros((chunks * step_rows - area, width), F32)
        pairs = raw[a, 0:area, :].reshape(planes // 2, 2, rows, width)
        even, odd = pairs[:, 0], pairs[:, 1]
        upper = iota(even.shape, 1) < STEPS
        band_out[a, 0] = jnp.where(upper, even, pltpu.roll(odd, STEPS, 1)).reshape(area // 2, width).astype(BF16)
        band_out[a, 1] = jnp.where(upper, pltpu.roll(even, STEPS, 1), odd).reshape(area // 2, width).astype(BF16)
        for s in range(2):
            only(1 - 2 * s, lambda: band_copy(a, s).start())

    for load in small_loads[1:]:
        load.wait()

    if not packed:
        blocks = columns.shape[0]
        names = owner[...].astype(F32)
        square = (blocks, blocks)
        before = (to_column(names, blocks) == names) & (iota(square, 0) < iota(square, 1))
        place = names * CAP + jnp.sum(jnp.where(before, 1.0, 0.0), axis=0, keepdims=True)
        lined = (blocks, GROUP * blocks)
        comb = jnp.where(lax.rem(iota(lined, 1), blocks) == iota(lined, 0), 1.0, 0.0).astype(BF16)
        place = jnp.broadcast_to(place, (16, blocks)).astype(BF16)
        place = jnp.dot(place, comb, preferred_element_type=F32)[0:1].astype(jnp.int32)
        code = digits(columns[...], to_column(counts[...].astype(F32), blocks))
        codes[...] = jnp.concatenate(code, axis=0).astype(BF16)

    def pack_round(k, h):
        shape = (slots * GROUP, GROUP * blocks)
        at = plane_of(k) * slots + jnp.right_shift(iota(shape, 0), 4)
        hit = (place == at) & (jnp.bitwise_and(iota(shape, 0), GROUP - 1) == iota(shape, 1) // blocks)
        pick = jnp.where(hit, 1.0, 0.0).astype(BF16)
        lo, size = parts[h]
        span = GROUP * blocks

        def put(first, values):
            for t in range(slots):
                part = values[t * GROUP : (t + 1) * GROUP].astype(BF16)
                sent[k, t // CAP, t % CAP, pl.ds(first, GROUP), :] = part

        pairs = (min(lo + size, height - GROUP) - lo) // (2 * GROUP)

        @pl.loop(0, pairs)
        def _(p):
            first = pl.multiple_of(lo + p * 2 * GROUP, GROUP)
            start = pl.multiple_of(first * blocks, span)
            both = jnp.concatenate([obs[pl.ds(start, span), :], obs[pl.ds(start + span, span), :]], axis=1)
            values = jnp.dot(pick, both, preferred_element_type=F32)
            put(first, values[:, :LANES])
            put(pl.multiple_of(first + GROUP, GROUP), values[:, LANES:])

        if lo + size == height:
            last = jnp.concatenate([obs[(height - GROUP) * blocks :, :], codes[...]], axis=0)
            put(height - GROUP, jnp.dot(pick, last, preferred_element_type=F32))

    def send_round(k, h):
        if not packed:
            pack_round(k, h)
        if k == 0 and h == 0:
            pl.semaphore_wait(
                barrier, n_lon - 1 + 3 * (has(-1).astype(jnp.int32) + has(1).astype(jnp.int32))
            )

        @pl.loop(1, n_lon)
        def _(i):
            block_copy(k, h, i).start()

        own_copy(k, h).start()

    if not packed:
        obs_load.wait()
    for h in range(len(parts)):
        send_round(0, h)
        if h == 0:
            send_bands(1)
            send_bands(0)

    for a, grid in ((1, coef), (0, field)):
        @pl.loop(0, rows)
        def _(r):
            for j in range(chunks):
                turned = jnp.transpose(raw[a, pl.ds(j * step_rows + r, LANES, stride=rows), :])
                grid[j, STEPS + r, EDGE : EDGE + width, :] = turned

        @pl.loop(0, rows // 2)
        def _(p):
            for j in range(chunks):
                pair = [STEPS + 2 * p + q for q in range(2)]
                left = [grid[j, r, EDGE : 2 * EDGE, :] for r in pair]
                right = [grid[j, r, width : width + EDGE, :] for r in pair]
                tile_f[0, j, p] = jnp.where(sub < STEPS, left[0], pltpu.roll(left[1], STEPS, 0))
                tile_f[1, j, p] = jnp.where(sub < STEPS, pltpu.roll(right[0], STEPS, 0), right[1])

        tile_out[a] = tile_f[...].reshape(2, chunks, rows * STEPS, LANES).astype(BF16)
        for k in range(len(SIDES)):
            only(-SIDES[k][0], lambda: tile_copy(a, k).start())

    for k in range(1, n_lat):
        for h in range(len(parts)):
            send_round(k, h)

    small_loads[0].wait()
    matrix = jac_in[...].astype(F32)
    matrix = jnp.concatenate([matrix, jnp.zeros((height - comps, planes), F32)], axis=0)
    if chunks * LANES > planes:
        matrix = jnp.concatenate([matrix, jnp.zeros((height, chunks * LANES - planes), F32)], axis=1)
    jac[...] = matrix.astype(BF16)
    scale[...] = jnp.broadcast_to(to_column(weight_in[...].reshape(1, comps), height), scale.shape)

    def pad_line(h):
        return comps - parts[h][0]

    def lanes(n):
        return pl.ds(pl.multiple_of(n * TILE, TILE), TILE)

    def reduce_peers(k, h, start, stop):
        lo, size = parts[h]

        @pl.loop(max(start, 1), stop)
        def _(i):
            block_copy(k, h, i).wait_recv()

        base = height - GROUP
        first = comps - base
        heads = [recv[k, i, c, base:height, :].astype(F32) for i in range(start, stop) for c in range(CAP)]
        code = jnp.concatenate(
            [(x[first + 1 : first + 2] - 1.0) * 32.0 + x[first + 2 : first + 3] for x in heads], axis=1
        ).astype(jnp.int32)

        @pl.loop(0, cells // TILE)
        def _(n):
            values = jnp.concatenate(
                [recv[k, i, c, lo : lo + size, :] for i in range(start, stop) for c in range(CAP)], axis=1
            )
            hot = jnp.where(iota((TILE, code.shape[1]), 0) == code - n * TILE, 1.0, 0.0).astype(BF16)
            part = lax.dot_general(values, hot, (((1,), (1,)), ((), ())), preferred_element_type=F32)
            target = sums.at[lo : lo + size, lanes(n)]
            if k < n_lat - 1:
                target = ring.at[k % 2, lo : lo + size, lanes(n)]
            target[...] = part if start == 0 else target[...] + part
            if k == n_lat - 1 and h == 0:
                line = pad_line(h)
                number[:, lanes(n)] = jnp.broadcast_to(part[line : line + 1], (8, TILE))

    def reduce(k, h, groups=1):
        own_copy(k, h).wait()
        for g in range(groups):
            peers = n_lon // groups
            reduce_peers(k, h, g * peers, (g + 1) * peers)
        if k < n_lat - 1:
            pl.when(jnp.logical_not(has(-1) & has(1)))(lambda: emit(k, h, False))

    def emit(k, h, joined):
        lo, size = parts[h]
        o = plane_of(k)
        if joined:
            part_copy(k, h, o, lat).wait_recv()

        @pl.loop(0, cells // TILE)
        def _(n):
            value = ring[k % 2, lo : lo + size, lanes(n)]
            if h == 0:
                line = pad_line(h)
                count = value[line : line + 1]
            if joined:
                more = part_in[o, lo : lo + size, lanes(n)].astype(F32)
                value = value + more
                if h == 0:
                    count = count + more[line : line + 1] + more[line + 1 : line + 2] * COUNT_BASE
            if h == 0:
                high = jnp.floor(count * (1.0 / COUNT_BASE))
                at = iota(value.shape, 0)
                value = jnp.where(at == line, count - high * COUNT_BASE, jnp.where(at == line + 1, high, value))
            part_out[k, lo : lo + size, lanes(n)] = value.astype(BF16)

        part_sent(k, h).start()

    def join(k, h):
        pl.when(has(-1) & has(1))(lambda: emit(k, h, True))

    def fill_rows(a, grid):
        def band(s):
            first = (rows + STEPS) * s

            def arrived():
                band_copy(a, s).wait_recv()
                band_f[0 : area // 2, :] = band_in[a, s].astype(F32)

                @pl.loop(0, STEPS)
                def _(r):
                    for j in range(chunks):
                        piece = band_f[pl.ds(j * STEPS * LANES + r, LANES, stride=STEPS), :]
                        grid[j, first + r, EDGE : EDGE + width, :] = jnp.transpose(piece)

            def closed():
                for r in range(STEPS):
                    for j in range(chunks):
                        grid[j, first + r] = jnp.zeros((wide, LANES), F32)

            pl.when(has(2 * s - 1))(arrived)
            pl.when(jnp.logical_not(has(2 * s - 1)))(closed)

        for s in range(2):
            band(s)

    def put_sides(grid, j, p, west, east_):
        pair = (
            jnp.where(sub < STEPS, east_, pltpu.roll(west, STEPS, 0)),
            jnp.where(sub < STEPS, pltpu.roll(east_, STEPS, 0), west),
        )
        for q in range(2):
            grid[j, 2 * p + q, 0:EDGE, :] = pair[q]
            grid[j, 2 * p + q, EDGE + width :, :] = pair[q]

    def fill_columns(a, grid):
        def sides(k, place, source_row, count):
            for side in (k, k + 1):
                tile_copy(a, side).wait_recv()
            span = slice(source_row * STEPS, (source_row + count) * STEPS)
            west, east_ = (
                tile_in[a, side, :, span, :].astype(F32).reshape(chunks, count // 2, EDGE, LANES)
                for side in (k, k + 1)
            )
            for j in range(chunks):
                for p in range(count // 2):
                    put_sides(grid, j, place // 2 + p, west[j, p], east_[j, p])

        sides(0, STEPS, 0, rows)
        only(-1, lambda: sides(2, 0, rows - STEPS, STEPS))
        only(1, lambda: sides(4, STEPS + rows, 0, STEPS))

    def spread(j, finish=None):
        for step in range(STEPS):
            first, last = step + 1, extent - 1 - step
            above = coef[j, first - 1] * (field[j, first] - field[j, first - 1])

            def line(r, above):
                here = field[j, r]
                down = coef[j, r] * (field[j, r + 1] - here)
                along = east[j, r] * (pltpu.roll(here, wide - 1, 0) - here)
                result = here + (down - above) + (along - pltpu.roll(along, 1, 0))
                if finish is not None and step == STEPS - 1:
                    finish(r - STEPS, result[EDGE : EDGE + width])
                else:
                    field[j, r] = result
                return down

            lax.fori_loop(first, last, line, above, unroll=2)

    def take_kappa():
        if chunks * LANES > planes:
            band_f[area // 2 :, :] = jnp.zeros((chunks * LANES * STEPS - area // 2, width), F32)
        fill_rows(1, coef)

    def take_control():
        fill_rows(0, field)

    def make_products():
        fill_columns(1, coef)

        @pl.loop(0, chunks)
        def _(j):
            @pl.loop(0, extent - 1)
            def _(r):
                here = coef[j, r]
                east[j, r] = here * pltpu.roll(here, wide - 1, 0)
                coef[j, r] = here * coef[j, r + 1]

    def make_state():
        fill_columns(0, field)
        pl.loop(0, chunks)(spread)

    def make_model():
        @pl.loop(0, rows)
        def _(r):
            state = jnp.concatenate(
                [field[j, STEPS + r, EDGE : EDGE + width, :].astype(BF16) for j in range(chunks)], axis=1
            )
            model[:, pl.ds(pl.multiple_of(r * width, width), width)] = lax.dot_general(
                jac[...], state, (((1,), (1,)), ((), ())), preferred_element_type=F32
            )

    stages = {1: [make_products, take_control], 3: [make_state, make_model]}
    take_kappa()
    for k in range(n_lat - 1):
        for h in range(len(parts)):
            reduce(k, h)
            if k > 0:
                join(k - 1, h)
            if k == n_lat - 2:
                join(k, h)
            for stage in stages.get(k * len(parts) + h, []):
                stage()

    for s, ref in enumerate((total_north, total_south)):
        def blank():
            ref[...] = jnp.zeros(ref.shape, BF16)
            side_in[2 + 2 * s] = jnp.zeros(side_in.shape[1:], BF16)
            side_in[3 + 2 * s] = jnp.zeros(side_in.shape[1:], BF16)

        pl.when(jnp.logical_not(has(2 * s - 1)))(blank)

    def add_part(slot, h):
        lo, size = parts[h]
        part_copy(0, h, slot, lat).wait_recv()

        @pl.loop(0, cells // TILE)
        def _(n):
            more = part_in[slot, lo : lo + size, lanes(n)].astype(F32)
            sums[lo : lo + size, lanes(n)] = sums[lo : lo + size, lanes(n)] + more
            if h == 0:
                line = pad_line(h)
                count = more[line : line + 1] + more[line + 1 : line + 2] * COUNT_BASE
                number[:, lanes(n)] = number[:, lanes(n)] + count

    for h, (lo, size) in enumerate(parts):
        reduce(n_lat - 1, h, groups=2 if h == len(parts) - 1 else 1)
        only(-1, lambda: add_part(lat, h))
        only(1, lambda: add_part(n_lat, h))
        for r in range(rows):
            at = slice(r * width, (r + 1) * width)
            value = number[0:1, at] * model[lo : lo + size, at] - sums[lo : lo + size, at]
            total[lo : lo + size, at] = (value * scale[lo : lo + size, :]).astype(BF16)
        for s in range(2):
            only(1 - 2 * s, lambda: row_copy(h, s).start())

    ends = (2 * rows * STEPS, cells)
    line = iota(ends, 0)
    spot = lax.rem(line, rows * STEPS)
    spot = (spot // STEPS) * width + lax.rem(spot, STEPS)
    spot = spot + jnp.where(line < rows * STEPS, 0, width - STEPS)
    ends = jnp.where(iota(ends, 1) == spot, 1.0, 0.0).astype(BF16)
    side_out[...] = lax.dot_general(
        ends, total[...], (((1,), (1,)), ((), ())), preferred_element_type=F32
    ).reshape(2, rows * STEPS, height).astype(BF16)
    for k in range(len(SIDES)):
        only(-SIDES[k][0], lambda: side_copy(k).start())

    def put_row(values, r):
        result = lax.dot_general(values, jac[...], (((0,), (0,)), ((), ())), preferred_element_type=F32)
        for j in range(chunks):
            field[j, r, EDGE : EDGE + width, :] = result[:, j * LANES : (j + 1) * LANES]

    @pl.loop(0, rows)
    def _(r):
        put_row(total[:, pl.ds(pl.multiple_of(r * width, width), width)], STEPS + r)

    for k in range(len(SIDES)):
        only(SIDES[k][0], lambda: side_copy(k).wait_recv())

    side = jnp.concatenate(
        [
            side_in[k, lines, :]
            for ks in ((2, 0, 4), (3, 1, 5))
            for k, lines in zip(ks, (slice((rows - STEPS) * STEPS, rows * STEPS), slice(None), slice(0, STEPS * STEPS)))
        ],
        axis=0,
    )
    result = jnp.dot(side, jac[...], preferred_element_type=F32)
    for j in range(chunks):
        for p in range(extent // 2):
            west, east_ = (
                result[first + p * EDGE : first + (p + 1) * EDGE, j * LANES : (j + 1) * LANES]
                for first in (0, extent * STEPS)
            )
            put_sides(field, j, p, west, east_)

    for h in range(len(parts)):
        for s in range(2):
            only(2 * s - 1, lambda: row_copy(h, s).wait_recv())

    @pl.loop(0, STEPS, unroll=STEPS)
    def _(r):
        at = pl.ds(pl.multiple_of(r * width, width), width)
        put_row(total_north[:, at], r)
        put_row(total_south[:, at], STEPS + rows + r)

    stores = []
    for j in range(chunks):
        def add_row(r, values):
            at = pl.ds(j * step_rows + r, LANES, stride=rows)
            raw[0, at, :] = raw[0, at, :] + jnp.transpose(values)

        spread(j, add_row)
        span = pl.ds(j * step_rows, min(step_rows, area - j * step_rows))
        stores.append(pltpu.make_async_copy(raw.at[0, span, :], out.at[span, :], store_sem.at[j]))
        stores[-1].start()

    for k in range(n_lat):
        for h in range(len(parts)):
            @pl.loop(1, n_lon)
            def _(i):
                block_copy(k, h, i).wait_send()
    for h in range(len(parts)):
        for k in range(n_lat - 1):
            part_sent(k, h).wait_send()
        for s in range(2):
            only(1 - 2 * s, lambda: row_copy(h, s).wait_send())
    for k in range(len(SIDES)):
        only(-SIDES[k][0], lambda: side_copy(k).wait_send())
    for a in range(2):
        for s in range(2):
            only(1 - 2 * s, lambda: band_copy(a, s).wait_send())
        for k in range(len(SIDES)):
            only(-SIDES[k][0], lambda: tile_copy(a, k).wait_send())
    for store in stores:
        store.wait()


def per_device(control, kappa, pc_obs, owner, columns, counts, jacobian, obs_weight):
    n_lat, n_lon = lax.axis_size("lat"), lax.axis_size("lon")
    fields, levels, rows, width = control.shape
    blocks, soundings, comps = pc_obs.shape
    planes = fields * levels
    cells = rows * width
    height = comps + TAIL
    chunks = -(-planes // LANES)
    extent, wide = rows + 2 * STEPS, width + 2 * EDGE
    half = height // 64 * 32
    parts = ((half, height - half), (0, half))
    obs = jnp.transpose(pc_obs, (2, 0, 1))
    slots_shape = (n_lat, n_lon, CAP, height, soundings)
    packed = blocks * GROUP > 1024
    if packed:
        source = pack(obs, owner, columns, counts, n_lat * n_lon, height).reshape(slots_shape)
        extra = []
    else:
        source = obs.reshape(comps * blocks, soundings)
        extra = [
            pltpu.VMEM(slots_shape, BF16),
            pltpu.VMEM(source.shape, BF16),
            pltpu.VMEM((TAIL * blocks, soundings), BF16),
        ]
    small = (jnp.transpose(jacobian), obs_weight, owner.reshape(1, blocks), counts[None, :], columns)
    n_parts, n_sides = len(parts), len(SIDES)
    grid = pltpu.VMEM((chunks, extent, wide, LANES), F32)
    dma = pltpu.SemaphoreType.DMA
    result = pl.pallas_call(
        functools.partial(main_kernel, n_lat, n_lon, planes, parts, packed),
        out_shape=jax.ShapeDtypeStruct((planes * rows, width), F32),
        in_specs=[pl.BlockSpec(memory_space=pl.ANY)] * (3 + len(small)),
        out_specs=pl.BlockSpec(memory_space=pl.ANY),
        scratch_shapes=[pltpu.VMEM(x.shape, x.dtype) for x in small]
        + extra
        + [
            pltpu.VMEM(slots_shape, BF16),
            pltpu.VMEM((2, height, cells), F32),
            pltpu.VMEM((n_lat - 1, height, cells), BF16),
            pltpu.VMEM((n_lat + 1, height, cells), BF16),
            pltpu.VMEM((height, cells), F32),
            pltpu.VMEM((8, cells), F32),
            pltpu.VMEM((height, cells), F32),
            pltpu.VMEM((height, chunks * LANES), BF16),
            pltpu.VMEM((height, LANES), F32),
            grid, grid, grid,
            pltpu.VMEM((2, chunks * LANES * rows, width), F32),
            pltpu.VMEM((2, 2, planes * STEPS, width), BF16),
            pltpu.VMEM((2, 2, planes * STEPS, width), BF16),
            pltpu.VMEM((chunks * LANES * STEPS, width), F32),
            pltpu.VMEM((2, chunks, rows // 2, EDGE, LANES), F32),
            pltpu.VMEM((2, 2, chunks, rows * STEPS, LANES), BF16),
            pltpu.VMEM((2, n_sides, chunks, rows * STEPS, LANES), BF16),
            pltpu.VMEM((height, cells), BF16),
            pltpu.VMEM((height, STEPS * width), BF16),
            pltpu.VMEM((height, STEPS * width), BF16),
            pltpu.VMEM((2, rows * STEPS, height), BF16),
            pltpu.VMEM((n_sides, rows * STEPS, height), BF16),
            dma((3 + len(small),)), dma((n_lat, n_parts)),
            dma((n_lat, n_parts, n_lon)), dma((n_lat, n_parts, n_lon)),
            dma((n_lat, n_parts)), dma((n_lat + 1, n_parts)),
            dma((2, 2)), dma((2, 2)), dma((2, n_sides)), dma((2, n_sides)),
            dma((n_parts, 2)), dma((n_parts, 2)), dma((n_sides,)), dma((n_sides,)),
            dma((chunks,)),
        ],
        compiler_params=pltpu.CompilerParams(
            vmem_limit_bytes=62 * 2**20, has_side_effects=True, collective_id=0
        ),
    )(
        source, control.reshape(planes * rows, width), kappa.reshape(planes * rows, width),
        *small,
    )
    return result.reshape(control.shape)


def solution(mesh):
    placed = (
        P(None, None, "lat", "lon"),
        P(None, None, "lat", "lon"),
        P(("lat", "lon"), None, None),
        P(("lat", "lon"), None),
        P(("lat", "lon"), None),
        P(("lat", "lon")),
        P(),
        P(),
    )
    return jax.shard_map(
        per_device,
        mesh=mesh,
        in_specs=placed,
        out_specs=P(None, None, "lat", "lon"),
        check_vma=False,
    )
```
